128 devices in a mesh: fsdp: 8 (over x_hi, z), seq: 2 (over x_lo), tp: 8 (over y, core).
Axes of the slice: x: 4 (x_hi: 2, x_lo: 2; x = x_hi * 2 + x_lo), y: 4, z: 4, core: 2. Of those that a mesh axis runs over, the one named last changes fastest.
Arguments:
- hidden_in: bfloat16 [24, 256, 1280], P('fsdp', 'seq'), may hold values from -6 to 6
- cotangent: bfloat16 [24, 256, 1280], P('fsdp', 'seq'), may hold values from -6 to 6
- lengths: int32 [24], P('fsdp'), may hold values from 1 to 256, as said below
- qkv_weight: bfloat16 [2, 3, 1280, 1280], P(None, None, ('fsdp', 'seq'), 'tp'), may hold values from -0.15625 to 0.15625
- qv_bias: bfloat16 [2, 2, 1280], P(None, None, 'tp'), may hold values from -4 to 4
- out_weight: bfloat16 [2, 1280, 1280], P(None, 'tp', ('fsdp', 'seq')), may hold values from -1 to 1
- out_bias: bfloat16 [2, 1280], P(None, ('fsdp', 'seq')), may hold values from -4 to 4
- up_weight: bfloat16 [2, 1280, 5120], P(None, ('fsdp', 'seq'), 'tp'), may hold values from -0.15625 to 0.15625
- up_bias: bfloat16 [2, 5120], P(None, 'tp'), may hold values from -6 to 6
- down_weight: bfloat16 [2, 5120, 1280], P(None, 'tp', ('fsdp', 'seq')), may hold values from -0.078125 to 0.078125
- down_bias: bfloat16 [2, 1280], P(None, ('fsdp', 'seq')), may hold values from -4 to 4
- ln_gain: bfloat16 [2, 2, 1280], P(None, None, ('fsdp', 'seq')), may hold values from 0.5 to 1.5
- ln_bias: bfloat16 [2, 2, 1280], P(None, None, ('fsdp', 'seq')), may hold values from -4 to 4
Outputs:
- out_hidden: float32 [24, 256, 1280], P('fsdp', 'seq')
- in_grad: float32 [24, 256, 1280], P('fsdp', 'seq')
- qkv_grad: float32 [2, 3, 1280, 1280], P(None, None, ('fsdp', 'seq'), 'tp')
- qv_bias_grad: float32 [2, 2, 1280], P(None, None, 'tp')
- out_weight_grad: float32 [2, 1280, 1280], P(None, 'tp', ('fsdp', 'seq'))
- out_bias_grad: float32 [2, 1280], P(None, ('fsdp', 'seq'))
- up_weight_grad: float32 [2, 1280, 5120], P(None, ('fsdp', 'seq'), 'tp')
- up_bias_grad: float32 [2, 5120], P(None, 'tp')
- down_weight_grad: float32 [2, 5120, 1280], P(None, 'tp', ('fsdp', 'seq'))
- down_bias_grad: float32 [2, 1280], P(None, ('fsdp', 'seq'))
- ln_gain_grad: float32 [2, 2, 1280], P(None, None, ('fsdp', 'seq'))
- ln_bias_grad: float32 [2, 2, 1280], P(None, None, ('fsdp', 'seq'))
The draws below stay inside these ranges and needn't reach their ends.
Inputs may be any that keep to these rules, and one draw needn't show every extreme that they name: `lengths`: clip c is on index c // 3 of fsdp, as micro-batch c % 3; among the 3 clips of each index of fsdp one has 256 valid tokens.
All inputs are finite; a program needn't handle non-finite values.
Results may differ from the reference program's by a relative error of at most 0.024.
Values may be sent and summed in bfloat16 or wider, within the bound.
A program may use at most 128 MiB of HBM per device.

```python
import math
import jax
import jax.numpy as jnp
from jax import lax

D = 1280
HEADS = 16
HD = 80
FF = 5120
LAYERS = 2
MICRO = 3
LEN = 256
CLIPS = 24
N_FSDP = 8


def draw_lengths(key, part):
    key = jax.random.fold_in(key, 7)
    key_base, key_pick = jax.random.split(key)
    base_len = jax.random.randint(key_base, (N_FSDP, MICRO), 1, LEN + 1)
    pick_slot = jax.random.randint(key_pick, (N_FSDP, 1), 0, MICRO)
    full_slot = jnp.arange(MICRO)[None, :] == pick_slot
    return jnp.where(full_slot, LEN, base_len).reshape(-1).astype(jnp.int32)


def steps_of(key, dims, cuts, smallest, largest):
    gain, own = 1.0, jax.random.fold_in(key, 6)
    for axis_at, shards_of in cuts:
        heights = jnp.exp(jax.random.uniform(jax.random.fold_in(own, axis_at), (shards_of,), jnp.float32, smallest / len(cuts), largest / len(cuts)))
        gain = gain * jnp.repeat(heights, dims[axis_at] // shards_of).reshape([-1 if axis == axis_at else 1 for axis in range(len(dims))])
    return gain


def normal_values(own_key, dims, deviation, bound, pieces=(), kind=jnp.bfloat16):
    drawn = jax.random.normal(own_key, dims, jnp.float32) * deviation
    if len(pieces) > 0:
        drawn = steps_of(own_key, dims, pieces, -0.22, 0.18) * drawn
    return jnp.clip(drawn, min=-bound, max=bound).astype(kind)


def setup_inputs(seed: int = 0) -> dict:
    keys = jax.random.split(jax.random.key(seed), 14)
    return {
        "hidden_in": normal_values(keys[0], (CLIPS, LEN, D), 1.0, 6.0, ((0, 8), (1, 2))),
        "cotangent": normal_values(keys[1], (CLIPS, LEN, D), 1.0, 6.0, ((0, 8), (1, 2))),
        "lengths": draw_lengths(jax.random.fold_in(keys[13], 71), 0),
        "qkv_weight": normal_values(keys[3], (LAYERS, 3, D, D), D ** -0.5, 0.15625, ((2, 16), (3, 8))),
        "qv_bias": normal_values(keys[4], (LAYERS, 2, D), 0.3, 4.0, ((2, 8),)),
        "out_weight": normal_values(keys[5], (LAYERS, D, D), (max(D * 8 // LEN, 1)) ** -0.5, 1.0, ((1, 8), (2, 16))),
        "out_bias": normal_values(keys[6], (LAYERS, D), 0.3, 4.0, ((1, 16),)),
        "up_weight": normal_values(keys[7], (LAYERS, D, FF), D ** -0.5, 0.15625, ((1, 16), (2, 8))),
        "up_bias": normal_values(keys[8], (LAYERS, FF), 0.5, 6.0, ((1, 8),)),
        "down_weight": normal_values(keys[9], (LAYERS, FF, D), FF ** -0.5, 0.078125, ((1, 8), (2, 16))),
        "down_bias": normal_values(keys[10], (LAYERS, D), 0.3, 4.0, ((1, 16),)),
        "ln_gain": jnp.clip(1.0 + 0.1 * jax.random.normal(keys[11], (LAYERS, 2, D), jnp.float32), 0.5, 1.5).astype(jnp.bfloat16),
        "ln_bias": normal_values(keys[12], (LAYERS, 2, D), 0.3, 4.0, ((2, 16),)),
    }


@jax.custom_vjp
def low(v):
    return lax.optimization_barrier(v.astype(jnp.bfloat16)).astype(jnp.float32)

@jax.custom_vjp
def low_back(v):
    return v

def low_keep(v):
    return (low(v), None)

def low_pass(kept, grad):
    return (grad,)

def back_keep(v):
    return (v, None)

def back_low(kept, grad):
    return (low(grad),)
low.defvjp(low_keep, low_pass)
low_back.defvjp(back_keep, back_low)
EPSILON = 1e-05
MASKED = -1000000000.0
HIGH = lax.Precision.HIGHEST

def layer_norm(values, gain_vec, shift_vec):
    row_mean = lax.optimization_barrier(jnp.mean(values, axis=-1, keepdims=True))
    centred = values - row_mean
    row_var = lax.optimization_barrier(jnp.mean(centred * centred, axis=-1, keepdims=True))
    return centred * lax.rsqrt(row_var + EPSILON) * gain_vec + shift_vec

def encoder_layer(hidden, weights, key_live):
    w_qkv, b_qv, w_out, b_out, w_up, b_up, w_down, b_down, gain_rows, shift_rows = weights
    clip_count, clip_len, model_width = hidden.shape
    normed = low(layer_norm(hidden, gain_rows[0], shift_rows[0]))
    projected = jnp.einsum('bld,jde->jble', normed, w_qkv, precision=HIGH)
    queries = low(low_back(projected[0] + b_qv[0])).reshape(clip_count, clip_len, HEADS, HD)
    keys_all = low(low_back(projected[1])).reshape(clip_count, clip_len, HEADS, HD)
    values_all = low(low_back(projected[2] + b_qv[1])).reshape(clip_count, clip_len, HEADS, HD)
    scores = low_back(jnp.einsum('bqhe,bkhe->bhqk', queries, keys_all, precision=HIGH) * (1.0 / math.sqrt(HD)))
    scores = jnp.where(key_live[:, None, None, :], scores, MASKED)
    soft_probs = jax.nn.softmax(scores, axis=-1)
    attended = jnp.einsum('bhqk,bkhe->bqhe', low(soft_probs), values_all, precision=HIGH)
    attended = low(low_back(attended)).reshape(clip_count, clip_len, model_width)
    middle = hidden + (low_back(jnp.einsum('bld,de->ble', attended, w_out, precision=HIGH)) + b_out)
    normed_two = low(layer_norm(middle, gain_rows[1], shift_rows[1]))
    pre_act = low_back(jnp.einsum('bld,df->blf', normed_two, w_up, precision=HIGH) + b_up)
    activated = low(jax.nn.gelu(pre_act, approximate=False))
    return middle + (low_back(jnp.einsum('blf,fd->bld', activated, w_down, precision=HIGH)) + b_down)

def reference(hidden_in, cotangent, lengths, qkv_weight, qv_bias, out_weight, out_bias, up_weight, up_bias, down_weight, down_bias, ln_gain, ln_bias):
    params = tuple((member_array.astype(jnp.float32) for member_array in (qkv_weight, qv_bias, out_weight, out_bias, up_weight, up_bias, down_weight, down_bias, ln_gain, ln_bias)))
    positions = jnp.arange(LEN)
    key_live = positions[None, :] < lengths[:, None]

    def network(hidden, weights):
        for layer_idx in range(LAYERS):
            hidden = encoder_layer(hidden, tuple((member_array[layer_idx] for member_array in weights)), key_live)
        return hidden
    out_hidden, network_back = jax.vjp(network, hidden_in.astype(jnp.float32), params)
    seed_grad = cotangent.astype(jnp.float32) * key_live[..., None].astype(jnp.float32)
    in_grad, param_grads = network_back(seed_grad)
    return (out_hidden, in_grad, param_grads[0], param_grads[1], param_grads[2], param_grads[3], param_grads[4], param_grads[5], param_grads[6], param_grads[7], param_grads[8], param_grads[9])
```

```python
from functools import partial
import math

import jax
import jax.numpy as jnp
from jax import lax
from jax.experimental import pallas as pl
from jax.experimental.pallas import tpu as pltpu
from jax.sharding import PartitionSpec as P

HD = 80
EPSILON = 1e-05
MASKED = -1000000000.0
MESH = pl.DeviceIdType.MESH
BF = jnp.bfloat16
F32 = jnp.float32
SCALING = 1.0 / math.sqrt(HD)

D = 1280
MICRO = 3
ROWS = 128
PART = 640
SHARDS = 16
SHARD = 80
WIDTH = 160


def dot_nn(a, b):
    return lax.dot_general(a, b, (((1,), (0,)), ((), ())), preferred_element_type=F32)


def dot_nt(a, b):
    return lax.dot_general(a, b, (((1,), (1,)), ((), ())), preferred_element_type=F32)


def dot_tn(a, b):
    return lax.dot_general(a, b, (((0,), (0,)), ((), ())), preferred_element_type=F32)


def norm_parts(values):
    row_mean = jnp.mean(values, axis=-1, keepdims=True)
    centred = values - row_mean
    row_var = jnp.mean(centred * centred, axis=-1, keepdims=True)
    inv = lax.rsqrt(row_var + EPSILON)
    return centred * inv, inv


def norm_back(grad, gain, unit, inv):
    scaled = grad * gain
    return inv * (
        scaled
        - jnp.mean(scaled, axis=-1, keepdims=True)
        - unit * jnp.mean(scaled * unit, axis=-1, keepdims=True)
    )


def split_heads(x):
    first = lax.broadcasted_iota(jnp.int32, x.shape, 1) < HD
    return jnp.concatenate([jnp.where(first, x, 0.0), jnp.where(first, 0.0, x)], axis=0)


def kernel(
    hid_ref, cot_ref, wown_ref, vec_ref, bqkv_ref, bup_ref, live_ref,
    out_ref, ingrad_ref, dwo_ref, vout_ref, bout_ref,
    W, dW, rsb, FB, BB, dr, yr, part, sb,
    qkv, kvo, prob, att, xrow, midrow, slope, act,
    gpre, gkeep, gproj, gks, gkr, gyrow, gmidrow,
    VG, V, GV, GT, vr, vr2, gb, br,
    gss, grs, rss, rrs, s1, r1, s2, r2, s3, r3, s4, r4, ks, kr, gs_s, gs_r, vs, vrs, es, er, lsem,
):
    f, s, t = lax.axis_index("fsdp"), lax.axis_index("seq"), lax.axis_index("tp")
    me = f * 2 + s
    y, core = t // 2, t % 2
    other = 1 - core

    def shard_dev(k):
        j = (me + k) % SHARDS
        return j, (j // 2, j % 2, t)

    def y_dev(k):
        j = (y + k) % 4
        return j, (f, s, j * 2 + core)

    core_dev = (f, s, y * 2 + other)
    seq_dev = (f, 1 - s, t)

    def remote(src, dst, ss, rs, dev):
        return pltpu.make_async_remote_copy(
            src_ref=src, dst_ref=dst, send_sem=ss, recv_sem=rs, device_id=dev, device_id_type=MESH
        )

    def wait_bytes(ref, sem):
        pltpu.make_async_copy(ref, ref, sem).wait()

    cp_h = pltpu.make_async_copy(hid_ref, FB.at[0], lsem.at[0])
    cp_c = pltpu.make_async_copy(cot_ref, BB.at[0], lsem.at[1])
    cp_h.start()
    cp_c.start()

    barrier = pltpu.get_barrier_semaphore()

    @pl.loop(1, SHARDS)
    def _(k):
        pl.semaphore_signal(barrier, inc=1, device_id=shard_dev(k)[1], device_id_type=MESH)

    @pl.loop(1, 8)
    def _(k):
        pl.semaphore_signal(barrier, inc=1, device_id=(f, s, (t + k) % 8), device_id_type=MESH)

    pl.semaphore_wait(barrier, 22)

    @pl.loop(1, SHARDS)
    def _(k):
        remote(vec_ref, VG.at[me], vs.at[0], vrs.at[0], shard_dev(k)[1]).start()

    VG[me] = vec_ref[...]

    def gather_start(l, p):
        @pl.loop(1, SHARDS)
        def _(k):
            remote(wown_ref.at[l, p], W.at[l, p, me], gss.at[l, p], grs.at[l, p], shard_dev(k)[1]).start()

        W[l, p, me] = wown_ref[l, p]

    def gather_wait(l, p):
        wait_bytes(W.at[l, p, pl.ds(0, SHARDS - 1)], grs.at[l, p])
        wait_bytes(W.at[l, p, pl.ds(0, SHARDS - 1)], gss.at[l, p])

    gather_start(0, 0)
    wait_bytes(VG.at[pl.ds(0, SHARDS - 1)], vrs.at[0])
    wait_bytes(VG.at[pl.ds(0, SHARDS - 1)], vs.at[0])
    V[...] = jnp.zeros_like(V)
    for i in range(SHARDS):
        low = SHARD * i // 128 * 128
        piece = VG[i].astype(F32)
        V[0, :, low : low + 256] += piece[0:8]
        V[1, :, low : low + 256] += piece[8:16]
    GV[...] = jnp.zeros_like(GV)
    gb[...] = jnp.zeros_like(gb)

    def vec(l, r):
        return V[l, r : r + 1, 0:D]

    cp_h.wait()
    cp_c.wait()
    for c in range(MICRO):
        whole = FB[0, c].reshape(ROWS, D).astype(F32)
        unit, _ = norm_parts(whole)
        xrow[0, c] = FB[0, c, y, core].astype(F32)
        FB[0, c] = (unit * vec(0, 0) + vec(0, 2)).astype(BF).reshape(4, 2, 16, D)
        gyrow[c] = BB[0, c, y, core].astype(F32)

    def rs_start(a, c, value):
        part[c] = value.astype(BF).reshape(4, 2, 16, D)
        remote(part.at[c, :, other], dr.at[a, c], s1.at[c], r1.at[a, c], core_dev).start()

    def rs_mid(a, c):
        wait_bytes(dr.at[a, c], r1.at[a, c])
        wait_bytes(dr.at[a, c], s1.at[c])
        sb[c] = (part[c, :, core].astype(F32) + dr[a, c].astype(F32)).astype(BF)
        for k in range(1, 4):
            j, dev = y_dev(k)
            remote(sb.at[c, j], yr.at[a, c, k - 1], s2.at[c], r2.at[a, c], dev).start()

    def rs_end(a, c):
        wait_bytes(yr.at[a, c], r2.at[a, c])
        wait_bytes(yr.at[a, c], s2.at[c])
        total = sb[c, y].astype(F32)
        for k in range(3):
            total = total + yr[a, c, k].astype(F32)
        return total

    def ag_start(buf, i, a, c, value):
        buf[i, c, y, core] = value.astype(BF)
        for k in range(1, 4):
            _, dev = y_dev(k)
            remote(buf.at[i, c, y, core], buf.at[i, c, y, core], s3.at[c], r3.at[a, c], dev).start()

    def ag_mid(buf, i, a, c):
        wait_bytes(yr.at[a, c], r3.at[a, c])
        wait_bytes(yr.at[a, c], s3.at[c])
        remote(buf.at[i, c, :, core], buf.at[i, c, :, core], s4.at[c], r4.at[a, c], core_dev).start()

    def ag_end(buf, i, a, c):
        wait_bytes(dr.at[a, c], r4.at[a, c])
        wait_bytes(dr.at[a, c], s4.at[c])

    def heads_of(l, c):
        own = qkv[l, c].astype(F32)
        far = kvo[l, c].astype(F32)
        q = own[:, 0:160]
        k = jnp.concatenate([own[:, 160:320], far[:, 32:192]], axis=0)
        v = jnp.concatenate([own[:, 320:480], far[:, 192:352]], axis=0)
        return split_heads(q).astype(BF), k, v

    def forward(l, carry):
        a0, a1 = 2 * l, 2 * l + 1

        @pl.when(l > 0)
        def _():
            gather_start(l, 0)

        gather_wait(l, 0)
        gather_start(l, 1)
        for c in range(MICRO):
            normed = FB[2 * l, c].reshape(ROWS, D)
            proj = dot_nn(normed, W[l, 0, :, :, 0:512].reshape(D, 512)) + bqkv_ref[l]
            qkv[l, c] = proj.astype(BF)
            remote(qkv.at[l, c, :, 128:512], kvo.at[l, c], ks.at[l, c], kr.at[l, c], seq_dev).start()
        for c in range(MICRO):
            wait_bytes(kvo.at[l, c], kr.at[l, c])
            wait_bytes(kvo.at[l, c], ks.at[l, c])
            q2, k, v = heads_of(l, c)
            scores = dot_nt(q2, k.astype(BF)) * SCALING
            scores = jnp.where(live_ref[c] > 0.0, scores, MASKED)
            top = jnp.max(scores, axis=-1, keepdims=True)
            powers = jnp.exp(scores - top)
            probs = powers / jnp.sum(powers, axis=-1, keepdims=True)
            prob[l, c] = probs
            low = probs.astype(BF)
            attended = dot_nn(
                jnp.concatenate([low[0:ROWS], low[ROWS:]], axis=1), split_heads(v).astype(BF)
            )
            wide = jnp.concatenate([jnp.zeros((ROWS, 96), F32), attended], axis=1).astype(BF)
            att[l, c] = wide
            rs_start(a0, c, dot_nt(wide, W[l, 0, :, :, 384:640].reshape(D, 256)))
        gather_wait(l, 1)
        gather_start(l, 2)
        for c in range(MICRO):
            rs_mid(a0, c)
        for c in range(MICRO):
            middle = xrow[l, c] + rs_end(a0, c) + vec(l, 4)
            midrow[l, c] = middle
            unit, _ = norm_parts(middle)
            ag_start(FB, 2 * l + 1, a0, c, unit * vec(l, 1) + vec(l, 3))
        for c in range(MICRO):
            ag_mid(FB, 2 * l + 1, a0, c)
        gather_wait(l, 2)
        for c in range(MICRO):
            ag_end(FB, 2 * l + 1, a0, c)
            normed = FB[2 * l + 1, c].reshape(ROWS, D)
            pre = dot_nn(normed, W[l, 1].reshape(D, PART)) + bup_ref[l]
            cdf = 0.5 * (1.0 + lax.erf(pre * math.sqrt(0.5)))
            activated = (pre * cdf).astype(BF)
            act[l, c] = activated
            slope[l, c] = cdf + pre * jnp.exp(-0.5 * pre * pre) * (1.0 / math.sqrt(2.0 * math.pi))
            rs_start(a1, c, dot_nt(activated, W[l, 2].reshape(D, PART)))
        for c in range(MICRO):
            rs_mid(a1, c)
        following = lax.rem(l + 1, 2)
        for c in range(MICRO):
            hidden = midrow[l, c] + rs_end(a1, c) + vec(l, 5)
            xrow[l + 1, c] = hidden
            unit, _ = norm_parts(hidden)
            normed = unit * vec(following, 0) + vec(following, 2)
            ag_start(FB, 2 * l + 2, a1, c, jnp.where(l == 1, hidden, normed))
        for c in range(MICRO):
            ag_mid(FB, 2 * l + 2, a1, c)
        for c in range(MICRO):
            ag_end(FB, 2 * l + 2, a1, c)
        return carry

    lax.fori_loop(0, 2, forward, 0)
    cp_o = pltpu.make_async_copy(FB.at[4], out_ref, lsem.at[0])
    cp_o.start()

    def send_part(l, p):
        @pl.loop(1, SHARDS)
        def _(k):
            j, dev = shard_dev(k)
            remote(dW.at[l, p, j], rsb.at[l, p, k - 1], rss.at[l, p], rrs.at[l, p], dev).start()

    def weight_grad(l, p, buf, i, right):
        @pl.loop(0, 2)
        def _(m):
            left = buf[i, :, :, :, :, pl.ds(pl.multiple_of(m * 640, 128), 640)].reshape(MICRO * ROWS, 640)
            dW[l, p, pl.ds(m * 8, 8)] = dot_tn(left, right).astype(BF).reshape(8, SHARD, PART)

        send_part(l, p)

    def backward(j, carry):
        l = 1 - j
        a0, a1 = 4 + 2 * j, 5 + 2 * j
        b0, b1, b2 = 2 * j, 2 * j + 1, 2 * j + 2
        for c in range(MICRO):
            grad_act = dot_nn(BB[b0, c].reshape(ROWS, D), W[l, 2].reshape(D, PART))
            grad_pre = (grad_act * slope[l, c]).astype(BF)
            gpre[c] = grad_pre
            gb[pl.ds(2 + l, 1), :] += jnp.sum(grad_pre.astype(F32), axis=0, keepdims=True)
            rs_start(a0, c, dot_nt(grad_pre, W[l, 1].reshape(D, PART)))
        weight_grad(l, 2, BB, b0, act[l].reshape(MICRO * ROWS, PART))
        for c in range(MICRO):
            rs_mid(a0, c)
        for c in range(MICRO):
            grad_norm = rs_end(a0, c)
            unit, inv = norm_parts(midrow[l, c])
            gy = gyrow[c]
            grad_mid = gy + norm_back(grad_norm, vec(l, 1), unit, inv)
            gmidrow[c] = grad_mid
            GV[l, 1:2, 0:D] += jnp.sum(grad_norm * unit, axis=0, keepdims=True)
            GV[l, 3:4, 0:D] += jnp.sum(grad_norm, axis=0, keepdims=True)
            GV[l, 4:5, 0:D] += jnp.sum(grad_mid, axis=0, keepdims=True)
            GV[l, 5:6, 0:D] += jnp.sum(gy, axis=0, keepdims=True)
            ag_start(BB, b1, a0, c, grad_mid)
        weight_grad(l, 1, FB, 2 * l + 1, gpre[...].reshape(MICRO * ROWS, PART))
        for c in range(MICRO):
            ag_mid(BB, b1, a0, c)
        for c in range(MICRO):
            ag_end(BB, b1, a0, c)
            wide = dot_nn(BB[b1, c].reshape(ROWS, D), W[l, 0, :, :, 384:640].reshape(D, 256))
            ga2 = split_heads(wide[:, 96:256]).astype(BF)
            q2, k, v = heads_of(l, c)
            probs = prob[l, c]
            grad_probs = dot_nt(ga2, v.astype(BF))
            grad_scores = probs * (
                grad_probs - jnp.sum(probs * grad_probs, axis=-1, keepdims=True)
            )
            low = grad_scores.astype(BF)
            grad_v = dot_tn(probs.astype(BF), ga2)
            grad_k = dot_tn(low, q2) * SCALING
            grad_q = (
                dot_nn(
                    jnp.concatenate([low[0:ROWS], low[ROWS:]], axis=1), split_heads(k).astype(BF)
                )
                * SCALING
            )
            pad = jnp.zeros((ROWS, 64), F32)
            gks[c] = jnp.concatenate([grad_k[ROWS:], grad_v[ROWS:], pad], axis=1).astype(BF)
            remote(gks.at[c], gkr.at[l, c], gs_s.at[c], gs_r.at[l, c], seq_dev).start()
            gkeep[c, :, 0:160] = grad_q
            gkeep[c, :, 160:320] = grad_k[0:ROWS]
            gkeep[c, :, 320:480] = grad_v[0:ROWS]
            gkeep[c, :, 480:512] = jnp.zeros((ROWS, 32), F32)
        for c in range(MICRO):
            wait_bytes(gkr.at[l, c], gs_r.at[l, c])
            wait_bytes(gkr.at[l, c], gs_s.at[c])
            far = gkr[l, c].astype(F32)
            gkeep[c, :, 160:480] += far[:, 0:320]
            grads = gkeep[c].astype(BF)
            gproj[c] = grads
            gb[pl.ds(l, 1), 0:512] += jnp.sum(grads.astype(F32), axis=0, keepdims=True)
            rs_start(a1, c, dot_nt(grads, W[l, 0, :, :, 0:512].reshape(D, 512)))

        @pl.loop(0, 2)
        def _(m):
            lanes = pl.ds(pl.multiple_of(m * 640, 128), 640)
            left = FB[2 * l, :, :, :, :, lanes].reshape(MICRO * ROWS, 640)
            first = dot_tn(left, gproj[...].reshape(MICRO * ROWS, 512))
            left_two = BB[b1, :, :, :, :, lanes].reshape(MICRO * ROWS, 640)
            second = dot_tn(left_two, att[l].reshape(MICRO * ROWS, 256))
            rows = pl.ds(m * 8, 8)
            dW[l, 0, rows, :, 0:384] = first[:, 0:384].astype(BF).reshape(8, SHARD, 384)
            dW[l, 0, rows, :, 384:512] = (first[:, 384:512] + second[:, 0:128]).astype(BF).reshape(8, SHARD, 128)
            dW[l, 0, rows, :, 512:640] = second[:, 128:256].astype(BF).reshape(8, SHARD, 128)

        send_part(l, 0)
        for c in range(MICRO):
            rs_mid(a1, c)
        for c in range(MICRO):
            grad_norm = rs_end(a1, c)
            unit, inv = norm_parts(xrow[l, c])
            gy = gmidrow[c] + norm_back(grad_norm, vec(l, 0), unit, inv)
            gyrow[c] = gy
            GV[l, 0:1, 0:D] += jnp.sum(grad_norm * unit, axis=0, keepdims=True)
            GV[l, 2:3, 0:D] += jnp.sum(grad_norm, axis=0, keepdims=True)
            ag_start(BB, b2, a1, c, gy)
        for c in range(MICRO):
            ag_mid(BB, b2, a1, c)
        for c in range(MICRO):
            ag_end(BB, b2, a1, c)
        return carry

    lax.fori_loop(0, 2, backward, 0)
    cp_g = pltpu.make_async_copy(BB.at[4], ingrad_ref, lsem.at[1])
    cp_g.start()

    for i in range(11):
        GT[i, 0:8] = GV[0, :, 128 * i : 128 * i + 128]
        GT[i, 8:16] = GV[1, :, 128 * i : 128 * i + 128]

    @pl.loop(1, SHARDS)
    def _(k):
        j, dev = shard_dev(k)
        remote(GT.at[pl.ds(SHARD * j // 128, 2)], vr.at[k - 1], es.at[0], er.at[0], dev).start()
        remote(gb, br.at[k - 1], es.at[1], er.at[1], dev).start()

    wait_bytes(vr, er.at[0])
    wait_bytes(vr, es.at[0])
    own = GT[pl.ds(SHARD * me // 128, 2)]
    for k in range(SHARDS - 1):
        own = own + vr[k]
    vr2[7] = own

    @pl.loop(1, 8)
    def _(k):
        remote(vr2.at[7], vr2.at[k - 1], es.at[2], er.at[2], (f, s, (t + k) % 8)).start()

    wait_bytes(br, er.at[1])
    wait_bytes(br, es.at[1])
    sums = gb[...]
    for k in range(SHARDS - 1):
        sums = sums + br[k]
    bout_ref[...] = sums

    for l in (1, 0):
        for p in (2, 1, 0):
            wait_bytes(rsb.at[l, p], rrs.at[l, p])
            wait_bytes(rsb.at[l, p], rss.at[l, p])
            total = dW[l, p, me].astype(F32)
            for k in range(SHARDS - 1):
                total = total + rsb[l, p, k].astype(F32)
            dwo_ref[l, p] = total

    wait_bytes(vr2.at[pl.ds(0, 7)], er.at[2])
    wait_bytes(vr2.at[pl.ds(0, 7)], es.at[2])
    own = vr2[7]
    for k in range(7):
        own = own + vr2[k]
    vout_ref[...] = own
    cp_o.wait()
    cp_g.wait()


def body(
    hidden_in, cotangent, lengths, qkv_weight, qv_bias, out_weight, out_bias,
    up_weight, up_bias, down_weight, down_bias, ln_gain, ln_bias,
):
    seq = lax.axis_index("seq")
    me = lax.axis_index("fsdp") * 2 + seq
    own_pos = seq * ROWS + jnp.arange(ROWS)
    far_pos = (1 - seq) * ROWS + jnp.arange(ROWS)
    keys = jnp.concatenate([own_pos, far_pos])
    live = (keys[None, :] < lengths[:, None]).astype(F32).reshape(MICRO, 1, 2 * ROWS)
    cot = jnp.where((own_pos[None, :] < lengths[:, None])[..., None], cotangent, jnp.zeros((), BF))
    first = jnp.concatenate(
        [qkv_weight[:, 0], qkv_weight[:, 1], qkv_weight[:, 2], jnp.swapaxes(out_weight, 1, 2)], axis=2
    )
    wown = jnp.stack([first, up_weight, jnp.swapaxes(down_weight, 1, 2)], axis=1)
    vectors = jnp.stack(
        [ln_gain[:, 0], ln_gain[:, 1], ln_bias[:, 0], ln_bias[:, 1], out_bias, down_bias], axis=1
    )
    vectors = jnp.pad(vectors, ((0, 0), (0, 2), (0, 0))).reshape(16, SHARD)
    offset = lax.rem(SHARD * me, 128)
    vectors = lax.dynamic_update_slice(jnp.zeros((16, 256), BF), vectors, (0, offset))
    zero = jnp.zeros((2, WIDTH), F32)
    qv = qv_bias.astype(F32)
    bqkv = jnp.concatenate([qv[:, 0], zero, qv[:, 1], zero[:, 0:32]], axis=1).reshape(2, 1, 512)
    bup = up_bias.astype(F32).reshape(2, 1, PART)

    vmem = pl.BlockSpec(memory_space=pltpu.VMEM)
    anys = pl.BlockSpec(memory_space=pl.ANY)
    dma = pltpu.SemaphoreType.DMA
    blocks = (MICRO, 4, 2, 16, D)
    scratch = [
        pltpu.VMEM((2, 3, SHARDS, SHARD, PART), BF),
        pltpu.VMEM((2, 3, SHARDS, SHARD, PART), BF),
        pltpu.VMEM((2, 3, SHARDS - 1, SHARD, PART), BF),
        pltpu.VMEM((5,) + blocks, BF),
        pltpu.VMEM((5,) + blocks, BF),
        pltpu.VMEM((8, MICRO, 4, 16, D), BF),
        pltpu.VMEM((8, MICRO, 3, 16, D), BF),
        pltpu.VMEM(blocks, BF),
        pltpu.VMEM((MICRO, 4, 16, D), BF),
        pltpu.VMEM((2, MICRO, ROWS, 512), BF),
        pltpu.VMEM((2, MICRO, ROWS, 384), BF),
        pltpu.VMEM((2, MICRO, 2 * ROWS, 2 * ROWS), F32),
        pltpu.VMEM((2, MICRO, ROWS, 256), BF),
        pltpu.VMEM((3, MICRO, 16, D), F32),
        pltpu.VMEM((2, MICRO, 16, D), F32),
        pltpu.VMEM((2, MICRO, ROWS, PART), F32),
        pltpu.VMEM((2, MICRO, ROWS, PART), BF),
        pltpu.VMEM((MICRO, ROWS, PART), BF),
        pltpu.VMEM((MICRO, ROWS, 512), F32),
        pltpu.VMEM((MICRO, ROWS, 512), BF),
        pltpu.VMEM((MICRO, ROWS, 384), BF),
        pltpu.VMEM((2, MICRO, ROWS, 384), BF),
        pltpu.VMEM((MICRO, 16, D), F32),
        pltpu.VMEM((MICRO, 16, D), F32),
        pltpu.VMEM((SHARDS, 16, 256), BF),
        pltpu.VMEM((2, 8, 1408), F32),
        pltpu.VMEM((2, 8, 1408), F32),
        pltpu.VMEM((11, 16, 128), F32),
        pltpu.VMEM((SHARDS - 1, 2, 16, 128), F32),
        pltpu.VMEM((8, 2, 16, 128), F32),
        pltpu.VMEM((8, PART), F32),
        pltpu.VMEM((SHARDS - 1, 8, PART), F32),
        dma((2, 3)), dma((2, 3)), dma((2, 3)), dma((2, 3)),
        dma((MICRO,)), dma((8, MICRO)), dma((MICRO,)), dma((8, MICRO)),
        dma((MICRO,)), dma((8, MICRO)), dma((MICRO,)), dma((8, MICRO)),
        dma((2, MICRO)), dma((2, MICRO)), dma((MICRO,)), dma((2, MICRO)),
        dma((1,)), dma((1,)), dma((3,)), dma((3,)), dma((2,)),
    ]
    out, ingrad, dwo, vout, bout = pl.pallas_call(
        kernel,
        name="encoder",
        out_shape=(
            jax.ShapeDtypeStruct(blocks, BF),
            jax.ShapeDtypeStruct(blocks, BF),
            jax.ShapeDtypeStruct((2, 3, SHARD, PART), F32),
            jax.ShapeDtypeStruct((2, 16, 128), F32),
            jax.ShapeDtypeStruct((8, PART), F32),
        ),
        in_specs=[anys, anys, vmem, vmem, vmem, vmem, vmem],
        out_specs=(anys, anys, vmem, vmem, vmem),
        scratch_shapes=scratch,
        compiler_params=pltpu.CompilerParams(
            collective_id=0, has_side_effects=True, vmem_limit_bytes=63 * 1024 * 1024
        ),
    )(hidden_in.reshape(blocks), cot.reshape(blocks), wown, vectors, bqkv, bup, live)

    out_hidden = out.reshape(MICRO, ROWS, D).astype(F32)
    in_grad = ingrad.reshape(MICRO, ROWS, D).astype(F32)
    first = dwo[:, 0]
    qkv_grad = jnp.stack([first[:, :, 0:160], first[:, :, 160:320], first[:, :, 320:480]], axis=1)
    out_grad = jnp.swapaxes(first[:, :, 480:640], 1, 2)
    up_grad = dwo[:, 1]
    down_grad = jnp.swapaxes(dwo[:, 2], 1, 2)
    rows = jnp.swapaxes(vout, 0, 1).reshape(16, 256)
    rows = lax.dynamic_slice(rows, (0, offset), (16, SHARD)).reshape(2, 8, SHARD)
    gain_grad = rows[:, 0:2]
    shift_grad = rows[:, 2:4]
    qv_grad = jnp.stack([bout[0:2, 0:160], bout[0:2, 320:480]], axis=1)
    return (
        out_hidden, in_grad, qkv_grad, qv_grad, out_grad, rows[:, 4], up_grad,
        bout[2:4], down_grad, rows[:, 5], gain_grad, shift_grad,
    )


def solution(mesh):
    placed = (
        P("fsdp", "seq", None),
        P("fsdp", "seq", None),
        P("fsdp"),
        P(None, None, ("fsdp", "seq"), "tp"),
        P(None, None, "tp"),
        P(None, "tp", ("fsdp", "seq")),
        P(None, ("fsdp", "seq")),
        P(None, ("fsdp", "seq"), "tp"),
        P(None, "tp"),
        P(None, "tp", ("fsdp", "seq")),
        P(None, ("fsdp", "seq")),
        P(None, None, ("fsdp", "seq")),
        P(None, None, ("fsdp", "seq")),
    )
    return jax.shard_map(
        body,
        mesh=mesh,
        in_specs=placed,
        out_specs=(
            P("fsdp", "seq", None),
            P("fsdp", "seq", None),
            P(None, None, ("fsdp", "seq"), "tp"),
            P(None, None, "tp"),
            P(None, "tp", ("fsdp", "seq")),
            P(None, ("fsdp", "seq")),
            P(None, ("fsdp", "seq"), "tp"),
            P(None, "tp"),
            P(None, "tp", ("fsdp", "seq")),
            P(None, ("fsdp", "seq")),
            P(None, None, ("fsdp", "seq")),
            P(None, None, ("fsdp", "seq")),
        ),
        check_vma=False,
    )
```

```python
from functools import partial
import math

import jax
import jax.numpy as jnp
from jax import lax
from jax.experimental import pallas as pl
from jax.experimental.pallas import tpu as pltpu
from jax.sharding import PartitionSpec as P

HD = 80
EPSILON = 1e-05
MASKED = -1000000000.0
MESH = pl.DeviceIdType.MESH
BF = jnp.bfloat16
F32 = jnp.float32
SCALING = 1.0 / math.sqrt(HD)

D = 1280
MICRO = 3
ROWS = 128
PART = 640
SHARDS = 16
SHARD = 80
WIDTH = 160

PIECES = (
    (0, (256, 512), (0, 256)),
    (0, (512, 640), None),
    (1, (384, 640), (0, 384)),
    (2, (384, 640), (0, 384)),
)
QKV, OUT, UP, DOWN = range(4)


def dot_nn(a, b):
    return lax.dot_general(a, b, (((1,), (0,)), ((), ())), preferred_element_type=F32)


def dot_nt(a, b):
    return lax.dot_general(a, b, (((1,), (1,)), ((), ())), preferred_element_type=F32)


def dot_tn(a, b):
    return lax.dot_general(a, b, (((0,), (0,)), ((), ())), preferred_element_type=F32)


def norm_parts(values):
    row_mean = jnp.mean(values, axis=-1, keepdims=True)
    centred = values - row_mean
    row_var = jnp.mean(centred * centred, axis=-1, keepdims=True)
    inv = lax.rsqrt(row_var + EPSILON)
    return centred * inv, inv


def norm_back(grad, gain, unit, inv):
    scaled = grad * gain
    return inv * (
        scaled
        - jnp.mean(scaled, axis=-1, keepdims=True)
        - unit * jnp.mean(scaled * unit, axis=-1, keepdims=True)
    )


def split_heads(x):
    first = lax.broadcasted_iota(jnp.int32, x.shape, 1) < HD
    return jnp.concatenate([jnp.where(first, x, 0.0), jnp.where(first, 0.0, x)], axis=0)


def kernel(
    hid_ref, cot_ref, wown_ref, vec_ref, bqkv_ref, bup_ref, live_ref,
    out_ref, ingrad_ref, dwo_ref, vout_ref, bout_ref,
    W, dW, rb1, rb2, rc, FB, BB, dr, yr, part, sb,
    qkv, kvo, prob, att, xrow, midrow, slope, act,
    gpre, gkeep, gproj, gks, gkr, gyrow, gmidrow,
    VG, V, GV, GT, vr, vr2, gb, br,
    g1s, g1r, g2s, g2r, q1s, q1r, q2s, q2r,
    s1, r1, s2, r2, s3, r3, s4, r4, ks, kr, gs_s, gs_r, vs, vrs, es, er, lsem,
):
    f, s, t = lax.axis_index("fsdp"), lax.axis_index("seq"), lax.axis_index("tp")
    me = f * 2 + s
    xh, z = f // 4, f % 4
    x = xh * 2 + s
    y, core = t // 2, t % 2
    other = 1 - core

    def shard_dev(k):
        j = (me + k) % SHARDS
        return j, (j // 2, j % 2, t)

    def x_dev(k):
        j = (x + k) % 4
        return j // 2, j % 2, ((j // 2) * 4 + z, j % 2, t)

    def z_dev(k):
        j = (z + k) % 4
        return j, (xh * 4 + j, s, t)

    def y_dev(k):
        j = (y + k) % 4
        return j, (f, s, j * 2 + core)

    core_dev = (f, s, y * 2 + other)
    seq_dev = (f, 1 - s, t)

    def remote(src, dst, ss, rs, dev):
        return pltpu.make_async_remote_copy(
            src_ref=src, dst_ref=dst, send_sem=ss, recv_sem=rs, device_id=dev, device_id_type=MESH
        )

    def wait_bytes(ref, sem):
        pltpu.make_async_copy(ref, ref, sem).wait()

    cp_h = pltpu.make_async_copy(hid_ref, FB.at[0], lsem.at[0])
    cp_c = pltpu.make_async_copy(cot_ref, BB.at[0], lsem.at[1])
    cp_h.start()
    cp_c.start()

    barrier = pltpu.get_barrier_semaphore()

    @pl.loop(1, SHARDS)
    def _(k):
        pl.semaphore_signal(barrier, inc=1, device_id=shard_dev(k)[1], device_id_type=MESH)

    @pl.loop(1, 8)
    def _(k):
        pl.semaphore_signal(barrier, inc=1, device_id=(f, s, (t + k) % 8), device_id_type=MESH)

    pl.semaphore_wait(barrier, 22)

    def piece(l, i):
        part_idx, one, two = PIECES[i]
        both = [(0, slice(*one))] + ([(1, slice(*two))] if two else [])
        return part_idx, both

    def gather_one(l, i):
        p, ways = piece(l, i)
        for way, cols in ways:
            W[l, p, xh, z, s, :, cols] = wown_ref[l, p, :, cols]
            own = W.at[l, p, xh, z, s, :, cols]
            for k in range(1, 4):
                dev = x_dev(k)[2] if way else z_dev(k)[1]
                remote(own, own, g1s.at[l, i, way], g1r.at[l, i, way], dev).start()

    def gather_mid(l, i):
        p, ways = piece(l, i)
        for way, cols in ways:
            three = W.at[l, p, 0, pl.ds(0, 3), 0, :, cols]
            wait_bytes(three, g1r.at[l, i, way])
            wait_bytes(three, g1s.at[l, i, way])

    def gather_two(l, i):
        p, ways = piece(l, i)
        gather_mid(l, i)
        for way, cols in ways:
            four = W.at[l, p, :, z, :, :, cols] if way else W.at[l, p, xh, :, s, :, cols]
            for k in range(1, 4):
                dev = z_dev(k)[1] if way else x_dev(k)[2]
                remote(four, four, g2s.at[l, i, way], g2r.at[l, i, way], dev).start()

    def gather_wait(l, i):
        p, ways = piece(l, i)
        for way, cols in ways:
            twelve = W.at[l, p, :, pl.ds(0, 3), :, :, cols]
            wait_bytes(twelve, g2r.at[l, i, way])
            wait_bytes(twelve, g2s.at[l, i, way])

    def reduce_one(l, i):
        p, ways = piece(l, i)
        for way, cols in ways:
            for k in range(1, 4):
                if way:
                    j, dev = z_dev(k)
                    four = dW.at[l, p, :, j, :, :, cols]
                    buf = rb2.at[l, p, k - 1, :, :, :, 0 : cols.stop - cols.start]
                else:
                    jh, jl, dev = x_dev(k)
                    four = dW.at[l, p, jh, :, jl, :, cols]
                    buf = rb1.at[l, p, k - 1, :, :, cols.start - 256 : cols.stop - 256]
                remote(four, buf, q1s.at[l, i, way], q1r.at[l, i, way], dev).start()

    def reduce_mid(l, i):
        p, ways = piece(l, i)
        for way, cols in ways:
            twelve = dW.at[l, p, :, pl.ds(0, 3), :, :, cols]
            wait_bytes(twelve, q1r.at[l, i, way])
            wait_bytes(twelve, q1s.at[l, i, way])

    def reduce_two(l, i):
        p, ways = piece(l, i)
        reduce_mid(l, i)

        @pl.loop(0, 4)
        def _(n):
            nh, nl = n // 2, n % 2
            for way, cols in ways:
                if way:
                    total = dW[l, p, nh, z, nl, :, cols].astype(F32)
                    for k in range(3):
                        total = total + rb2[l, p, k, nh, nl, :, 0 : cols.stop - cols.start].astype(F32)
                    dW[l, p, nh, z, nl, :, cols] = total.astype(BF)
                else:
                    total = dW[l, p, xh, n, s, :, cols].astype(F32)
                    for k in range(3):
                        total = total + rb1[l, p, k, n, :, cols.start - 256 : cols.stop - 256].astype(F32)
                    dW[l, p, xh, n, s, :, cols] = total.astype(BF)

        for way, cols in ways:
            for k in range(1, 4):
                if way:
                    jh, jl, dev = x_dev(k)
                    one = dW.at[l, p, jh, z, jl, :, cols]
                else:
                    j, dev = z_dev(k)
                    one = dW.at[l, p, xh, j, s, :, cols]
                remote(one, rc.at[l, p, k - 1, :, cols], q2s.at[l, i, way], q2r.at[l, i, way], dev).start()

    def reduce_last(l, i):
        p, ways = piece(l, i)
        for way, cols in ways:
            three = dW.at[l, p, 0, pl.ds(0, 3), 0, :, cols]
            wait_bytes(three, q2r.at[l, i, way])
            wait_bytes(three, q2s.at[l, i, way])

    def reduce_three(l, i):
        p, ways = piece(l, i)
        reduce_last(l, i)
        for way, cols in ways:
            total = dW[l, p, xh, z, s, :, cols].astype(F32)
            for k in range(3):
                total = total + rc[l, p, k, :, cols].astype(F32)
            dwo_ref[l, p, :, cols] = total

    def vec(l, r):
        return V[l, r : r + 1, 0:D]

    def rs_start(a, c, value):
        part[c] = value.astype(BF).reshape(4, 2, 16, D)
        remote(part.at[c, :, other], dr.at[a, c], s1.at[c], r1.at[a, c], core_dev).start()

    def rs_mid(a, c):
        wait_bytes(dr.at[a, c], r1.at[a, c])
        wait_bytes(dr.at[a, c], s1.at[c])
        sb[c] = (part[c, :, core].astype(F32) + dr[a, c].astype(F32)).astype(BF)
        for k in range(1, 4):
            j, dev = y_dev(k)
            remote(sb.at[c, j], yr.at[a, c, k - 1], s2.at[c], r2.at[a, c], dev).start()

    def rs_end(a, c):
        wait_bytes(yr.at[a, c], r2.at[a, c])
        wait_bytes(yr.at[a, c], s2.at[c])
        total = sb[c, y].astype(F32)
        for k in range(3):
            total = total + yr[a, c, k].astype(F32)
        return total

    def ag_start(buf, i, a, c, value):
        buf[i, c, y, core] = value.astype(BF)
        for k in range(1, 4):
            _, dev = y_dev(k)
            remote(buf.at[i, c, y, core], buf.at[i, c, y, core], s3.at[c], r3.at[a, c], dev).start()

    def ag_mid(buf, i, a, c):
        wait_bytes(yr.at[a, c], r3.at[a, c])
        wait_bytes(yr.at[a, c], s3.at[c])
        remote(buf.at[i, c, :, core], buf.at[i, c, :, core], s4.at[c], r4.at[a, c], core_dev).start()

    def ag_end(a, c):
        wait_bytes(dr.at[a, c], r4.at[a, c])
        wait_bytes(dr.at[a, c], s4.at[c])

    def heads_of(l, c):
        own = qkv[l, c].astype(F32)
        far = kvo[l, c].astype(F32)
        q = own[:, 0:160]
        k = jnp.concatenate([own[:, 160:320], far[:, 32:192]], axis=0)
        v = jnp.concatenate([own[:, 320:480], far[:, 192:352]], axis=0)
        return split_heads(q).astype(BF), k, v

    def project(l, c):
        normed = FB[2 * l, c].reshape(ROWS, D)
        proj = dot_nn(normed, W[l, 0, :, :, :, :, 0:512].reshape(D, 512)) + bqkv_ref[l]
        qkv[l, c] = proj.astype(BF)
        remote(qkv.at[l, c, :, 128:512], kvo.at[l, c], ks.at[l, c], kr.at[l, c], seq_dev).start()

    def attend(l, c):
        wait_bytes(kvo.at[l, c], kr.at[l, c])
        wait_bytes(kvo.at[l, c], ks.at[l, c])
        q2, k, v = heads_of(l, c)
        scores = dot_nt(q2, k.astype(BF)) * SCALING
        scores = jnp.where(live_ref[c] > 0.0, scores, MASKED)
        top = jnp.max(scores, axis=-1, keepdims=True)
        powers = jnp.exp(scores - top)
        probs = powers / jnp.sum(powers, axis=-1, keepdims=True)
        prob[l, c] = probs
        low = probs.astype(BF)
        attended = dot_nn(
            jnp.concatenate([low[0:ROWS], low[ROWS:]], axis=1), split_heads(v).astype(BF)
        )
        wide = jnp.concatenate([jnp.zeros((ROWS, 96), F32), attended], axis=1).astype(BF)
        att[l, c] = wide
        rs_start(2 * l, c, dot_nt(wide, W[l, 0, :, :, :, :, 384:640].reshape(D, 256)))

    def attend_rows(l, c):
        a = 2 * l
        middle = xrow[l, c] + rs_end(a, c) + vec(l, 4)
        midrow[l, c] = middle
        unit, _ = norm_parts(middle)
        ag_start(FB, 2 * l + 1, a, c, unit * vec(l, 1) + vec(l, 3))

    def feed(l, c):
        normed = FB[2 * l + 1, c].reshape(ROWS, D)
        pre = dot_nn(normed, W[l, 1].reshape(D, PART)) + bup_ref[l]
        cdf = 0.5 * (1.0 + lax.erf(pre * math.sqrt(0.5)))
        activated = (pre * cdf).astype(BF)
        act[l, c] = activated
        slope[l, c] = cdf + pre * jnp.exp(-0.5 * pre * pre) * (1.0 / math.sqrt(2.0 * math.pi))
        rs_start(2 * l + 1, c, dot_nt(activated, W[l, 2].reshape(D, PART)))

    def feed_rows(l, c):
        a = 2 * l + 1
        hidden = midrow[l, c] + rs_end(a, c) + vec(l, 5)
        if l == 0:
            xrow[1, c] = hidden
            unit, _ = norm_parts(hidden)
            hidden = unit * vec(1, 0) + vec(1, 2)
        ag_start(FB, 2 * l + 2, a, c, hidden)

    def feed_back(l, c):
        grad_act = dot_nn(BB[2 - 2 * l, c].reshape(ROWS, D), W[l, 2].reshape(D, PART))
        grad_pre = (grad_act * slope[l, c]).astype(BF)
        gpre[c] = grad_pre
        gb[2 + l : 3 + l, :] += jnp.sum(grad_pre.astype(F32), axis=0, keepdims=True)
        rs_start(6 - 2 * l, c, dot_nt(grad_pre, W[l, 1].reshape(D, PART)))

    def feed_back_rows(l, c):
        a = 6 - 2 * l
        grad_norm = rs_end(a, c)
        unit, inv = norm_parts(midrow[l, c])
        gy = gyrow[c]
        grad_mid = gy + norm_back(grad_norm, vec(l, 1), unit, inv)
        gmidrow[c] = grad_mid
        ag_start(BB, 3 - 2 * l, a, c, grad_mid)
        GV[l, 1:2, 0:D] += jnp.sum(grad_norm * unit, axis=0, keepdims=True)
        GV[l, 3:4, 0:D] += jnp.sum(grad_norm, axis=0, keepdims=True)
        GV[l, 4:5, 0:D] += jnp.sum(grad_mid, axis=0, keepdims=True)
        GV[l, 5:6, 0:D] += jnp.sum(gy, axis=0, keepdims=True)

    def attend_back(l, c):
        wide = dot_nn(BB[3 - 2 * l, c].reshape(ROWS, D), W[l, 0, :, :, :, :, 384:640].reshape(D, 256))
        ga2 = split_heads(wide[:, 96:256]).astype(BF)
        q2, k, v = heads_of(l, c)
        probs = prob[l, c]
        grad_probs = dot_nt(ga2, v.astype(BF))
        grad_scores = probs * (grad_probs - jnp.sum(probs * grad_probs, axis=-1, keepdims=True))
        low = grad_scores.astype(BF)
        grad_v = dot_tn(probs.astype(BF), ga2)
        grad_k = dot_tn(low, q2) * SCALING
        pad = jnp.zeros((ROWS, 64), F32)
        gks[c] = jnp.concatenate([grad_k[ROWS:], grad_v[ROWS:], pad], axis=1).astype(BF)
        remote(gks.at[c], gkr.at[l, c], gs_s.at[c], gs_r.at[l, c], seq_dev).start()
        grad_q = (
            dot_nn(jnp.concatenate([low[0:ROWS], low[ROWS:]], axis=1), split_heads(k).astype(BF))
            * SCALING
        )
        gkeep[c, :, 0:160] = grad_q
        gkeep[c, :, 160:320] = grad_k[0:ROWS]
        gkeep[c, :, 320:480] = grad_v[0:ROWS]
        gkeep[c, :, 480:512] = jnp.zeros((ROWS, 32), F32)

    def project_back(l, c):
        wait_bytes(gkr.at[l, c], gs_r.at[l, c])
        wait_bytes(gkr.at[l, c], gs_s.at[c])
        far = gkr[l, c].astype(F32)
        gkeep[c, :, 160:480] += far[:, 0:320]
        grads = gkeep[c].astype(BF)
        gproj[c] = grads
        gb[l : l + 1, 0:512] += jnp.sum(grads.astype(F32), axis=0, keepdims=True)
        rs_start(7 - 2 * l, c, dot_nt(grads, W[l, 0, :, :, :, :, 0:512].reshape(D, 512)))

    def project_back_rows(l, c):
        a = 7 - 2 * l
        grad_norm = rs_end(a, c)
        unit, inv = norm_parts(xrow[l, c])
        gy = gmidrow[c] + norm_back(grad_norm, vec(l, 0), unit, inv)
        gyrow[c] = gy
        ag_start(BB, 4 - 2 * l, a, c, gy)
        GV[l, 0:1, 0:D] += jnp.sum(grad_norm * unit, axis=0, keepdims=True)
        GV[l, 2:3, 0:D] += jnp.sum(grad_norm, axis=0, keepdims=True)

    def left_of(buf, i, m):
        return buf[i, :, :, :, :, 640 * m : 640 * m + 640].reshape(MICRO * ROWS, 640)

    def down_grad(l, m):
        right = act[l].reshape(MICRO * ROWS, PART)
        dW[l, 2, m] = dot_tn(left_of(BB, 2 - 2 * l, m), right).astype(BF).reshape(4, 2, SHARD, PART)

    def up_grad(l, m):
        right = gpre[...].reshape(MICRO * ROWS, PART)
        dW[l, 1, m] = dot_tn(left_of(FB, 2 * l + 1, m), right).astype(BF).reshape(4, 2, SHARD, PART)

    def out_grad(l, m):
        grad = dot_tn(left_of(BB, 3 - 2 * l, m), att[l].reshape(MICRO * ROWS, 256))
        dW[l, 0, m, :, :, :, 384:640] = grad.astype(BF).reshape(4, 2, SHARD, 256)

    def qkv_grad(l, m):
        grad = dot_tn(left_of(FB, 2 * l, m), gproj[...].reshape(MICRO * ROWS, 512))
        dW[l, 0, m, :, :, :, 0:384] = grad[:, 0:384].astype(BF).reshape(4, 2, SHARD, 384)
        rest = dW[l, 0, m, :, :, :, 384:512].astype(F32).reshape(640, 128) + grad[:, 384:512]
        dW[l, 0, m, :, :, :, 384:512] = rest.astype(BF).reshape(4, 2, SHARD, 128)

    @pl.loop(1, SHARDS)
    def _(k):
        remote(vec_ref, VG.at[me], vs.at[0], vrs.at[0], shard_dev(k)[1]).start()

    VG[me] = vec_ref[...]
    gather_one(0, QKV)
    V[...] = jnp.zeros_like(V)
    GV[...] = jnp.zeros_like(GV)
    gb[...] = jnp.zeros_like(gb)
    gather_two(0, QKV)
    gather_one(0, OUT)
    gather_one(0, UP)
    wait_bytes(VG.at[pl.ds(0, SHARDS - 1)], vrs.at[0])
    wait_bytes(VG.at[pl.ds(0, SHARDS - 1)], vs.at[0])
    for i in range(SHARDS):
        low = SHARD * i // 128 * 128
        held = VG[i].astype(F32)
        V[0, :, low : low + 256] += held[0:8]
        V[1, :, low : low + 256] += held[8:16]
    cp_h.wait()
    cp_c.wait()
    for c in range(MICRO):
        whole = FB[0, c].reshape(ROWS, D).astype(F32)
        unit, _ = norm_parts(whole)
        xrow[0, c] = FB[0, c, y, core].astype(F32)
        FB[0, c] = (unit * vec(0, 0) + vec(0, 2)).astype(BF).reshape(4, 2, 16, D)
        gyrow[c] = BB[0, c, y, core].astype(F32)
    gather_two(0, OUT)
    gather_wait(0, QKV)
    gather_two(0, UP)
    gather_one(0, DOWN)

    cp_o = pltpu.make_async_copy(FB.at[4], out_ref, lsem.at[0])
    cp_g = pltpu.make_async_copy(BB.at[4], ingrad_ref, lsem.at[1])

    steps = []
    sums = {}
    for l in (0, 1):
        for c in range(MICRO):
            steps.append((partial(project, l, c), None))
        for c in range(MICRO):
            steps.append((partial(attend, l, c), (2 * l, c)))
            sums[2 * l, c] = (partial(attend_rows, l, c), FB, 2 * l + 1)
        for c in range(MICRO):
            steps.append((partial(feed, l, c), (2 * l + 1, c)))
            sums[2 * l + 1, c] = (partial(feed_rows, l, c), FB, 2 * l + 2)
    for l in (1, 0):
        a0, a1 = 6 - 2 * l, 7 - 2 * l
        for c in range(MICRO):
            steps.append((partial(feed_back, l, c), (a0, c)))
            sums[a0, c] = (partial(feed_back_rows, l, c), BB, 3 - 2 * l)
        for c in range(MICRO):
            steps.append((partial(attend_back, l, c), None))
        for c in range(MICRO):
            steps.append((partial(project_back, l, c), (a1, c)))
            sums[a1, c] = (partial(project_back_rows, l, c), BB, 4 - 2 * l)

    g1, g2, g3 = gather_one, gather_two, gather_wait
    d1, d2 = reduce_one, reduce_two
    before = {
        3: [(g3, 0, OUT)],
        6: [(g3, 0, UP), (g3, 0, DOWN)],
        9: [(g3, 1, QKV)],
        12: [(g3, 1, OUT)],
        15: [(g3, 1, UP), (g3, 1, DOWN)],
    }
    between = {
        3: [(g2, 0, DOWN), (g1, 1, QKV), (g1, 1, OUT)],
        5: [(g2, 1, QKV), (g2, 1, OUT), (g1, 1, UP)],
        8: [(g2, 1, UP), (g1, 1, DOWN)],
        11: [(g2, 1, DOWN)],
        18: [(down_grad, 1, 0)],
        19: [(down_grad, 1, 1), (d1, 1, DOWN)],
        21: [(up_grad, 1, 0)],
        22: [(up_grad, 1, 1), (d1, 1, UP)],
        23: [(d2, 1, DOWN)],
        24: [(out_grad, 1, 0)],
        25: [(out_grad, 1, 1), (d1, 1, OUT)],
        26: [(d2, 1, UP)],
        27: [(qkv_grad, 1, 0)],
        28: [(qkv_grad, 1, 1), (d1, 1, QKV)],
        29: [(down_grad, 0, 0), (d2, 1, OUT)],
        30: [(down_grad, 0, 1), (d1, 0, DOWN)],
        31: [(up_grad, 0, 0)],
        32: [(up_grad, 0, 1), (d1, 0, UP)],
        33: [(out_grad, 0, 0), (d2, 1, QKV)],
        34: [(out_grad, 0, 1), (d1, 0, OUT)],
        35: [(d2, 0, DOWN)],
        36: [(qkv_grad, 0, 0), (qkv_grad, 0, 1), (d1, 0, QKV)],
        37: [(d2, 0, UP)],
    }
    for n in range(len(steps) + 2):
        for fn, l, i in before.get(n, ()):
            fn(l, i)
        if n < len(steps):
            steps[n][0]()
        for fn, l, i in between.get(n, ()):
            fn(l, i)
        if n < len(steps) and steps[n][1] is not None:
            rs_mid(*steps[n][1])
        if 1 <= n <= len(steps) and steps[n - 1][1] is not None:
            sums[steps[n - 1][1]][0]()
        if n >= 2 and steps[n - 2][1] is not None:
            a, c = steps[n - 2][1]
            ag_mid(sums[a, c][1], sums[a, c][2], a, c)
            ag_end(a, c)
        if n == 19:
            cp_o.start()

    for i in range(11):
        GT[i, 0:8] = GV[0, :, 128 * i : 128 * i + 128]
        GT[i, 8:16] = GV[1, :, 128 * i : 128 * i + 128]

    @pl.loop(1, SHARDS)
    def _(k):
        j, dev = shard_dev(k)
        remote(GT.at[pl.ds(SHARD * j // 128, 2)], vr.at[k - 1], es.at[0], er.at[0], dev).start()
        remote(gb, br.at[k - 1], es.at[1], er.at[1], dev).start()

    cp_g.start()
    wait_bytes(vr, er.at[0])
    wait_bytes(vr, es.at[0])
    own = GT[pl.ds(SHARD * me // 128, 2)]
    for k in range(SHARDS - 1):
        own = own + vr[k]
    vr2[7] = own

    @pl.loop(1, 8)
    def _(k):
        remote(vr2.at[7], vr2.at[k - 1], es.at[2], er.at[2], (f, s, (t + k) % 8)).start()

    reduce_two(0, OUT)
    reduce_two(0, QKV)
    wait_bytes(br, er.at[1])
    wait_bytes(br, es.at[1])
    totals = gb[...]
    for k in range(SHARDS - 1):
        totals = totals + br[k]
    bout_ref[...] = totals
    for l, i in ((1, DOWN), (1, UP), (1, OUT), (1, QKV), (0, DOWN), (0, UP), (0, OUT)):
        reduce_three(l, i)
    wait_bytes(vr2.at[pl.ds(0, 7)], er.at[2])
    wait_bytes(vr2.at[pl.ds(0, 7)], es.at[2])
    own = vr2[7]
    for k in range(7):
        own = own + vr2[k]
    vout_ref[...] = own
    reduce_three(0, QKV)
    cp_o.wait()
    cp_g.wait()


def body(
    hidden_in, cotangent, lengths, qkv_weight, qv_bias, out_weight, out_bias,
    up_weight, up_bias, down_weight, down_bias, ln_gain, ln_bias,
):
    seq = lax.axis_index("seq")
    me = lax.axis_index("fsdp") * 2 + seq
    own_pos = seq * ROWS + jnp.arange(ROWS)
    far_pos = (1 - seq) * ROWS + jnp.arange(ROWS)
    keys = jnp.concatenate([own_pos, far_pos])
    live = (keys[None, :] < lengths[:, None]).astype(F32).reshape(MICRO, 1, 2 * ROWS)
    cot = jnp.where((own_pos[None, :] < lengths[:, None])[..., None], cotangent, jnp.zeros((), BF))
    first = jnp.concatenate(
        [qkv_weight[:, 0], qkv_weight[:, 1], qkv_weight[:, 2], jnp.swapaxes(out_weight, 1, 2)], axis=2
    )
    wown = jnp.stack([first, up_weight, jnp.swapaxes(down_weight, 1, 2)], axis=1)
    vectors = jnp.stack(
        [ln_gain[:, 0], ln_gain[:, 1], ln_bias[:, 0], ln_bias[:, 1], out_bias, down_bias], axis=1
    )
    vectors = jnp.pad(vectors, ((0, 0), (0, 2), (0, 0))).reshape(16, SHARD)
    offset = lax.rem(SHARD * me, 128)
    vectors = lax.dynamic_update_slice(jnp.zeros((16, 256), BF), vectors, (0, offset))
    zero = jnp.zeros((2, WIDTH), F32)
    qv = qv_bias.astype(F32)
    bqkv = jnp.concatenate([qv[:, 0], zero, qv[:, 1], zero[:, 0:32]], axis=1).reshape(2, 1, 512)
    bup = up_bias.astype(F32).reshape(2, 1, PART)

    vmem = pl.BlockSpec(memory_space=pltpu.VMEM)
    anys = pl.BlockSpec(memory_space=pl.ANY)
    dma = pltpu.SemaphoreType.DMA
    blocks = (MICRO, 4, 2, 16, D)
    scratch = [
        pltpu.VMEM((2, 3, 2, 4, 2, SHARD, PART), BF),
        pltpu.VMEM((2, 3, 2, 4, 2, SHARD, PART), BF),
        pltpu.VMEM((2, 3, 3, 4, SHARD, 384), BF),
        pltpu.VMEM((2, 3, 3, 2, 2, SHARD, 384), BF),
        pltpu.VMEM((2, 3, 3, SHARD, PART), BF),
        pltpu.VMEM((5,) + blocks, BF),
        pltpu.VMEM((5,) + blocks, BF),
        pltpu.VMEM((8, MICRO, 4, 16, D), BF),
        pltpu.VMEM((8, MICRO, 3, 16, D), BF),
        pltpu.VMEM(blocks, BF),
        pltpu.VMEM((MICRO, 4, 16, D), BF),
        pltpu.VMEM((2, MICRO, ROWS, 512), BF),
        pltpu.VMEM((2, MICRO, ROWS, 384), BF),
        pltpu.VMEM((2, MICRO, 2 * ROWS, 2 * ROWS), F32),
        pltpu.VMEM((2, MICRO, ROWS, 256), BF),
        pltpu.VMEM((2, MICRO, 16, D), F32),
        pltpu.VMEM((2, MICRO, 16, D), F32),
        pltpu.VMEM((2, MICRO, ROWS, PART), F32),
        pltpu.VMEM((2, MICRO, ROWS, PART), BF),
        pltpu.VMEM((MICRO, ROWS, PART), BF),
        pltpu.VMEM((MICRO, ROWS, 512), F32),
        pltpu.VMEM((MICRO, ROWS, 512), BF),
        pltpu.VMEM((MICRO, ROWS, 384), BF),
        pltpu.VMEM((2, MICRO, ROWS, 384), BF),
        pltpu.VMEM((MICRO, 16, D), F32),
        pltpu.VMEM((MICRO, 16, D), F32),
        pltpu.VMEM((SHARDS, 16, 256), BF),
        pltpu.VMEM((2, 8, 1408), F32),
        pltpu.VMEM((2, 8, 1408), F32),
        pltpu.VMEM((11, 16, 128), F32),
        pltpu.VMEM((SHARDS - 1, 2, 16, 128), F32),
        pltpu.VMEM((8, 2, 16, 128), F32),
        pltpu.VMEM((8, PART), F32),
        pltpu.VMEM((SHARDS - 1, 8, PART), F32),
        dma((2, 4, 2)), dma((2, 4, 2)), dma((2, 4, 2)), dma((2, 4, 2)),
        dma((2, 4, 2)), dma((2, 4, 2)), dma((2, 4, 2)), dma((2, 4, 2)),
        dma((MICRO,)), dma((8, MICRO)), dma((MICRO,)), dma((8, MICRO)),
        dma((MICRO,)), dma((8, MICRO)), dma((MICRO,)), dma((8, MICRO)),
        dma((2, MICRO)), dma((2, MICRO)), dma((MICRO,)), dma((2, MICRO)),
        dma((1,)), dma((1,)), dma((3,)), dma((3,)), dma((2,)),
    ]
    out, ingrad, dwo, vout, bout = pl.pallas_call(
        kernel,
        name="encoder",
        out_shape=(
            jax.ShapeDtypeStruct(blocks, BF),
            jax.ShapeDtypeStruct(blocks, BF),
            jax.ShapeDtypeStruct((2, 3, SHARD, PART), F32),
            jax.ShapeDtypeStruct((2, 16, 128), F32),
            jax.ShapeDtypeStruct((8, PART), F32),
        ),
        in_specs=[anys, anys, vmem, vmem, vmem, vmem, vmem],
        out_specs=(anys, anys, vmem, vmem, vmem),
        scratch_shapes=scratch,
        compiler_params=pltpu.CompilerParams(
            collective_id=0, has_side_effects=True, vmem_limit_bytes=63 * 1024 * 1024
        ),
    )(hidden_in.reshape(blocks), cot.reshape(blocks), wown, vectors, bqkv, bup, live)

    out_hidden = out.reshape(MICRO, ROWS, D).astype(F32)
    in_grad = ingrad.reshape(MICRO, ROWS, D).astype(F32)
    first = dwo[:, 0]
    qkv_grad = jnp.stack([first[:, :, 0:160], first[:, :, 160:320], first[:, :, 320:480]], axis=1)
    out_grad = jnp.swapaxes(first[:, :, 480:640], 1, 2)
    up_grad = dwo[:, 1]
    down_grad = jnp.swapaxes(dwo[:, 2], 1, 2)
    rows = jnp.swapaxes(vout, 0, 1).reshape(16, 256)
    rows = lax.dynamic_slice(rows, (0, offset), (16, SHARD)).reshape(2, 8, SHARD)
    gain_grad = rows[:, 0:2]
    shift_grad = rows[:, 2:4]
    qv_grad = jnp.stack([bout[0:2, 0:160], bout[0:2, 320:480]], axis=1)
    return (
        out_hidden, in_grad, qkv_grad, qv_grad, out_grad, rows[:, 4], up_grad,
        bout[2:4], down_grad, rows[:, 5], gain_grad, shift_grad,
    )


def solution(mesh):
    placed = (
        P("fsdp", "seq", None),
        P("fsdp", "seq", None),
        P("fsdp"),
        P(None, None, ("fsdp", "seq"), "tp"),
        P(None, None, "tp"),
        P(None, "tp", ("fsdp", "seq")),
        P(None, ("fsdp", "seq")),
        P(None, ("fsdp", "seq"), "tp"),
        P(None, "tp"),
        P(None, "tp", ("fsdp", "seq")),
        P(None, ("fsdp", "seq")),
        P(None, None, ("fsdp", "seq")),
        P(None, None, ("fsdp", "seq")),
    )
    return jax.shard_map(
        body,
        mesh=mesh,
        in_specs=placed,
        out_specs=(
            P("fsdp", "seq", None),
            P("fsdp", "seq", None),
            P(None, None, ("fsdp", "seq"), "tp"),
            P(None, None, "tp"),
            P(None, "tp", ("fsdp", "seq")),
            P(None, ("fsdp", "seq")),
            P(None, ("fsdp", "seq"), "tp"),
            P(None, "tp"),
            P(None, "tp", ("fsdp", "seq")),
            P(None, ("fsdp", "seq")),
            P(None, None, ("fsdp", "seq")),
            P(None, None, ("fsdp", "seq")),
        ),
        check_vma=False,
    )
```

```python
from functools import partial
import math

import jax
import jax.numpy as jnp
from jax import lax
from jax.experimental import pallas as pl
from jax.experimental.pallas import tpu as pltpu
from jax.sharding import PartitionSpec as P

HD = 80
EPSILON = 1e-05
MASKED = -1000000000.0
MESH = pl.DeviceIdType.MESH
BF = jnp.bfloat16
F32 = jnp.float32
SCALING = 1.0 / math.sqrt(HD)

D = 1280
MICRO = 3
ROWS = 128
PART = 640
SHARDS = 16
SHARD = 80

PIECES = (
    (0, (256, 512), (0, 256)),
    (0, (512, 640), None),
    (1, (384, 640), (0, 384)),
    (2, (384, 640), (0, 384)),
)
QKV, OUT, UP, DOWN = range(4)
LOADS = (
    (0, 0, (256, 512), (0, 256)),
    (0, 0, (512, 640), None),
    (0, 1, None, (0, 640)),
    (0, 2, (0, 256), None),
    (0, 2, None, (256, 640)),
    (1, 0, (384, 640), (0, 384)),
    (1, 1, (384, 640), (0, 384)),
    (1, 2, (384, 640), (0, 384)),
)
QKV0, OUT0, UP0, DOWN0X, DOWN0Z, PROJ1, UP1, DOWN1 = range(8)


def dot_nn(a, b):
    return lax.dot_general(a, b, (((1,), (0,)), ((), ())), preferred_element_type=F32)


def dot_nt(a, b):
    return lax.dot_general(a, b, (((1,), (1,)), ((), ())), preferred_element_type=F32)


def dot_tn(a, b):
    return lax.dot_general(a, b, (((0,), (0,)), ((), ())), preferred_element_type=F32)


def norm_parts(values):
    row_mean = jnp.mean(values, axis=-1, keepdims=True)
    centred = values - row_mean
    row_var = jnp.mean(centred * centred, axis=-1, keepdims=True)
    inv = lax.rsqrt(row_var + EPSILON)
    return centred * inv, inv


def norm_back(grad, gain, unit, inv):
    scaled = grad * gain
    return inv * (
        scaled
        - jnp.mean(scaled, axis=-1, keepdims=True)
        - unit * jnp.mean(scaled * unit, axis=-1, keepdims=True)
    )


def split_heads(x):
    first = lax.broadcasted_iota(jnp.int32, x.shape, 1) < HD
    return jnp.concatenate([jnp.where(first, x, 0.0), jnp.where(first, 0.0, x)], axis=0)


def kernel(
    hid_ref, cot_ref, len_ref, wqkv_ref, bqv_ref, wout_ref, bout_ref, wup_ref, bup_ref, wdown_ref, bdown_ref,
    gain_ref, shift_ref,
    out_ref, ingrad_ref, dwo_ref, vsum_ref, bsum_ref,
    W, dW, rb1, rb2, rc, FB, BB, dr, yr, part, sb,
    qkv, kvo, prob, att, xrow, midrow, slope, act,
    gpre, gkeep, gproj, gks, gkr, gyrow, gmidrow,
    VG, V, GV, GT, vr, vr2, gb, br, vrow, bqkv,
    g1s, g1r, g2s, g2r, g3s, g3r, q1s, q1r, q2s, q2r,
    s1, r1, s2, r2, s3, r3, s4, r4, ks, kr, gs_s, gs_r, vs, vrs, es, er, lsem,
):
    f, s, t = lax.axis_index("fsdp"), lax.axis_index("seq"), lax.axis_index("tp")
    me = f * 2 + s
    xh, z = f // 4, f % 4
    x = xh * 2 + s
    y, core = t // 2, t % 2
    other = 1 - core

    def shard_dev(k):
        j = (me + k) % SHARDS
        return j, (j // 2, j % 2, t)

    def x_dev(k):
        j = (x + k) % 4
        return j // 2, j % 2, ((j // 2) * 4 + z, j % 2, t)

    def z_dev(k):
        j = (z + k) % 4
        return j, (xh * 4 + j, s, t)

    def y_dev(k):
        j = (y + k) % 4
        return j, (f, s, j * 2 + core)

    core_dev = (f, s, y * 2 + other)
    seq_dev = (f, 1 - s, t)

    def remote(src, dst, ss, rs, dev):
        return pltpu.make_async_remote_copy(
            src_ref=src, dst_ref=dst, send_sem=ss, recv_sem=rs, device_id=dev, device_id_type=MESH
        )

    def wait_bytes(ref, sem):
        pltpu.make_async_copy(ref, ref, sem).wait()

    cp_h = pltpu.make_async_copy(hid_ref, FB.at[0], lsem.at[0])
    cp_c = pltpu.make_async_copy(cot_ref, BB.at[0], lsem.at[1])
    cp_h.start()
    cp_c.start()

    barrier = pltpu.get_barrier_semaphore()

    @pl.loop(1, SHARDS)
    def _(k):
        pl.semaphore_signal(barrier, inc=1, device_id=shard_dev(k)[1], device_id_type=MESH)

    @pl.loop(1, 8)
    def _(k):
        pl.semaphore_signal(barrier, inc=1, device_id=(f, s, (t + k) % 8), device_id_type=MESH)

    def pack(l, p):
        if p == 0:
            parts = [wqkv_ref[l, i].astype(F32) for i in range(3)] + [wout_ref[l].astype(F32).T]
            W[l, 0, xh, z, s] = jnp.concatenate(parts, axis=1).astype(BF)
        elif p == 1:
            W[l, 1, xh, z, s] = wup_ref[l]
        else:
            W[l, 2, xh, z, s] = wdown_ref[l].astype(F32).T.astype(BF)

    vrow[...] = jnp.zeros_like(vrow)
    for l in range(2):
        for r in range(2):
            vrow[8 * l + r : 8 * l + r + 1, 0:SHARD] = gain_ref[l, r : r + 1, :].astype(F32)
            vrow[8 * l + 2 + r : 8 * l + 3 + r, 0:SHARD] = shift_ref[l, r : r + 1, :].astype(F32)
        vrow[8 * l + 4 : 8 * l + 5, 0:SHARD] = bout_ref[l : l + 1, :].astype(F32)
        vrow[8 * l + 5 : 8 * l + 6, 0:SHARD] = bdown_ref[l : l + 1, :].astype(F32)
    VG[me] = pltpu.roll(vrow[...], (SHARD * me) % 128, 1).astype(BF)
    pack(0, 0)
    pl.semaphore_wait(barrier, 22)

    def load(n):
        l, p, one, two = LOADS[n]
        ways = ([(0, slice(*one))] if one else []) + ([(1, slice(*two))] if two else [])
        return l, p, ways

    def gather_one(n):
        l, p, ways = load(n)
        for way, cols in ways:
            own = W.at[l, p, xh, z, s, :, cols]
            for k in range(1, 4):
                dev = x_dev(k)[2] if way else z_dev(k)[1]
                remote(own, own, g1s.at[n, way], g1r.at[n, way], dev).start()

    def gather_mid(n):
        l, p, ways = load(n)
        for way, cols in ways:
            three = W.at[l, p, 0, pl.ds(0, 3), 0, :, cols]
            wait_bytes(three, g1r.at[n, way])
            wait_bytes(three, g1s.at[n, way])

    def gather_two(n):
        l, p, ways = load(n)
        gather_mid(n)
        for way, cols in ways:
            four = W.at[l, p, :, z, :, :, cols] if way else W.at[l, p, xh, :, s, :, cols]
            for k in range(1, 4):
                dev = z_dev(k)[1] if way else x_dev(k)[2]
                remote(four, four, g2s.at[n, way], g2r.at[n, way], dev).start()

    def gather_wait(n):
        l, p, ways = load(n)
        for way, cols in ways:
            twelve = W.at[l, p, :, pl.ds(0, 3), :, :, cols]
            wait_bytes(twelve, g2r.at[n, way])
            wait_bytes(twelve, g2s.at[n, way])

    def ring_dev(way, k):
        return z_dev(k)[1] if way else x_dev(k)[2]

    def ring_two(n):
        l, p, ways = load(n)
        gather_mid(n)
        for way, cols in ways:
            four = W.at[l, p, :, z, :, :, cols] if way else W.at[l, p, xh, :, s, :, cols]
            for k in (1, 3):
                remote(four, four, g2s.at[n, way], g2r.at[n, way], ring_dev(way, k)).start()

    def ring_mid(n):
        l, p, ways = load(n)
        for way, cols in ways:
            eight = W.at[l, p, 0, :, :, :, cols]
            wait_bytes(eight, g2r.at[n, way])
            wait_bytes(eight, g2s.at[n, way])

    def ring_three(n):
        l, p, ways = load(n)
        ring_mid(n)
        for way, cols in ways:
            if way:
                left = W.at[l, p, 0, (z + 3) % 4, :, :, cols]
                right = W.at[l, p, 1, (z + 1) % 4, :, :, cols]
            else:
                il, ir = (x + 3) % 4, (x + 1) % 4
                left = W.at[l, p, il // 2, pl.ds(0, 2), il % 2, :, cols]
                right = W.at[l, p, ir // 2, pl.ds(2, 2), ir % 2, :, cols]
            remote(left, left, g3s.at[n, way], g3r.at[n, way], ring_dev(way, 1)).start()
            remote(right, right, g3s.at[n, way], g3r.at[n, way], ring_dev(way, 3)).start()

    def ring_wait(n):
        l, p, ways = load(n)
        for way, cols in ways:
            four = W.at[l, p, 0, pl.ds(0, 2), :, :, cols]
            wait_bytes(four, g3r.at[n, way])
            wait_bytes(four, g3s.at[n, way])

    def piece(l, i):
        part_idx, one, two = PIECES[i]
        both = [(0, slice(*one))] + ([(1, slice(*two))] if two else [])
        return part_idx, both

    def reduce_one(l, i):
        p, ways = piece(l, i)
        for way, cols in ways:
            for k in range(1, 4):
                if way:
                    j, dev = z_dev(k)
                    four = dW.at[l, p, :, j, :, :, cols]
                    buf = rb2.at[l, p, k - 1, :, :, :, 0 : cols.stop - cols.start]
                else:
                    jh, jl, dev = x_dev(k)
                    four = dW.at[l, p, jh, :, jl, :, cols]
                    buf = rb1.at[l, p, k - 1, :, :, cols.start - 256 : cols.stop - 256]
                remote(four, buf, q1s.at[l, i, way], q1r.at[l, i, way], dev).start()

    def reduce_mid(l, i):
        p, ways = piece(l, i)
        for way, cols in ways:
            twelve = dW.at[l, p, :, pl.ds(0, 3), :, :, cols]
            wait_bytes(twelve, q1r.at[l, i, way])
            wait_bytes(twelve, q1s.at[l, i, way])

    def reduce_two(l, i):
        p, ways = piece(l, i)
        reduce_mid(l, i)

        @pl.loop(0, 4)
        def _(n):
            nh, nl = n // 2, n % 2
            for way, cols in ways:
                if way:
                    total = dW[l, p, nh, z, nl, :, cols].astype(F32)
                    for k in range(3):
                        total = total + rb2[l, p, k, nh, nl, :, 0 : cols.stop - cols.start].astype(F32)
                    dW[l, p, nh, z, nl, :, cols] = total.astype(BF)
                else:
                    total = dW[l, p, xh, n, s, :, cols].astype(F32)
                    for k in range(3):
                        total = total + rb1[l, p, k, n, :, cols.start - 256 : cols.stop - 256].astype(F32)
                    dW[l, p, xh, n, s, :, cols] = total.astype(BF)

        for way, cols in ways:
            for k in range(1, 4):
                if way:
                    jh, jl, dev = x_dev(k)
                    one = dW.at[l, p, jh, z, jl, :, cols]
                else:
                    j, dev = z_dev(k)
                    one = dW.at[l, p, xh, j, s, :, cols]
                remote(one, rc.at[l, p, k - 1, :, cols], q2s.at[l, i, way], q2r.at[l, i, way], dev).start()

    def reduce_last(l, i):
        p, ways = piece(l, i)
        for way, cols in ways:
            three = dW.at[l, p, 0, pl.ds(0, 3), 0, :, cols]
            wait_bytes(three, q2r.at[l, i, way])
            wait_bytes(three, q2s.at[l, i, way])

    def reduce_three(l, i):
        p, ways = piece(l, i)
        reduce_last(l, i)
        for way, cols in ways:
            total = dW[l, p, xh, z, s, :, cols].astype(F32)
            for k in range(3):
                total = total + rc[l, p, k, :, cols].astype(F32)
            dwo_ref[l, p, :, cols] = total

    def vec(l, r):
        return V[l, r : r + 1, 0:D]

    def rs_start(a, c, value):
        part[c] = value.astype(BF).reshape(4, 2, 16, D)
        remote(part.at[c, :, other], dr.at[a, c], s1.at[c], r1.at[a, c], core_dev).start()

    def rs_mid(a, c):
        wait_bytes(dr.at[a, c], r1.at[a, c])
        wait_bytes(dr.at[a, c], s1.at[c])
        sb[c] = (part[c, :, core].astype(F32) + dr[a, c].astype(F32)).astype(BF)
        for k in range(1, 4):
            j, dev = y_dev(k)
            remote(sb.at[c, j], yr.at[a, c, k - 1], s2.at[c], r2.at[a, c], dev).start()

    def rs_end(a, c):
        wait_bytes(yr.at[a, c], r2.at[a, c])
        wait_bytes(yr.at[a, c], s2.at[c])
        total = sb[c, y].astype(F32)
        for k in range(3):
            total = total + yr[a, c, k].astype(F32)
        return total

    def ag_start(buf, i, a, c, value):
        buf[i, c, y, core] = value.astype(BF)
        for k in range(1, 4):
            _, dev = y_dev(k)
            remote(buf.at[i, c, y, core], buf.at[i, c, y, core], s3.at[c], r3.at[a, c], dev).start()

    def ag_mid(buf, i, a, c):
        wait_bytes(yr.at[a, c], r3.at[a, c])
        wait_bytes(yr.at[a, c], s3.at[c])
        remote(buf.at[i, c, :, core], buf.at[i, c, :, core], s4.at[c], r4.at[a, c], core_dev).start()

    def ag_end(a, c):
        wait_bytes(dr.at[a, c], r4.at[a, c])
        wait_bytes(dr.at[a, c], s4.at[c])

    def heads_of(l, c):
        own = qkv[l, c].astype(F32)
        far = kvo[l, c].astype(F32)
        q = own[:, 0:160]
        k = jnp.concatenate([own[:, 160:320], far[:, 32:192]], axis=0)
        v = jnp.concatenate([own[:, 320:480], far[:, 192:352]], axis=0)
        return split_heads(q).astype(BF), k, v

    def project(l, c):
        normed = FB[2 * l, c].reshape(ROWS, D)
        proj = dot_nn(normed, W[l, 0, :, :, :, :, 0:512].reshape(D, 512)) + bqkv[l]
        qkv[l, c] = proj.astype(BF)
        remote(qkv.at[l, c, :, 128:512], kvo.at[l, c], ks.at[l, c], kr.at[l, c], seq_dev).start()

    def attend(l, c):
        wait_bytes(kvo.at[l, c], kr.at[l, c])
        wait_bytes(kvo.at[l, c], ks.at[l, c])
        q2, k, v = heads_of(l, c)
        scores = dot_nt(q2, k.astype(BF)) * SCALING
        slot = lax.broadcasted_iota(jnp.int32, (1, 2 * ROWS), 1)
        slot = jnp.where(slot < ROWS, slot + s * ROWS, slot - s * ROWS)
        scores = jnp.where(slot < len_ref[c], scores, MASKED)
        top = jnp.max(scores, axis=-1, keepdims=True)
        powers = jnp.exp(scores - top)
        probs = powers / jnp.sum(powers, axis=-1, keepdims=True)
        prob[l, c] = probs
        low = probs.astype(BF)
        attended = dot_nn(
            jnp.concatenate([low[0:ROWS], low[ROWS:]], axis=1), split_heads(v).astype(BF)
        )
        wide = jnp.concatenate([jnp.zeros((ROWS, 96), F32), attended], axis=1).astype(BF)
        att[l, c] = wide
        rs_start(2 * l, c, dot_nt(wide, W[l, 0, :, :, :, :, 384:640].reshape(D, 256)))

    def attend_rows(l, c):
        a = 2 * l
        middle = xrow[l, c] + rs_end(a, c) + vec(l, 4)
        midrow[l, c] = middle
        unit, _ = norm_parts(middle)
        ag_start(FB, 2 * l + 1, a, c, unit * vec(l, 1) + vec(l, 3))

    def feed(l, c):
        normed = FB[2 * l + 1, c].reshape(ROWS, D)
        pre = dot_nn(normed, W[l, 1].reshape(D, PART)) + bup_ref[l : l + 1, :].astype(F32)
        cdf = 0.5 * (1.0 + lax.erf(pre * math.sqrt(0.5)))
        activated = (pre * cdf).astype(BF)
        act[l, c] = activated
        slope[l, c] = cdf + pre * jnp.exp(-0.5 * pre * pre) * (1.0 / math.sqrt(2.0 * math.pi))
        if c == 0 and l == 0:
            ring_wait(DOWN0X)
            ring_wait(DOWN0Z)
        elif c == 0:
            ring_wait(DOWN1)
        rs_start(2 * l + 1, c, dot_nt(activated, W[l, 2].reshape(D, PART)))

    def feed_rows(l, c):
        a = 2 * l + 1
        hidden = midrow[l, c] + rs_end(a, c) + vec(l, 5)
        if l == 0:
            xrow[1, c] = hidden
            unit, _ = norm_parts(hidden)
            hidden = unit * vec(1, 0) + vec(1, 2)
        ag_start(FB, 2 * l + 2, a, c, hidden)

    def feed_back(l, c):
        grad_act = dot_nn(BB[2 - 2 * l, c].reshape(ROWS, D), W[l, 2].reshape(D, PART))
        grad_pre = (grad_act * slope[l, c]).astype(BF)
        gpre[c] = grad_pre
        gb[2 + l : 3 + l, :] += jnp.sum(grad_pre.astype(F32), axis=0, keepdims=True)
        rs_start(6 - 2 * l, c, dot_nt(grad_pre, W[l, 1].reshape(D, PART)))

    def feed_back_rows(l, c):
        a = 6 - 2 * l
        grad_norm = rs_end(a, c)
        unit, inv = norm_parts(midrow[l, c])
        gy = gyrow[c]
        grad_mid = gy + norm_back(grad_norm, vec(l, 1), unit, inv)
        gmidrow[c] = grad_mid
        ag_start(BB, 3 - 2 * l, a, c, grad_mid)
        GV[l, 1:2, 0:D] += jnp.sum(grad_norm * unit, axis=0, keepdims=True)
        GV[l, 3:4, 0:D] += jnp.sum(grad_norm, axis=0, keepdims=True)
        GV[l, 4:5, 0:D] += jnp.sum(grad_mid, axis=0, keepdims=True)
        GV[l, 5:6, 0:D] += jnp.sum(gy, axis=0, keepdims=True)

    def attend_back(l, c):
        wide = dot_nn(BB[3 - 2 * l, c].reshape(ROWS, D), W[l, 0, :, :, :, :, 384:640].reshape(D, 256))
        ga2 = split_heads(wide[:, 96:256]).astype(BF)
        q2, k, v = heads_of(l, c)
        probs = prob[l, c]
        grad_probs = dot_nt(ga2, v.astype(BF))
        grad_scores = probs * (grad_probs - jnp.sum(probs * grad_probs, axis=-1, keepdims=True))
        low = grad_scores.astype(BF)
        grad_v = dot_tn(probs.astype(BF), ga2)
        grad_k = dot_tn(low, q2) * SCALING
        pad = jnp.zeros((ROWS, 64), F32)
        gks[c] = jnp.concatenate([grad_k[ROWS:], grad_v[ROWS:], pad], axis=1).astype(BF)
        remote(gks.at[c], gkr.at[l, c], gs_s.at[c], gs_r.at[l, c], seq_dev).start()
        grad_q = (
            dot_nn(jnp.concatenate([low[0:ROWS], low[ROWS:]], axis=1), split_heads(k).astype(BF))
            * SCALING
        )
        gkeep[c, :, 0:160] = grad_q
        gkeep[c, :, 160:320] = grad_k[0:ROWS]
        gkeep[c, :, 320:480] = grad_v[0:ROWS]
        gkeep[c, :, 480:512] = jnp.zeros((ROWS, 32), F32)

    def project_back(l, c):
        wait_bytes(gkr.at[l, c], gs_r.at[l, c])
        wait_bytes(gkr.at[l, c], gs_s.at[c])
        far = gkr[l, c].astype(F32)
        gkeep[c, :, 160:480] += far[:, 0:320]
        grads = gkeep[c].astype(BF)
        gproj[c] = grads
        gb[l : l + 1, 0:512] += jnp.sum(grads.astype(F32), axis=0, keepdims=True)
        rs_start(7 - 2 * l, c, dot_nt(grads, W[l, 0, :, :, :, :, 0:512].reshape(D, 512)))

    def project_back_rows(l, c):
        a = 7 - 2 * l
        grad_norm = rs_end(a, c)
        unit, inv = norm_parts(xrow[l, c])
        gy = gmidrow[c] + norm_back(grad_norm, vec(l, 0), unit, inv)
        gyrow[c] = gy
        ag_start(BB, 4 - 2 * l, a, c, gy)
        GV[l, 0:1, 0:D] += jnp.sum(grad_norm * unit, axis=0, keepdims=True)
        GV[l, 2:3, 0:D] += jnp.sum(grad_norm, axis=0, keepdims=True)

    def left_of(buf, i, m):
        return buf[i, :, :, :, :, 640 * m : 640 * m + 640].reshape(MICRO * ROWS, 640)

    def down_grad(l, m):
        right = act[l].reshape(MICRO * ROWS, PART)
        dW[l, 2, m] = dot_tn(left_of(BB, 2 - 2 * l, m), right).astype(BF).reshape(4, 2, SHARD, PART)

    def up_grad(l, m):
        right = gpre[...].reshape(MICRO * ROWS, PART)
        dW[l, 1, m] = dot_tn(left_of(FB, 2 * l + 1, m), right).astype(BF).reshape(4, 2, SHARD, PART)

    def out_grad(l, m):
        grad = dot_tn(left_of(BB, 3 - 2 * l, m), att[l].reshape(MICRO * ROWS, 256))
        dW[l, 0, m, :, :, :, 384:640] = grad.astype(BF).reshape(4, 2, SHARD, 256)

    def qkv_grad(l, m):
        grad = dot_tn(left_of(FB, 2 * l, m), gproj[...].reshape(MICRO * ROWS, 512))
        dW[l, 0, m, :, :, :, 0:384] = grad[:, 0:384].astype(BF).reshape(4, 2, SHARD, 384)
        rest = dW[l, 0, m, :, :, :, 384:512].astype(F32).reshape(640, 128) + grad[:, 384:512]
        dW[l, 0, m, :, :, :, 384:512] = rest.astype(BF).reshape(4, 2, SHARD, 128)

    @pl.loop(1, SHARDS)
    def _(k):
        remote(VG.at[me], VG.at[me], vs.at[0], vrs.at[0], shard_dev(k)[1]).start()

    gather_one(QKV0)
    gather_one(OUT0)
    pack(0, 1)
    pack(0, 2)
    V[...] = jnp.zeros_like(V)
    GV[...] = jnp.zeros_like(GV)
    gb[...] = jnp.zeros_like(gb)
    bqkv[...] = jnp.zeros_like(bqkv)
    for l in range(2):
        bqkv[l, :, 0:160] = bqv_ref[l, 0:1, :].astype(F32)
        bqkv[l, :, 320:480] = bqv_ref[l, 1:2, :].astype(F32)
    gather_two(QKV0)
    wait_bytes(VG.at[pl.ds(0, SHARDS - 1)], vrs.at[0])
    wait_bytes(VG.at[pl.ds(0, SHARDS - 1)], vs.at[0])
    for i in range(SHARDS):
        low = SHARD * i // 128 * 128
        held = VG[i].astype(F32)
        V[0, :, low : low + 256] += held[0:8]
        V[1, :, low : low + 256] += held[8:16]
    cp_h.wait()
    cp_c.wait()
    for c in range(MICRO):
        whole = FB[0, c].reshape(ROWS, D).astype(F32)
        unit, _ = norm_parts(whole)
        xrow[0, c] = FB[0, c, y, core].astype(F32)
        FB[0, c] = (unit * vec(0, 0) + vec(0, 2)).astype(BF).reshape(4, 2, 16, D)
        if c == 0:
            gather_one(UP0)
            gather_one(DOWN0X)
    gather_two(OUT0)
    gather_wait(QKV0)

    def mask_grads():
        row = lax.broadcasted_iota(jnp.int32, (ROWS, 1), 0) + s * ROWS
        for c in range(MICRO):
            masked = jnp.where(row < len_ref[c], BB[0, c].reshape(ROWS, D).astype(F32), 0.0)
            BB[0, c] = masked.astype(BF).reshape(4, 2, 16, D)
            gyrow[c] = BB[0, c, y, core].astype(F32)

    def bias_sums():
        @pl.loop(1, SHARDS)
        def _(k):
            remote(gb, br.at[k - 1], es.at[1], er.at[1], shard_dev(k)[1]).start()

    cp_o = pltpu.make_async_copy(FB.at[4], out_ref, lsem.at[0])
    cp_g = pltpu.make_async_copy(BB.at[4], ingrad_ref, lsem.at[1])

    steps = []
    sums = {}
    for l in (0, 1):
        for c in range(MICRO):
            steps.append((partial(project, l, c), None))
        for c in range(MICRO):
            steps.append((partial(attend, l, c), (2 * l, c)))
            sums[2 * l, c] = (partial(attend_rows, l, c), FB, 2 * l + 1)
        for c in range(MICRO):
            steps.append((partial(feed, l, c), (2 * l + 1, c)))
            sums[2 * l + 1, c] = (partial(feed_rows, l, c), FB, 2 * l + 2)
    for l in (1, 0):
        a0, a1 = 6 - 2 * l, 7 - 2 * l
        for c in range(MICRO):
            steps.append((partial(feed_back, l, c), (a0, c)))
            sums[a0, c] = (partial(feed_back_rows, l, c), BB, 3 - 2 * l)
        for c in range(MICRO):
            steps.append((partial(attend_back, l, c), None))
        for c in range(MICRO):
            steps.append((partial(project_back, l, c), (a1, c)))
            sums[a1, c] = (partial(project_back_rows, l, c), BB, 4 - 2 * l)

    g1, g2, g3, g4 = gather_one, ring_two, ring_three, ring_wait
    d1, d2 = reduce_one, reduce_two
    before = {
        0: [(g2, UP0), (g1, DOWN0Z)],
        2: [(g2, DOWN0X)],
        3: [(gather_wait, OUT0), (g2, DOWN0Z)],
        4: [(g3, UP0), (g1, PROJ1)],
        5: [(g3, DOWN0X), (g3, DOWN0Z), (g2, PROJ1)],
        6: [(g4, UP0), (g1, UP1)],
        7: [(g3, PROJ1), (g2, UP1), (g1, DOWN1)],
        9: [(g4, PROJ1), (g3, UP1), (g2, DOWN1)],
        12: [(g3, DOWN1)],
        15: [(g4, UP1)],
    }
    between = {
        3: [(pack, 1, 0)],
        4: [(pack, 1, 1)],
        5: [(pack, 1, 2)],
        6: [(mask_grads,)],
        18: [(down_grad, 1, 0), (down_grad, 1, 1), (d1, 1, DOWN)],
        21: [(up_grad, 1, 0), (up_grad, 1, 1), (d1, 1, UP)],
        23: [(out_grad, 1, 0), (out_grad, 1, 1), (d1, 1, OUT)],
        24: [(d2, 1, DOWN)],
        25: [(d2, 1, UP)],
        26: [(qkv_grad, 1, 0), (qkv_grad, 1, 1), (d1, 1, QKV)],
        27: [(d2, 1, OUT)],
        29: [(down_grad, 0, 0), (down_grad, 0, 1), (d1, 0, DOWN)],
        30: [(up_grad, 0, 0), (up_grad, 0, 1), (d1, 0, UP)],
        31: [(d2, 1, QKV)],
        32: [(out_grad, 0, 0), (out_grad, 0, 1), (d1, 0, OUT)],
        33: [(d2, 0, DOWN)],
        34: [(d2, 0, UP)],
        35: [(qkv_grad, 0, 0), (qkv_grad, 0, 1), (d1, 0, QKV), (bias_sums,)],
        36: [(d2, 0, OUT)],
    }
    for n in range(len(steps) + 2):
        for fn, *where in before.get(n, ()):
            fn(*where)
        if n < len(steps):
            steps[n][0]()
        for fn, *where in between.get(n, ()):
            fn(*where)
        if n < len(steps) and steps[n][1] is not None:
            rs_mid(*steps[n][1])
        if 1 <= n <= len(steps) and steps[n - 1][1] is not None:
            sums[steps[n - 1][1]][0]()
        if n >= 2 and steps[n - 2][1] is not None:
            a, c = steps[n - 2][1]
            ag_mid(sums[a, c][1], sums[a, c][2], a, c)
            ag_end(a, c)
        if n == 19:
            cp_o.start()

    for i in range(11):
        GT[i, 0:8] = GV[0, :, 128 * i : 128 * i + 128]
        GT[i, 8:16] = GV[1, :, 128 * i : 128 * i + 128]

    @pl.loop(1, SHARDS)
    def _(k):
        j, dev = shard_dev(k)
        remote(GT.at[pl.ds(SHARD * j // 128, 2)], vr.at[k - 1], es.at[0], er.at[0], dev).start()

    cp_g.start()
    wait_bytes(vr, er.at[0])
    wait_bytes(vr, es.at[0])
    own = GT[pl.ds(SHARD * me // 128, 2)]
    for k in range(SHARDS - 1):
        own = own + vr[k]
    vr2[7] = own

    @pl.loop(1, 8)
    def _(k):
        remote(vr2.at[7], vr2.at[k - 1], es.at[2], er.at[2], (f, s, (t + k) % 8)).start()

    reduce_two(0, QKV)
    wait_bytes(br, er.at[1])
    wait_bytes(br, es.at[1])
    totals = gb[...]
    for k in range(SHARDS - 1):
        totals = totals + br[k]
    bsum_ref[...] = totals
    for l, i in ((1, DOWN), (1, UP), (1, OUT), (1, QKV), (0, DOWN), (0, UP), (0, OUT)):
        reduce_three(l, i)
    wait_bytes(vr2.at[pl.ds(0, 7)], er.at[2])
    wait_bytes(vr2.at[pl.ds(0, 7)], es.at[2])
    own = vr2[7]
    for k in range(7):
        own = own + vr2[k]
    vsum_ref[...] = own
    reduce_three(0, QKV)
    cp_o.wait()
    cp_g.wait()


def finish(
    out_ref, ingrad_ref, dwo_ref, vsum_ref, bsum_ref,
    hidden_ref, grad_ref, gqkv_ref, gqv_ref, gout_ref, gbout_ref, gup_ref, gbup_ref, gdown_ref, gbdown_ref,
    ggain_ref, gshift_ref,
):
    me = lax.axis_index("fsdp") * 2 + lax.axis_index("seq")
    hidden_ref[...] = out_ref[...].astype(F32)
    grad_ref[...] = ingrad_ref[...].astype(F32)
    rows = jnp.concatenate([vsum_ref[0], vsum_ref[1]], axis=1)
    rows = pltpu.roll(rows, (256 - (SHARD * me) % 128) % 256, 1)
    for l in range(2):
        proj = dwo_ref[l, 0]
        for i in range(3):
            gqkv_ref[l, i] = proj[:, 160 * i : 160 * i + 160]
        gout_ref[l] = proj[:, 480:640].T
        gup_ref[l] = dwo_ref[l, 1]
        gdown_ref[l] = dwo_ref[l, 2].T
        gqv_ref[l, 0:1, :] = bsum_ref[l : l + 1, 0:160]
        gqv_ref[l, 1:2, :] = bsum_ref[l : l + 1, 320:480]
        gbup_ref[l : l + 1, :] = bsum_ref[2 + l : 3 + l, :]
        ggain_ref[l] = rows[8 * l : 8 * l + 2, 0:SHARD]
        gshift_ref[l] = rows[8 * l + 2 : 8 * l + 4, 0:SHARD]
        gbout_ref[l : l + 1, :] = rows[8 * l + 4 : 8 * l + 5, 0:SHARD]
        gbdown_ref[l : l + 1, :] = rows[8 * l + 5 : 8 * l + 6, 0:SHARD]


def body(
    hidden_in, cotangent, lengths, qkv_weight, qv_bias, out_weight, out_bias,
    up_weight, up_bias, down_weight, down_bias, ln_gain, ln_bias,
):
    vmem = pl.BlockSpec(memory_space=pltpu.VMEM)
    anys = pl.BlockSpec(memory_space=pl.ANY)
    smem = pl.BlockSpec(memory_space=pltpu.SMEM)
    dma = pltpu.SemaphoreType.DMA
    blocks = (MICRO, 4, 2, 16, D)
    scratch = [
        pltpu.VMEM((2, 3, 2, 4, 2, SHARD, PART), BF),
        pltpu.VMEM((2, 3, 2, 4, 2, SHARD, PART), BF),
        pltpu.VMEM((2, 3, 3, 4, SHARD, 384), BF),
        pltpu.VMEM((2, 3, 3, 2, 2, SHARD, 384), BF),
        pltpu.VMEM((2, 3, 3, SHARD, PART), BF),
        pltpu.VMEM((5,) + blocks, BF),
        pltpu.VMEM((5,) + blocks, BF),
        pltpu.VMEM((8, MICRO, 4, 16, D), BF),
        pltpu.VMEM((8, MICRO, 3, 16, D), BF),
        pltpu.VMEM(blocks, BF),
        pltpu.VMEM((MICRO, 4, 16, D), BF),
        pltpu.VMEM((2, MICRO, ROWS, 512), BF),
        pltpu.VMEM((2, MICRO, ROWS, 384), BF),
        pltpu.VMEM((2, MICRO, 2 * ROWS, 2 * ROWS), F32),
        pltpu.VMEM((2, MICRO, ROWS, 256), BF),
        pltpu.VMEM((2, MICRO, 16, D), F32),
        pltpu.VMEM((2, MICRO, 16, D), F32),
        pltpu.VMEM((2, MICRO, ROWS, PART), F32),
        pltpu.VMEM((2, MICRO, ROWS, PART), BF),
        pltpu.VMEM((MICRO, ROWS, PART), BF),
        pltpu.VMEM((MICRO, ROWS, 512), F32),
        pltpu.VMEM((MICRO, ROWS, 512), BF),
        pltpu.VMEM((MICRO, ROWS, 384), BF),
        pltpu.VMEM((2, MICRO, ROWS, 384), BF),
        pltpu.VMEM((MICRO, 16, D), F32),
        pltpu.VMEM((MICRO, 16, D), F32),
        pltpu.VMEM((SHARDS, 16, 256), BF),
        pltpu.VMEM((2, 8, 1408), F32),
        pltpu.VMEM((2, 8, 1408), F32),
        pltpu.VMEM((11, 16, 128), F32),
        pltpu.VMEM((SHARDS - 1, 2, 16, 128), F32),
        pltpu.VMEM((8, 2, 16, 128), F32),
        pltpu.VMEM((8, PART), F32),
        pltpu.VMEM((SHARDS - 1, 8, PART), F32),
        pltpu.VMEM((16, 256), F32),
        pltpu.VMEM((2, 1, 512), F32),
        dma((8, 2)), dma((8, 2)), dma((8, 2)), dma((8, 2)), dma((8, 2)), dma((8, 2)),
        dma((2, 4, 2)), dma((2, 4, 2)), dma((2, 4, 2)), dma((2, 4, 2)),
        dma((MICRO,)), dma((8, MICRO)), dma((MICRO,)), dma((8, MICRO)),
        dma((MICRO,)), dma((8, MICRO)), dma((MICRO,)), dma((8, MICRO)),
        dma((2, MICRO)), dma((2, MICRO)), dma((MICRO,)), dma((2, MICRO)),
        dma((1,)), dma((1,)), dma((3,)), dma((3,)), dma((2,)),
    ]
    out, ingrad, dwo, vsum, bsum = pl.pallas_call(
        kernel,
        name="encoder",
        out_shape=(
            jax.ShapeDtypeStruct(blocks, BF),
            jax.ShapeDtypeStruct(blocks, BF),
            jax.ShapeDtypeStruct((2, 3, SHARD, PART), F32),
            jax.ShapeDtypeStruct((2, 16, 128), F32),
            jax.ShapeDtypeStruct((8, PART), F32),
        ),
        in_specs=[anys, anys, smem] + [vmem] * 10,
        out_specs=(anys, anys, vmem, vmem, vmem),
        scratch_shapes=scratch,
        compiler_params=pltpu.CompilerParams(
            collective_id=0, has_side_effects=True, vmem_limit_bytes=63 * 1024 * 1024
        ),
    )(
        hidden_in.reshape(blocks), cotangent.reshape(blocks), lengths, qkv_weight, qv_bias, out_weight,
        out_bias, up_weight, up_bias, down_weight, down_bias, ln_gain, ln_bias,
    )
    rows = (MICRO, ROWS, D)
    shapes = (
        rows, rows, (2, 3, SHARD, 160), (2, 2, 160), (2, 160, SHARD), (2, SHARD), (2, SHARD, PART),
        (2, PART), (2, PART, SHARD), (2, SHARD), (2, 2, SHARD), (2, 2, SHARD),
    )
    return pl.pallas_call(
        finish,
        name="finish",
        out_shape=tuple(jax.ShapeDtypeStruct(shape, F32) for shape in shapes),
        in_specs=[vmem] * 5,
        out_specs=(vmem,) * 12,
        compiler_params=pltpu.CompilerParams(vmem_limit_bytes=32 * 1024 * 1024),
    )(out.reshape(rows), ingrad.reshape(rows), dwo, vsum, bsum)


def solution(mesh):
    placed = (
        P("fsdp", "seq", None),
        P("fsdp", "seq", None),
        P("fsdp"),
        P(None, None, ("fsdp", "seq"), "tp"),
        P(None, None, "tp"),
        P(None, "tp", ("fsdp", "seq")),
        P(None, ("fsdp", "seq")),
        P(None, ("fsdp", "seq"), "tp"),
        P(None, "tp"),
        P(None, "tp", ("fsdp", "seq")),
        P(None, ("fsdp", "seq")),
        P(None, None, ("fsdp", "seq")),
        P(None, None, ("fsdp", "seq")),
    )
    return jax.shard_map(
        body,
        mesh=mesh,
        in_specs=placed,
        out_specs=(
            P("fsdp", "seq", None),
            P("fsdp", "seq", None),
            P(None, None, ("fsdp", "seq"), "tp"),
            P(None, None, "tp"),
            P(None, "tp", ("fsdp", "seq")),
            P(None, ("fsdp", "seq")),
            P(None, ("fsdp", "seq"), "tp"),
            P(None, "tp"),
            P(None, "tp", ("fsdp", "seq")),
            P(None, ("fsdp", "seq")),
            P(None, None, ("fsdp", "seq")),
            P(None, None, ("fsdp", "seq")),
        ),
        check_vma=False,
    )
```

```python
from functools import partial
import math

import jax
import jax.numpy as jnp
from jax import lax
from jax.experimental import pallas as pl
from jax.experimental.pallas import tpu as pltpu
from jax.sharding import PartitionSpec as P

HD = 80
EPSILON = 1e-05
MASKED = -1000000000.0
MESH = pl.DeviceIdType.MESH
BF = jnp.bfloat16
F32 = jnp.float32
SCALING = 1.0 / math.sqrt(HD)

D = 1280
MICRO = 3
ROWS = 128
PART = 640
SHARDS = 16
SHARD = 80

PIECES = (
    (0, (256, 512), (0, 256)),
    (0, (512, 640), None),
    (1, (384, 640), (0, 384)),
    (2, (384, 640), (0, 384)),
)
QKV, OUT, UP, DOWN = range(4)
LOADS = (
    (0, 0, (256, 512), (0, 256)),
    (0, 0, (512, 640), None),
    (0, 1, None, (0, 640)),
    (0, 2, (0, 256), None),
    (0, 2, None, (256, 640)),
    (1, 0, (384, 640), (0, 384)),
    (1, 1, (384, 640), (0, 384)),
    (1, 2, (384, 640), (0, 384)),
)
QKV0, OUT0, UP0, DOWN0X, DOWN0Z, PROJ1, UP1, DOWN1 = range(8)


def dot_nn(a, b):
    return lax.dot_general(a, b, (((1,), (0,)), ((), ())), preferred_element_type=F32)


def dot_nt(a, b):
    return lax.dot_general(a, b, (((1,), (1,)), ((), ())), preferred_element_type=F32)


def dot_tn(a, b):
    return lax.dot_general(a, b, (((0,), (0,)), ((), ())), preferred_element_type=F32)


def norm_parts(values):
    row_mean = jnp.mean(values, axis=-1, keepdims=True)
    centred = values - row_mean
    row_var = jnp.mean(centred * centred, axis=-1, keepdims=True)
    inv = lax.rsqrt(row_var + EPSILON)
    return centred * inv, inv


def norm_back(grad, gain, unit, inv):
    scaled = grad * gain
    return inv * (
        scaled
        - jnp.mean(scaled, axis=-1, keepdims=True)
        - unit * jnp.mean(scaled * unit, axis=-1, keepdims=True)
    )


def split_heads(x):
    first = lax.broadcasted_iota(jnp.int32, x.shape, 1) < HD
    return jnp.concatenate([jnp.where(first, x, 0.0), jnp.where(first, 0.0, x)], axis=0)


def kernel(
    hid_ref, cot_ref, len_ref, wqkv_ref, bqv_ref, wout_ref, bout_ref, wup_ref, bup_ref, wdown_ref, bdown_ref,
    gain_ref, shift_ref,
    out_ref, ingrad_ref, dwo_ref, vsum_ref, bsum_ref,
    W, dW, rb1, rb2, rc, FB, BB, dr, yr, part, sb,
    qkv, kvo, prob, att, xrow, midrow, slope, act,
    gpre, gkeep, gproj, gks, gkr, gyrow, gmidrow,
    VG, V, GV, GT, vr, vr2, gb, br, gq, bq, vrow, bqkv, dwo,
    g1s, g1r, g2s, g2r, g3s, g3r, q1s, q1r, q2s, q2r,
    s1, r1, s2, r2, s3, r3, s4, r4, ks, kr, gs_s, gs_r, vs, vrs, es, er, lsem, wsem, osem,
):
    f, s, t = lax.axis_index("fsdp"), lax.axis_index("seq"), lax.axis_index("tp")
    me = f * 2 + s
    xh, z = f // 4, f % 4
    x = xh * 2 + s
    y, core = t // 2, t % 2
    other = 1 - core

    def shard_dev(k):
        j = (me + k) % SHARDS
        return j, (j // 2, j % 2, t)

    def x_dev(k):
        j = (x + k) % 4
        return j // 2, j % 2, ((j // 2) * 4 + z, j % 2, t)

    def z_dev(k):
        j = (z + k) % 4
        return j, (xh * 4 + j, s, t)

    def y_dev(k):
        j = (y + k) % 4
        return j, (f, s, j * 2 + core)

    core_dev = (f, s, y * 2 + other)
    seq_dev = (f, 1 - s, t)

    def remote(src, dst, ss, rs, dev):
        return pltpu.make_async_remote_copy(
            src_ref=src, dst_ref=dst, send_sem=ss, recv_sem=rs, device_id=dev, device_id_type=MESH
        )

    def wait_bytes(ref, sem):
        pltpu.make_async_copy(ref, ref, sem).wait()

    cp_h = pltpu.make_async_copy(hid_ref, FB.at[0], lsem.at[0])
    cp_c = pltpu.make_async_copy(cot_ref, BB.at[0], lsem.at[1])
    cp_h.start()
    cp_c.start()

    for l in range(2):
        for p in range(2):
            pltpu.make_async_copy((wup_ref, wdown_ref)[p].at[l], W.at[l, p + 1, xh, z, s], wsem.at[l, p]).start()

    barrier = pltpu.get_barrier_semaphore()

    @pl.loop(1, SHARDS)
    def _(k):
        pl.semaphore_signal(barrier, inc=1, device_id=shard_dev(k)[1], device_id_type=MESH)

    @pl.loop(1, 8)
    def _(k):
        pl.semaphore_signal(barrier, inc=1, device_id=(f, s, (t + k) % 8), device_id_type=MESH)

    def pack(l, p):
        if p == 0:
            parts = [wqkv_ref[l, i].astype(F32) for i in range(3)] + [wout_ref[l].astype(F32).T]
            W[l, 0, xh, z, s] = jnp.concatenate(parts, axis=1).astype(BF)
        else:
            pltpu.make_async_copy((wup_ref, wdown_ref)[p - 1].at[l], W.at[l, p, xh, z, s], wsem.at[l, p - 1]).wait()

    vrow[...] = jnp.zeros_like(vrow)
    for l in range(2):
        for r in range(2):
            vrow[8 * l + r : 8 * l + r + 1, 0:SHARD] = gain_ref[l, r : r + 1, :].astype(F32)
            vrow[8 * l + 2 + r : 8 * l + 3 + r, 0:SHARD] = shift_ref[l, r : r + 1, :].astype(F32)
        vrow[8 * l + 4 : 8 * l + 5, 0:SHARD] = bout_ref[l : l + 1, :].astype(F32)
        vrow[8 * l + 5 : 8 * l + 6, 0:SHARD] = bdown_ref[l : l + 1, :].astype(F32)
    VG[me] = pltpu.roll(vrow[...], (SHARD * me) % 128, 1).astype(BF)
    pack(0, 0)
    pl.semaphore_wait(barrier, 22)

    def load(n):
        l, p, one, two = LOADS[n]
        ways = ([(0, slice(*one))] if one else []) + ([(1, slice(*two))] if two else [])
        return l, p, ways

    def gather_one(n):
        l, p, ways = load(n)
        for way, cols in ways:
            own = W.at[l, p, xh, z, s, :, cols]
            for k in range(1, 4):
                dev = x_dev(k)[2] if way else z_dev(k)[1]
                remote(own, own, g1s.at[n, way], g1r.at[n, way], dev).start()

    def gather_mid(n):
        l, p, ways = load(n)
        for way, cols in ways:
            three = W.at[l, p, 0, pl.ds(0, 3), 0, :, cols]
            wait_bytes(three, g1r.at[n, way])
            wait_bytes(three, g1s.at[n, way])

    def gather_two(n):
        l, p, ways = load(n)
        gather_mid(n)
        for way, cols in ways:
            four = W.at[l, p, :, z, :, :, cols] if way else W.at[l, p, xh, :, s, :, cols]
            for k in range(1, 4):
                dev = z_dev(k)[1] if way else x_dev(k)[2]
                remote(four, four, g2s.at[n, way], g2r.at[n, way], dev).start()

    def gather_wait(n):
        l, p, ways = load(n)
        for way, cols in ways:
            twelve = W.at[l, p, :, pl.ds(0, 3), :, :, cols]
            wait_bytes(twelve, g2r.at[n, way])
            wait_bytes(twelve, g2s.at[n, way])

    def ring_dev(way, k):
        return z_dev(k)[1] if way else x_dev(k)[2]

    def ring_two(n):
        l, p, ways = load(n)
        gather_mid(n)
        for way, cols in ways:
            four = W.at[l, p, :, z, :, :, cols] if way else W.at[l, p, xh, :, s, :, cols]
            for k in (1, 3):
                remote(four, four, g2s.at[n, way], g2r.at[n, way], ring_dev(way, k)).start()

    def ring_mid(n):
        l, p, ways = load(n)
        for way, cols in ways:
            eight = W.at[l, p, 0, :, :, :, cols]
            wait_bytes(eight, g2r.at[n, way])
            wait_bytes(eight, g2s.at[n, way])

    def ring_three(n):
        l, p, ways = load(n)
        ring_mid(n)
        for way, cols in ways:
            if way:
                left = W.at[l, p, 0, (z + 3) % 4, :, :, cols]
                right = W.at[l, p, 1, (z + 1) % 4, :, :, cols]
            else:
                il, ir = (x + 3) % 4, (x + 1) % 4
                left = W.at[l, p, il // 2, pl.ds(0, 2), il % 2, :, cols]
                right = W.at[l, p, ir // 2, pl.ds(2, 2), ir % 2, :, cols]
            remote(left, left, g3s.at[n, way], g3r.at[n, way], ring_dev(way, 1)).start()
            remote(right, right, g3s.at[n, way], g3r.at[n, way], ring_dev(way, 3)).start()

    def ring_wait(n):
        l, p, ways = load(n)
        for way, cols in ways:
            four = W.at[l, p, 0, pl.ds(0, 2), :, :, cols]
            wait_bytes(four, g3r.at[n, way])
            wait_bytes(four, g3s.at[n, way])

    def piece(l, i):
        part_idx, one, two = PIECES[i]
        both = [(0, slice(*one))] + ([(1, slice(*two))] if two else [])
        return part_idx, both

    def reduce_one(l, i):
        p, ways = piece(l, i)
        for way, cols in ways:
            for k in range(1, 4):
                if way:
                    j, dev = z_dev(k)
                    four = dW.at[l, p, :, j, :, :, cols]
                    buf = rb2.at[l, p, k - 1, :, :, :, 0 : cols.stop - cols.start]
                else:
                    jh, jl, dev = x_dev(k)
                    four = dW.at[l, p, jh, :, jl, :, cols]
                    buf = rb1.at[l, p, k - 1, :, :, cols.start - 256 : cols.stop - 256]
                remote(four, buf, q1s.at[l, i, way], q1r.at[l, i, way], dev).start()

    def reduce_mid(l, i):
        p, ways = piece(l, i)
        for way, cols in ways:
            twelve = dW.at[l, p, :, pl.ds(0, 3), :, :, cols]
            wait_bytes(twelve, q1r.at[l, i, way])
            wait_bytes(twelve, q1s.at[l, i, way])

    def reduce_two(l, i):
        p, ways = piece(l, i)
        reduce_mid(l, i)

        @pl.loop(0, 4)
        def _(n):
            nh, nl = n // 2, n % 2
            for way, cols in ways:
                if way:
                    total = dW[l, p, nh, z, nl, :, cols].astype(F32)
                    for k in range(3):
                        total = total + rb2[l, p, k, nh, nl, :, 0 : cols.stop - cols.start].astype(F32)
                    dW[l, p, nh, z, nl, :, cols] = total.astype(BF)
                else:
                    total = dW[l, p, xh, n, s, :, cols].astype(F32)
                    for k in range(3):
                        total = total + rb1[l, p, k, n, :, cols.start - 256 : cols.stop - 256].astype(F32)
                    dW[l, p, xh, n, s, :, cols] = total.astype(BF)

        for way, cols in ways:
            for k in range(1, 4):
                if way:
                    jh, jl, dev = x_dev(k)
                    one = dW.at[l, p, jh, z, jl, :, cols]
                else:
                    j, dev = z_dev(k)
                    one = dW.at[l, p, xh, j, s, :, cols]
                remote(one, rc.at[l, p, k - 1, :, cols], q2s.at[l, i, way], q2r.at[l, i, way], dev).start()

    def reduce_last(l, i):
        p, ways = piece(l, i)
        for way, cols in ways:
            three = dW.at[l, p, 0, pl.ds(0, 3), 0, :, cols]
            wait_bytes(three, q2r.at[l, i, way])
            wait_bytes(three, q2s.at[l, i, way])

    def reduce_three(l, i):
        p, ways = piece(l, i)
        reduce_last(l, i)
        for way, cols in ways:
            total = dW[l, p, xh, z, s, :, cols].astype(F32)
            for k in range(3):
                total = total + rc[l, p, k, :, cols].astype(F32)
            dwo[l, p, :, cols] = total
            own = dwo.at[l, p, :, cols]
            pltpu.make_async_copy(own, dwo_ref.at[l, p, :, cols], osem.at[l, i, way]).start()

    def vec(l, r):
        return V[l, r : r + 1, 0:D]

    def rs_start(a, c, value_of):
        for h in range(2):
            lanes = slice(640 * h, 640 * h + 640)
            part[c, :, :, :, lanes] = value_of(h).astype(BF).reshape(4, 2, 16, 640)
            remote(
                part.at[c, :, other, :, lanes], dr.at[a, c, :, :, lanes], s1.at[c, h], r1.at[a, c, h], core_dev
            ).start()

    def rs_mid(a, c):
        for h in range(2):
            lanes = slice(640 * h, 640 * h + 640)
            half = dr.at[a, c, :, :, lanes]
            wait_bytes(half, r1.at[a, c, h])
            wait_bytes(half, s1.at[c, h])
            sb[c, :, :, lanes] = (
                part[c, :, core, :, lanes].astype(F32) + dr[a, c, :, :, lanes].astype(F32)
            ).astype(BF)
            for k in (2, 1, 3):
                j, dev = y_dev(k)
                remote(
                    sb.at[c, j, :, lanes], yr.at[a, c, k - 1, :, lanes], s2.at[c], r2.at[a, c], dev
                ).start()

    def rs_end(a, c):
        wait_bytes(yr.at[a, c], r2.at[a, c])
        wait_bytes(yr.at[a, c], s2.at[c])
        total = sb[c, y].astype(F32)
        for k in range(3):
            total = total + yr[a, c, k].astype(F32)
        return total

    def ag_start(buf, i, a, c, value):
        buf[i, c, y, core] = value.astype(BF)
        for k in (2, 1, 3):
            _, dev = y_dev(k)
            remote(buf.at[i, c, y, core], buf.at[i, c, y, core], s3.at[c], r3.at[a, c], dev).start()

    def ag_mid(buf, i, a, c):
        wait_bytes(yr.at[a, c], r3.at[a, c])
        wait_bytes(yr.at[a, c], s3.at[c])
        remote(buf.at[i, c, :, core], buf.at[i, c, :, core], s4.at[c], r4.at[a, c], core_dev).start()

    def ag_end(a, c):
        wait_bytes(dr.at[a, c], r4.at[a, c])
        wait_bytes(dr.at[a, c], s4.at[c])

    def heads_of(l, c):
        own = qkv[l, c].astype(F32)
        far = kvo[l, c].astype(F32)
        q = own[:, 0:160]
        k = jnp.concatenate([own[:, 160:320], far[:, 32:192]], axis=0)
        v = jnp.concatenate([own[:, 320:480], far[:, 192:352]], axis=0)
        return split_heads(q).astype(BF), k, v

    def project(l, c):
        normed = FB[2 * l, c].reshape(ROWS, D)
        proj = dot_nn(normed, W[l, 0, :, :, :, :, 0:512].reshape(D, 512)) + bqkv[l]
        qkv[l, c] = proj.astype(BF)
        remote(qkv.at[l, c, :, 128:512], kvo.at[l, c], ks.at[l, c], kr.at[l, c], seq_dev).start()

    def attend(l, c):
        wait_bytes(kvo.at[l, c], kr.at[l, c])
        wait_bytes(kvo.at[l, c], ks.at[l, c])
        q2, k, v = heads_of(l, c)
        scores = dot_nt(q2, k.astype(BF)) * SCALING
        slot = lax.broadcasted_iota(jnp.int32, (1, 2 * ROWS), 1)
        slot = jnp.where(slot < ROWS, slot + s * ROWS, slot - s * ROWS)
        scores = jnp.where(slot < len_ref[c], scores, MASKED)
        top = jnp.max(scores, axis=-1, keepdims=True)
        powers = jnp.exp(scores - top)
        probs = powers / jnp.sum(powers, axis=-1, keepdims=True)
        prob[l, c] = probs
        low = probs.astype(BF)
        attended = dot_nn(
            jnp.concatenate([low[0:ROWS], low[ROWS:]], axis=1), split_heads(v).astype(BF)
        )
        wide = jnp.concatenate([jnp.zeros((ROWS, 96), F32), attended], axis=1).astype(BF)
        att[l, c] = wide
        rs_start(2 * l, c, lambda h: dot_nt(wide, W[l, 0, h, :, :, :, 384:640].reshape(640, 256)))

    def attend_rows(l, c):
        a = 2 * l
        middle = xrow[l, c] + rs_end(a, c) + vec(l, 4)
        midrow[l, c] = middle
        unit, _ = norm_parts(middle)
        ag_start(FB, 2 * l + 1, a, c, unit * vec(l, 1) + vec(l, 3))

    def feed(l, c):
        normed = FB[2 * l + 1, c].reshape(ROWS, D)
        pre = dot_nn(normed, W[l, 1].reshape(D, PART)) + bup_ref[l : l + 1, :].astype(F32)
        cdf = 0.5 * (1.0 + lax.erf(pre * math.sqrt(0.5)))
        activated = (pre * cdf).astype(BF)
        act[l, c] = activated
        slope[l, c] = cdf + pre * jnp.exp(-0.5 * pre * pre) * (1.0 / math.sqrt(2.0 * math.pi))
        if c == 0 and l == 0:
            ring_wait(DOWN0X)
            ring_wait(DOWN0Z)
        elif c == 0:
            ring_wait(DOWN1)
        rs_start(2 * l + 1, c, lambda h: dot_nt(activated, W[l, 2, h].reshape(640, PART)))

    def feed_rows(l, c):
        a = 2 * l + 1
        hidden = midrow[l, c] + rs_end(a, c) + vec(l, 5)
        if l == 0:
            xrow[1, c] = hidden
            unit, _ = norm_parts(hidden)
            hidden = unit * vec(1, 0) + vec(1, 2)
        ag_start(FB, 2 * l + 2, a, c, hidden)

    def feed_back(l, c):
        grad_act = dot_nn(BB[2 - 2 * l, c].reshape(ROWS, D), W[l, 2].reshape(D, PART))
        grad_pre = (grad_act * slope[l, c]).astype(BF)
        gpre[c] = grad_pre
        gb[2 + l : 3 + l, :] += jnp.sum(grad_pre.astype(F32), axis=0, keepdims=True)
        rs_start(6 - 2 * l, c, lambda h: dot_nt(grad_pre, W[l, 1, h].reshape(640, PART)))

    def feed_back_rows(l, c):
        a = 6 - 2 * l
        grad_norm = rs_end(a, c)
        unit, inv = norm_parts(midrow[l, c])
        gy = gyrow[c]
        grad_mid = gy + norm_back(grad_norm, vec(l, 1), unit, inv)
        gmidrow[c] = grad_mid
        ag_start(BB, 3 - 2 * l, a, c, grad_mid)
        GV[l, 1:2, 0:D] += jnp.sum(grad_norm * unit, axis=0, keepdims=True)
        GV[l, 3:4, 0:D] += jnp.sum(grad_norm, axis=0, keepdims=True)
        GV[l, 4:5, 0:D] += jnp.sum(grad_mid, axis=0, keepdims=True)
        GV[l, 5:6, 0:D] += jnp.sum(gy, axis=0, keepdims=True)

    def attend_back(l, c):
        wide = dot_nn(BB[3 - 2 * l, c].reshape(ROWS, D), W[l, 0, :, :, :, :, 384:640].reshape(D, 256))
        ga2 = split_heads(wide[:, 96:256]).astype(BF)
        q2, k, v = heads_of(l, c)
        probs = prob[l, c]
        grad_probs = dot_nt(ga2, v.astype(BF))
        grad_scores = probs * (grad_probs - jnp.sum(probs * grad_probs, axis=-1, keepdims=True))
        low = grad_scores.astype(BF)
        grad_v = dot_tn(probs.astype(BF), ga2)
        grad_k = dot_tn(low, q2) * SCALING
        pad = jnp.zeros((ROWS, 64), F32)
        gks[c] = jnp.concatenate([grad_k[ROWS:], grad_v[ROWS:], pad], axis=1).astype(BF)
        remote(gks.at[c], gkr.at[l, c], gs_s.at[c], gs_r.at[l, c], seq_dev).start()
        grad_q = (
            dot_nn(jnp.concatenate([low[0:ROWS], low[ROWS:]], axis=1), split_heads(k).astype(BF))
            * SCALING
        )
        gkeep[c, :, 0:160] = grad_q
        gkeep[c, :, 160:320] = grad_k[0:ROWS]
        gkeep[c, :, 320:480] = grad_v[0:ROWS]
        gkeep[c, :, 480:512] = jnp.zeros((ROWS, 32), F32)

    def project_back(l, c):
        wait_bytes(gkr.at[l, c], gs_r.at[l, c])
        wait_bytes(gkr.at[l, c], gs_s.at[c])
        far = gkr[l, c].astype(F32)
        gkeep[c, :, 160:480] += far[:, 0:320]
        grads = gkeep[c].astype(BF)
        gproj[c] = grads
        total = jnp.sum(grads.astype(F32), axis=0, keepdims=True)
        if l:
            gb[1:2, 0:512] += total
        else:
            for i in range(4):
                gq[i : i + 1, :] += total[:, 128 * i : 128 * i + 128]
        rs_start(7 - 2 * l, c, lambda h: dot_nt(grads, W[l, 0, h, :, :, :, 0:512].reshape(640, 512)))

    def project_back_rows(l, c):
        a = 7 - 2 * l
        grad_norm = rs_end(a, c)
        unit, inv = norm_parts(xrow[l, c])
        gy = gmidrow[c] + norm_back(grad_norm, vec(l, 0), unit, inv)
        gyrow[c] = gy
        ag_start(BB, 4 - 2 * l, a, c, gy)
        GV[l, 0:1, 0:D] += jnp.sum(grad_norm * unit, axis=0, keepdims=True)
        GV[l, 2:3, 0:D] += jnp.sum(grad_norm, axis=0, keepdims=True)

    def left_of(buf, i, m):
        return buf[i, :, :, :, :, 640 * m : 640 * m + 640].reshape(MICRO * ROWS, 640)

    def down_grad(l, m):
        right = act[l].reshape(MICRO * ROWS, PART)
        dW[l, 2, m] = dot_tn(left_of(BB, 2 - 2 * l, m), right).astype(BF).reshape(4, 2, SHARD, PART)

    def up_grad(l, m):
        right = gpre[...].reshape(MICRO * ROWS, PART)
        dW[l, 1, m] = dot_tn(left_of(FB, 2 * l + 1, m), right).astype(BF).reshape(4, 2, SHARD, PART)

    def out_grad(l, m):
        grad = dot_tn(left_of(BB, 3 - 2 * l, m), att[l].reshape(MICRO * ROWS, 256))
        dW[l, 0, m, :, :, :, 384:640] = grad.astype(BF).reshape(4, 2, SHARD, 256)

    def qkv_grad(l, m):
        grad = dot_tn(left_of(FB, 2 * l, m), gproj[...].reshape(MICRO * ROWS, 512))
        dW[l, 0, m, :, :, :, 0:384] = grad[:, 0:384].astype(BF).reshape(4, 2, SHARD, 384)
        rest = dW[l, 0, m, :, :, :, 384:512].astype(F32).reshape(640, 128) + grad[:, 384:512]
        dW[l, 0, m, :, :, :, 384:512] = rest.astype(BF).reshape(4, 2, SHARD, 128)

    @pl.loop(1, SHARDS)
    def _(k):
        remote(VG.at[me], VG.at[me], vs.at[0], vrs.at[0], shard_dev(k)[1]).start()

    gather_one(QKV0)
    gather_one(OUT0)
    pack(0, 1)
    pack(0, 2)
    V[...] = jnp.zeros_like(V)
    GV[...] = jnp.zeros_like(GV)
    gb[...] = jnp.zeros_like(gb)
    gq[...] = jnp.zeros_like(gq)
    bqkv[...] = jnp.zeros_like(bqkv)
    for l in range(2):
        bqkv[l, :, 0:160] = bqv_ref[l, 0:1, :].astype(F32)
        bqkv[l, :, 320:480] = bqv_ref[l, 1:2, :].astype(F32)
    gather_two(QKV0)
    wait_bytes(VG.at[pl.ds(0, SHARDS - 1)], vrs.at[0])
    wait_bytes(VG.at[pl.ds(0, SHARDS - 1)], vs.at[0])
    for i in range(SHARDS):
        low = SHARD * i // 128 * 128
        held = VG[i].astype(F32)
        V[0, :, low : low + 256] += held[0:8]
        V[1, :, low : low + 256] += held[8:16]
    cp_h.wait()
    cp_c.wait()
    gather_one(UP0)
    gather_one(DOWN0Z)
    gather_one(DOWN0X)
    for c in range(MICRO):
        whole = FB[0, c].reshape(ROWS, D).astype(F32)
        unit, _ = norm_parts(whole)
        xrow[0, c] = FB[0, c, y, core].astype(F32)
        FB[0, c] = (unit * vec(0, 0) + vec(0, 2)).astype(BF).reshape(4, 2, 16, D)
    gather_two(OUT0)
    ring_two(UP0)
    gather_wait(QKV0)

    def mask_grads():
        row = lax.broadcasted_iota(jnp.int32, (ROWS, 1), 0) + s * ROWS
        for c in range(MICRO):
            masked = jnp.where(row < len_ref[c], BB[0, c].reshape(ROWS, D).astype(F32), 0.0)
            BB[0, c] = masked.astype(BF).reshape(4, 2, 16, D)
            gyrow[c] = BB[0, c, y, core].astype(F32)

    def bias_sums():
        @pl.loop(1, SHARDS)
        def _(k):
            remote(gb, br.at[k - 1], es.at[1], er.at[1], shard_dev(k)[1]).start()

    def last_sums():
        @pl.loop(1, SHARDS)
        def _(k):
            remote(gq, bq.at[k - 1], es.at[3], er.at[3], shard_dev(k)[1]).start()

    def norm_sums():
        for i in range(11):
            GT[i, 0:8] = GV[0, :, 128 * i : 128 * i + 128]
            GT[i, 8:16] = GV[1, :, 128 * i : 128 * i + 128]

        @pl.loop(1, SHARDS)
        def _(k):
            j, dev = shard_dev(k)
            remote(GT.at[pl.ds(SHARD * j // 128, 2)], vr.at[k - 1], es.at[0], er.at[0], dev).start()

    cp_o = pltpu.make_async_copy(FB.at[4], out_ref, lsem.at[0])
    cp_g = pltpu.make_async_copy(BB.at[4], ingrad_ref, lsem.at[1])

    steps = []
    sums = {}
    for l in (0, 1):
        for c in range(MICRO):
            steps.append((partial(project, l, c), None))
        for c in range(MICRO):
            steps.append((partial(attend, l, c), (2 * l, c)))
            sums[2 * l, c] = (partial(attend_rows, l, c), FB, 2 * l + 1)
        for c in range(MICRO):
            steps.append((partial(feed, l, c), (2 * l + 1, c)))
            sums[2 * l + 1, c] = (partial(feed_rows, l, c), FB, 2 * l + 2)
    for l in (1, 0):
        a0, a1 = 6 - 2 * l, 7 - 2 * l
        for c in range(MICRO):
            steps.append((partial(feed_back, l, c), (a0, c)))
            sums[a0, c] = (partial(feed_back_rows, l, c), BB, 3 - 2 * l)
        for c in range(MICRO):
            steps.append((partial(attend_back, l, c), None))
        for c in range(MICRO):
            steps.append((partial(project_back, l, c), (a1, c)))
            sums[a1, c] = (partial(project_back_rows, l, c), BB, 4 - 2 * l)

    g1, g2, g3, g4 = gather_one, ring_two, ring_three, ring_wait
    d1, d2, d3 = reduce_one, reduce_two, reduce_three
    before = {
        2: [(g2, DOWN0X)],
        3: [(g2, DOWN0Z), (gather_wait, OUT0)],
        4: [(g3, UP0), (g1, PROJ1)],
        5: [(g3, DOWN0Z), (g3, DOWN0X)],
        6: [(g4, UP0), (g2, PROJ1), (g1, UP1)],
        8: [(g3, PROJ1), (g2, UP1), (g1, DOWN1)],
        9: [(g4, PROJ1)],
        10: [(g3, UP1), (g2, DOWN1)],
        12: [(g3, DOWN1)],
        15: [(g4, UP1)],
    }
    between = {
        3: [(pack, 1, 0)],
        4: [(pack, 1, 1)],
        5: [(pack, 1, 2)],
        6: [(mask_grads,)],
        18: [(down_grad, 1, 0)],
        20: [(up_grad, 1, 0)],
        24: [(out_grad, 1, 0), (out_grad, 1, 1), (d1, 1, OUT)],
        25: [(d2, 1, UP)],
        26: [(qkv_grad, 1, 0)],
        27: [(d2, 1, OUT)],
        29: [(down_grad, 0, 0)],
        30: [(up_grad, 0, 0)],
        31: [(up_grad, 0, 1), (d1, 0, UP), (bias_sums,)],
        33: [(out_grad, 0, 0), (out_grad, 0, 1), (d1, 0, OUT)],
        34: [(d2, 0, DOWN)],
        35: [(qkv_grad, 0, 0), (qkv_grad, 0, 1), (d1, 0, QKV), (last_sums,)],
        36: [(d2, 0, OUT)],
    }
    later = {
        18: [(down_grad, 1, 1), (d1, 1, DOWN)],
        20: [(up_grad, 1, 1), (d1, 1, UP)],
        24: [(d2, 1, DOWN)],
        26: [(qkv_grad, 1, 1), (d1, 1, QKV)],
        27: [(d3, 1, DOWN)],
        28: [(d3, 1, UP)],
        29: [(down_grad, 0, 1), (d1, 0, DOWN)],
        33: [(d2, 1, QKV)],
        34: [(d2, 0, UP), (d3, 1, OUT)],
    }
    for n in range(len(steps) + 2):
        for fn, *where in before.get(n, ()):
            fn(*where)
        if n < len(steps):
            steps[n][0]()
        for fn, *where in between.get(n, ()):
            fn(*where)
        if n < len(steps) and steps[n][1] is not None:
            rs_mid(*steps[n][1])
        if 1 <= n <= len(steps) and steps[n - 1][1] is not None:
            sums[steps[n - 1][1]][0]()
        if n == len(steps):
            norm_sums()
        if n >= 2 and steps[n - 2][1] is not None:
            a, c = steps[n - 2][1]
            ag_mid(sums[a, c][1], sums[a, c][2], a, c)
        for fn, *where in later.get(n, ()):
            fn(*where)
        if n >= 2 and steps[n - 2][1] is not None:
            ag_end(*steps[n - 2][1])
        if n == 19:
            cp_o.start()

    cp_g.start()
    for l, i in ((1, QKV), (0, DOWN), (0, UP)):
        reduce_three(l, i)
    wait_bytes(vr, er.at[0])
    wait_bytes(vr, es.at[0])
    own = GT[pl.ds(SHARD * me // 128, 2)]
    for k in range(SHARDS - 1):
        own = own + vr[k]
    vr2[7] = own

    @pl.loop(1, 8)
    def _(k):
        remote(vr2.at[7], vr2.at[k - 1], es.at[2], er.at[2], (f, s, (t + k) % 8)).start()

    wait_bytes(br, er.at[1])
    wait_bytes(br, es.at[1])
    wait_bytes(bq, er.at[3])
    wait_bytes(bq, es.at[3])
    totals = gb[...]
    lasts = gq[...]
    for k in range(SHARDS - 1):
        totals = totals + br[k]
        lasts = lasts + bq[k]
    bsum_ref[...] = totals
    for i in range(4):
        bsum_ref[0:1, 128 * i : 128 * i + 128] = lasts[i : i + 1]
    reduce_two(0, QKV)
    for l, i in ((0, OUT),):
        reduce_three(l, i)
    wait_bytes(vr2.at[pl.ds(0, 7)], er.at[2])
    wait_bytes(vr2.at[pl.ds(0, 7)], es.at[2])
    own = vr2[7]
    for k in range(7):
        own = own + vr2[k]
    vsum_ref[...] = own
    reduce_three(0, QKV)
    for l in range(2):
        for i in range(4):
            p, ways = piece(l, i)
            for way, cols in ways:
                pltpu.make_async_copy(dwo.at[l, p, :, cols], dwo_ref.at[l, p, :, cols], osem.at[l, i, way]).wait()
    cp_o.wait()
    cp_g.wait()


def finish(
    out_ref, ingrad_ref, dwo_ref, vsum_ref, bsum_ref,
    hidden_ref, grad_ref, gqkv_ref, gqv_ref, gout_ref, gbout_ref, gup_ref, gbup_ref, gdown_ref, gbdown_ref,
    ggain_ref, gshift_ref,
    narrow, wide, dwo, in_sem, out_sem, w_sem, g_sem,
):
    me = lax.axis_index("fsdp") * 2 + lax.axis_index("seq")
    tasks = [(a, c) for c in range(MICRO) for a in range(2)]
    sources, targets = (out_ref, ingrad_ref), (hidden_ref, grad_ref)

    def fetch(a, c):
        return pltpu.make_async_copy(sources[a].at[c], narrow.at[a, c], in_sem.at[a, c])

    def store(a, c):
        return pltpu.make_async_copy(wide.at[a, c], targets[a].at[c], out_sem.at[a, c])

    weights = pltpu.make_async_copy(dwo_ref, dwo, w_sem.at[0])
    for a, c in tasks:
        fetch(a, c).start()
    weights.start()
    ups = pltpu.make_async_copy(dwo.at[:, 1], gup_ref, g_sem.at[0])
    downs = pltpu.make_async_copy(dwo.at[:, 2], gdown_ref, g_sem.at[1])
    for a, c in tasks:
        fetch(a, c).wait()
        wide[a, c] = narrow[a, c].astype(F32)
        store(a, c).start()
    weights.wait()
    ups.start()
    downs.start()
    rows = jnp.concatenate([vsum_ref[0], vsum_ref[1]], axis=1)
    rows = pltpu.roll(rows, (256 - (SHARD * me) % 128) % 256, 1)
    for l in range(2):
        proj = dwo[l, 0]
        for i in range(3):
            gqkv_ref[l, i] = proj[:, 160 * i : 160 * i + 160]
        gout_ref[l] = proj[:, 480:640].T
        gqv_ref[l, 0:1, :] = bsum_ref[l : l + 1, 0:160]
        gqv_ref[l, 1:2, :] = bsum_ref[l : l + 1, 320:480]
        gbup_ref[l : l + 1, :] = bsum_ref[2 + l : 3 + l, :]
        ggain_ref[l] = rows[8 * l : 8 * l + 2, 0:SHARD]
        gshift_ref[l] = rows[8 * l + 2 : 8 * l + 4, 0:SHARD]
        gbout_ref[l : l + 1, :] = rows[8 * l + 4 : 8 * l + 5, 0:SHARD]
        gbdown_ref[l : l + 1, :] = rows[8 * l + 5 : 8 * l + 6, 0:SHARD]
    ups.wait()
    downs.wait()
    for a, c in tasks:
        store(a, c).wait()


def body(
    hidden_in, cotangent, lengths, qkv_weight, qv_bias, out_weight, out_bias,
    up_weight, up_bias, down_weight, down_bias, ln_gain, ln_bias,
):
    vmem = pl.BlockSpec(memory_space=pltpu.VMEM)
    anys = pl.BlockSpec(memory_space=pl.ANY)
    smem = pl.BlockSpec(memory_space=pltpu.SMEM)
    dma = pltpu.SemaphoreType.DMA
    blocks = (MICRO, 4, 2, 16, D)
    scratch = [
        pltpu.VMEM((2, 3, 2, 4, 2, SHARD, PART), BF),
        pltpu.VMEM((2, 3, 2, 4, 2, SHARD, PART), BF),
        pltpu.VMEM((2, 3, 3, 4, SHARD, 384), BF),
        pltpu.VMEM((2, 3, 3, 2, 2, SHARD, 384), BF),
        pltpu.VMEM((2, 3, 3, SHARD, PART), BF),
        pltpu.VMEM((5,) + blocks, BF),
        pltpu.VMEM((5,) + blocks, BF),
        pltpu.VMEM((8, MICRO, 4, 16, D), BF),
        pltpu.VMEM((8, MICRO, 3, 16, D), BF),
        pltpu.VMEM(blocks, BF),
        pltpu.VMEM((MICRO, 4, 16, D), BF),
        pltpu.VMEM((2, MICRO, ROWS, 512), BF),
        pltpu.VMEM((2, MICRO, ROWS, 384), BF),
        pltpu.VMEM((2, MICRO, 2 * ROWS, 2 * ROWS), F32),
        pltpu.VMEM((2, MICRO, ROWS, 256), BF),
        pltpu.VMEM((2, MICRO, 16, D), F32),
        pltpu.VMEM((2, MICRO, 16, D), F32),
        pltpu.VMEM((2, MICRO, ROWS, PART), F32),
        pltpu.VMEM((2, MICRO, ROWS, PART), BF),
        pltpu.VMEM((MICRO, ROWS, PART), BF),
        pltpu.VMEM((MICRO, ROWS, 512), F32),
        pltpu.VMEM((MICRO, ROWS, 512), BF),
        pltpu.VMEM((MICRO, ROWS, 384), BF),
        pltpu.VMEM((2, MICRO, ROWS, 384), BF),
        pltpu.VMEM((MICRO, 16, D), F32),
        pltpu.VMEM((MICRO, 16, D), F32),
        pltpu.VMEM((SHARDS, 16, 256), BF),
        pltpu.VMEM((2, 8, 1408), F32),
        pltpu.VMEM((2, 8, 1408), F32),
        pltpu.VMEM((11, 16, 128), F32),
        pltpu.VMEM((SHARDS - 1, 2, 16, 128), F32),
        pltpu.VMEM((8, 2, 16, 128), F32),
        pltpu.VMEM((8, PART), F32),
        pltpu.VMEM((SHARDS - 1, 8, PART), F32),
        pltpu.VMEM((8, 128), F32),
        pltpu.VMEM((SHARDS - 1, 8, 128), F32),
        pltpu.VMEM((16, 256), F32),
        pltpu.VMEM((2, 1, 512), F32),
        pltpu.VMEM((2, 3, SHARD, PART), F32),
        dma((8, 2)), dma((8, 2)), dma((8, 2)), dma((8, 2)), dma((8, 2)), dma((8, 2)),
        dma((2, 4, 2)), dma((2, 4, 2)), dma((2, 4, 2)), dma((2, 4, 2)),
        dma((MICRO, 2)), dma((8, MICRO, 2)), dma((MICRO,)), dma((8, MICRO)),
        dma((MICRO,)), dma((8, MICRO)), dma((MICRO,)), dma((8, MICRO)),
        dma((2, MICRO)), dma((2, MICRO)), dma((MICRO,)), dma((2, MICRO)),
        dma((1,)), dma((1,)), dma((4,)), dma((4,)), dma((2,)), dma((2, 2)), dma((2, 4, 2)),
    ]
    out, ingrad, dwo, vsum, bsum = pl.pallas_call(
        kernel,
        name="encoder",
        out_shape=(
            jax.ShapeDtypeStruct(blocks, BF),
            jax.ShapeDtypeStruct(blocks, BF),
            jax.ShapeDtypeStruct((2, 3, SHARD, PART), F32),
            jax.ShapeDtypeStruct((2, 16, 128), F32),
            jax.ShapeDtypeStruct((8, PART), F32),
        ),
        in_specs=[anys, anys, smem, vmem, vmem, vmem, vmem, anys, vmem, anys, vmem, vmem, vmem],
        out_specs=(anys, anys, anys, vmem, vmem),
        scratch_shapes=scratch,
        compiler_params=pltpu.CompilerParams(
            collective_id=0, has_side_effects=True, vmem_limit_bytes=63 * 1024 * 1024
        ),
    )(
        hidden_in.reshape(blocks), cotangent.reshape(blocks), lengths, qkv_weight, qv_bias, out_weight,
        out_bias, up_weight, up_bias, jnp.swapaxes(down_weight, 1, 2), down_bias, ln_gain, ln_bias,
    )
    rows = (MICRO, ROWS, D)
    shapes = (
        rows, rows, (2, 3, SHARD, 160), (2, 2, 160), (2, 160, SHARD), (2, SHARD), (2, SHARD, PART),
        (2, PART), (2, SHARD, PART), (2, SHARD), (2, 2, SHARD), (2, 2, SHARD),
    )
    outs = pl.pallas_call(
        finish,
        name="finish",
        out_shape=tuple(jax.ShapeDtypeStruct(shape, F32) for shape in shapes),
        in_specs=[anys, anys, anys, vmem, vmem],
        out_specs=(anys, anys, vmem, vmem, vmem, vmem, anys, vmem, anys, vmem, vmem, vmem),
        scratch_shapes=[
            pltpu.VMEM((2,) + rows, BF),
            pltpu.VMEM((2,) + rows, F32),
            pltpu.VMEM((2, 3, SHARD, PART), F32),
            dma((2, MICRO)), dma((2, MICRO)), dma((1,)), dma((2,)),
        ],
        compiler_params=pltpu.CompilerParams(vmem_limit_bytes=32 * 1024 * 1024),
    )(out.reshape(rows), ingrad.reshape(rows), dwo, vsum, bsum)
    return outs[:8] + (jnp.swapaxes(outs[8], 1, 2),) + outs[9:]


def solution(mesh):
    placed = (
        P("fsdp", "seq", None),
        P("fsdp", "seq", None),
        P("fsdp"),
        P(None, None, ("fsdp", "seq"), "tp"),
        P(None, None, "tp"),
        P(None, "tp", ("fsdp", "seq")),
        P(None, ("fsdp", "seq")),
        P(None, ("fsdp", "seq"), "tp"),
        P(None, "tp"),
        P(None, "tp", ("fsdp", "seq")),
        P(None, ("fsdp", "seq")),
        P(None, None, ("fsdp", "seq")),
        P(None, None, ("fsdp", "seq")),
    )
    return jax.shard_map(
        body,
        mesh=mesh,
        in_specs=placed,
        out_specs=(
            P("fsdp", "seq", None),
            P("fsdp", "seq", None),
            P(None, None, ("fsdp", "seq"), "tp"),
            P(None, None, "tp"),
            P(None, "tp", ("fsdp", "seq")),
            P(None, ("fsdp", "seq")),
            P(None, ("fsdp", "seq"), "tp"),
            P(None, "tp"),
            P(None, "tp", ("fsdp", "seq")),
            P(None, ("fsdp", "seq")),
            P(None, None, ("fsdp", "seq")),
            P(None, None, ("fsdp", "seq")),
        ),
        check_vma=False,
    )
```

```python
from functools import partial
import math

import jax
import jax.numpy as jnp
from jax import lax
from jax.experimental import pallas as pl
from jax.experimental.pallas import tpu as pltpu
from jax.sharding import PartitionSpec as P

HD = 80
EPSILON = 1e-05
MASKED = -1000000000.0
MESH = pl.DeviceIdType.MESH
BF = jnp.bfloat16
F32 = jnp.float32
SCALING = 1.0 / math.sqrt(HD)

D = 1280
MICRO = 3
ROWS = 128
PART = 640
SHARDS = 16
SHARD = 80

PIECES = (
    (0, (256, 512), (0, 256)),
    (0, (512, 640), None),
    (1, (384, 640), (0, 384)),
    (2, (384, 640), (0, 384)),
)
QKV, OUT, UP, DOWN = range(4)
LOADS = (
    (0, 0, (256, 512), (0, 256)),
    (0, 0, (512, 640), None),
    (0, 1, None, (0, 640)),
    (0, 2, (0, 256), None),
    (0, 2, None, (256, 640)),
    (1, 0, (384, 640), (0, 384)),
    (1, 1, (384, 640), (0, 384)),
    (1, 2, (384, 640), (0, 384)),
)
QKV0, OUT0, UP0, DOWN0X, DOWN0Z, PROJ1, UP1, DOWN1 = range(8)


def dot_nn(a, b):
    return lax.dot_general(a, b, (((1,), (0,)), ((), ())), preferred_element_type=F32)


def dot_nt(a, b):
    return lax.dot_general(a, b, (((1,), (1,)), ((), ())), preferred_element_type=F32)


def dot_tn(a, b):
    return lax.dot_general(a, b, (((0,), (0,)), ((), ())), preferred_element_type=F32)


def norm_parts(values):
    row_mean = jnp.mean(values, axis=-1, keepdims=True)
    centred = values - row_mean
    row_var = jnp.mean(centred * centred, axis=-1, keepdims=True)
    inv = lax.rsqrt(row_var + EPSILON)
    return centred * inv, inv


def norm_back(grad, gain, unit, inv):
    scaled = grad * gain
    return inv * (
        scaled
        - jnp.mean(scaled, axis=-1, keepdims=True)
        - unit * jnp.mean(scaled * unit, axis=-1, keepdims=True)
    )


def split_heads(x):
    first = lax.broadcasted_iota(jnp.int32, x.shape, 1) < HD
    return jnp.concatenate([jnp.where(first, x, 0.0), jnp.where(first, 0.0, x)], axis=0)


def kernel(
    hid_ref, cot_ref, len_ref, wqkv_ref, bqv_ref, wout_ref, bout_ref, wup_ref, bup_ref, wdown_ref, bdown_ref,
    gain_ref, shift_ref,
    out_ref, ingrad_ref, dwo_ref, vsum_ref, bsum_ref,
    W, dW, rb1, rb2, rc, FB, BB, dr, yr, part, sb,
    qkv, kvo, prob, att, xrow, midrow, slope, act,
    gpre, gkeep, gproj, gks, gkr, gyrow, gmidrow,
    VG, V, GV, GT, vr, vr2, gb, br, gq, bq, vrow, bqkv, dwo,
    g1s, g1r, g2s, g2r, g3s, g3r, q1s, q1r, q2s, q2r,
    s1, r1, s2, r2, s3, r3, s4, r4, ks, kr, gs_s, gs_r, vs, vrs, es, er, lsem, wsem, osem,
):
    f, s, t = lax.axis_index("fsdp"), lax.axis_index("seq"), lax.axis_index("tp")
    me = f * 2 + s
    xh, z = f // 4, f % 4
    x = xh * 2 + s
    y, core = t // 2, t % 2
    other = 1 - core

    def shard_dev(k):
        j = (me + k) % SHARDS
        return j, (j // 2, j % 2, t)

    def x_dev(k):
        j = (x + k) % 4
        return j // 2, j % 2, ((j // 2) * 4 + z, j % 2, t)

    def z_dev(k):
        j = (z + k) % 4
        return j, (xh * 4 + j, s, t)

    def y_dev(k):
        j = (y + k) % 4
        return j, (f, s, j * 2 + core)

    core_dev = (f, s, y * 2 + other)
    seq_dev = (f, 1 - s, t)

    def remote(src, dst, ss, rs, dev):
        return pltpu.make_async_remote_copy(
            src_ref=src, dst_ref=dst, send_sem=ss, recv_sem=rs, device_id=dev, device_id_type=MESH
        )

    def wait_bytes(ref, sem):
        pltpu.make_async_copy(ref, ref, sem).wait()

    cp_h = pltpu.make_async_copy(hid_ref, FB.at[0], lsem.at[0])
    cp_c = pltpu.make_async_copy(cot_ref, BB.at[0], lsem.at[1])
    cp_h.start()
    cp_c.start()

    for l in range(2):
        for p in range(2):
            pltpu.make_async_copy((wup_ref, wdown_ref)[p].at[l], W.at[l, p + 1, xh, z, s], wsem.at[l, p]).start()

    barrier = pltpu.get_barrier_semaphore()

    @pl.loop(1, SHARDS)
    def _(k):
        pl.semaphore_signal(barrier, inc=1, device_id=shard_dev(k)[1], device_id_type=MESH)

    @pl.loop(1, 8)
    def _(k):
        pl.semaphore_signal(barrier, inc=1, device_id=(f, s, (t + k) % 8), device_id_type=MESH)

    def pack(l, p):
        if p == 0:
            parts = [wqkv_ref[l, i].astype(F32) for i in range(3)] + [wout_ref[l].astype(F32).T]
            W[l, 0, xh, z, s] = jnp.concatenate(parts, axis=1).astype(BF)
        else:
            pltpu.make_async_copy((wup_ref, wdown_ref)[p - 1].at[l], W.at[l, p, xh, z, s], wsem.at[l, p - 1]).wait()

    vrow[...] = jnp.zeros_like(vrow)
    for l in range(2):
        for r in range(2):
            vrow[8 * l + r : 8 * l + r + 1, 0:SHARD] = gain_ref[l, r : r + 1, :].astype(F32)
            vrow[8 * l + 2 + r : 8 * l + 3 + r, 0:SHARD] = shift_ref[l, r : r + 1, :].astype(F32)
        vrow[8 * l + 4 : 8 * l + 5, 0:SHARD] = bout_ref[l : l + 1, :].astype(F32)
        vrow[8 * l + 5 : 8 * l + 6, 0:SHARD] = bdown_ref[l : l + 1, :].astype(F32)
    VG[me] = pltpu.roll(vrow[...], (SHARD * me) % 128, 1).astype(BF)
    pack(0, 0)
    pl.semaphore_wait(barrier, 22)

    def load(n):
        l, p, one, two = LOADS[n]
        ways = ([(0, slice(*one))] if one else []) + ([(1, slice(*two))] if two else [])
        return l, p, ways

    def gather_one(n):
        l, p, ways = load(n)
        for way, cols in ways:
            own = W.at[l, p, xh, z, s, :, cols]
            for k in range(1, 4):
                dev = x_dev(k)[2] if way else z_dev(k)[1]
                remote(own, own, g1s.at[n, way], g1r.at[n, way], dev).start()

    def gather_mid(n):
        l, p, ways = load(n)
        for way, cols in ways:
            three = W.at[l, p, 0, pl.ds(0, 3), 0, :, cols]
            wait_bytes(three, g1r.at[n, way])
            wait_bytes(three, g1s.at[n, way])

    def gather_two(n):
        l, p, ways = load(n)
        gather_mid(n)
        for way, cols in ways:
            four = W.at[l, p, :, z, :, :, cols] if way else W.at[l, p, xh, :, s, :, cols]
            for k in range(1, 4):
                dev = z_dev(k)[1] if way else x_dev(k)[2]
                remote(four, four, g2s.at[n, way], g2r.at[n, way], dev).start()

    def gather_wait(n):
        l, p, ways = load(n)
        for way, cols in ways:
            twelve = W.at[l, p, :, pl.ds(0, 3), :, :, cols]
            wait_bytes(twelve, g2r.at[n, way])
            wait_bytes(twelve, g2s.at[n, way])

    def ring_dev(way, k):
        return z_dev(k)[1] if way else x_dev(k)[2]

    def ring_two(n):
        l, p, ways = load(n)
        gather_mid(n)
        for way, cols in ways:
            four = W.at[l, p, :, z, :, :, cols] if way else W.at[l, p, xh, :, s, :, cols]
            for k in (1, 3):
                remote(four, four, g2s.at[n, way], g2r.at[n, way], ring_dev(way, k)).start()

    def ring_mid(n):
        l, p, ways = load(n)
        for way, cols in ways:
            eight = W.at[l, p, 0, :, :, :, cols]
            wait_bytes(eight, g2r.at[n, way])
            wait_bytes(eight, g2s.at[n, way])

    def ring_three(n):
        l, p, ways = load(n)
        ring_mid(n)
        for way, cols in ways:
            if way:
                left = W.at[l, p, 0, (z + 3) % 4, :, :, cols]
                right = W.at[l, p, 1, (z + 1) % 4, :, :, cols]
            else:
                il, ir = (x + 3) % 4, (x + 1) % 4
                left = W.at[l, p, il // 2, pl.ds(0, 2), il % 2, :, cols]
                right = W.at[l, p, ir // 2, pl.ds(2, 2), ir % 2, :, cols]
            remote(left, left, g3s.at[n, way], g3r.at[n, way], ring_dev(way, 1)).start()
            remote(right, right, g3s.at[n, way], g3r.at[n, way], ring_dev(way, 3)).start()

    def ring_wait(n):
        l, p, ways = load(n)
        for way, cols in ways:
            four = W.at[l, p, 0, pl.ds(0, 2), :, :, cols]
            wait_bytes(four, g3r.at[n, way])
            wait_bytes(four, g3s.at[n, way])

    def piece(l, i):
        part_idx, one, two = PIECES[i]
        both = [(0, slice(*one))] + ([(1, slice(*two))] if two else [])
        return part_idx, both

    def reduce_one(l, i):
        p, ways = piece(l, i)
        for way, cols in ways:
            for k in range(1, 4):
                if way:
                    j, dev = z_dev(k)
                    four = dW.at[l, p, :, j, :, :, cols]
                    buf = rb2.at[l, p, k - 1, :, :, :, 0 : cols.stop - cols.start]
                else:
                    jh, jl, dev = x_dev(k)
                    four = dW.at[l, p, jh, :, jl, :, cols]
                    buf = rb1.at[l, p, k - 1, :, :, cols.start - 256 : cols.stop - 256]
                remote(four, buf, q1s.at[l, i, way], q1r.at[l, i, way], dev).start()

    def reduce_mid(l, i):
        p, ways = piece(l, i)
        for way, cols in ways:
            twelve = dW.at[l, p, :, pl.ds(0, 3), :, :, cols]
            wait_bytes(twelve, q1r.at[l, i, way])
            wait_bytes(twelve, q1s.at[l, i, way])

    def reduce_two(l, i):
        p, ways = piece(l, i)
        reduce_mid(l, i)

        @pl.loop(0, 4)
        def _(n):
            nh, nl = n // 2, n % 2
            for way, cols in ways:
                if way:
                    total = dW[l, p, nh, z, nl, :, cols].astype(F32)
                    for k in range(3):
                        total = total + rb2[l, p, k, nh, nl, :, 0 : cols.stop - cols.start].astype(F32)
                    dW[l, p, nh, z, nl, :, cols] = total.astype(BF)
                else:
                    total = dW[l, p, xh, n, s, :, cols].astype(F32)
                    for k in range(3):
                        total = total + rb1[l, p, k, n, :, cols.start - 256 : cols.stop - 256].astype(F32)
                    dW[l, p, xh, n, s, :, cols] = total.astype(BF)

        for way, cols in ways:
            for k in range(1, 4):
                if way:
                    jh, jl, dev = x_dev(k)
                    one = dW.at[l, p, jh, z, jl, :, cols]
                else:
                    j, dev = z_dev(k)
                    one = dW.at[l, p, xh, j, s, :, cols]
                remote(one, rc.at[l, p, k - 1, :, cols], q2s.at[l, i, way], q2r.at[l, i, way], dev).start()

    def reduce_last(l, i):
        p, ways = piece(l, i)
        for way, cols in ways:
            three = dW.at[l, p, 0, pl.ds(0, 3), 0, :, cols]
            wait_bytes(three, q2r.at[l, i, way])
            wait_bytes(three, q2s.at[l, i, way])

    def reduce_three(l, i):
        p, ways = piece(l, i)
        reduce_last(l, i)
        for way, cols in ways:
            total = dW[l, p, xh, z, s, :, cols].astype(F32)
            for k in range(3):
                total = total + rc[l, p, k, :, cols].astype(F32)
            dwo[l, p, :, cols] = total
            own = dwo.at[l, p, :, cols]
            pltpu.make_async_copy(own, dwo_ref.at[l, p, :, cols], osem.at[l, i, way]).start()

    def vec(l, r):
        return V[l, r : r + 1, 0:D]

    def rs_start(a, c, value_of):
        for h in range(2):
            lanes = slice(640 * h, 640 * h + 640)
            part[c, :, :, :, lanes] = value_of(h).astype(BF).reshape(4, 2, 16, 640)
            remote(
                part.at[c, :, other, :, lanes], dr.at[a, c, :, :, lanes], s1.at[c, h], r1.at[a, c, h], core_dev
            ).start()

    def rs_mid(a, c):
        for h in range(2):
            lanes = slice(640 * h, 640 * h + 640)
            half = dr.at[a, c, :, :, lanes]
            wait_bytes(half, r1.at[a, c, h])
            wait_bytes(half, s1.at[c, h])
            sb[c, :, :, lanes] = (
                part[c, :, core, :, lanes].astype(F32) + dr[a, c, :, :, lanes].astype(F32)
            ).astype(BF)
            for k in (2, 1, 3):
                j, dev = y_dev(k)
                remote(
                    sb.at[c, j, :, lanes], yr.at[a, c, k - 1, :, lanes], s2.at[c], r2.at[a, c], dev
                ).start()

    def rs_end(a, c):
        wait_bytes(yr.at[a, c], r2.at[a, c])
        wait_bytes(yr.at[a, c], s2.at[c])
        total = sb[c, y].astype(F32)
        for k in range(3):
            total = total + yr[a, c, k].astype(F32)
        return total

    def ag_start(buf, i, a, c, value):
        buf[i, c, y, core] = value.astype(BF)
        for k in (2, 1, 3):
            _, dev = y_dev(k)
            remote(buf.at[i, c, y, core], buf.at[i, c, y, core], s3.at[c], r3.at[a, c], dev).start()

    def ag_mid(buf, i, a, c):
        wait_bytes(yr.at[a, c], r3.at[a, c])
        wait_bytes(yr.at[a, c], s3.at[c])
        remote(buf.at[i, c, :, core], buf.at[i, c, :, core], s4.at[c], r4.at[a, c], core_dev).start()

    def ag_end(a, c):
        wait_bytes(dr.at[a, c], r4.at[a, c])
        wait_bytes(dr.at[a, c], s4.at[c])

    def heads_of(l, c):
        own = qkv[l, c].astype(F32)
        far = kvo[l, c].astype(F32)
        q = own[:, 0:160]
        k = jnp.concatenate([own[:, 160:320], far[:, 32:192]], axis=0)
        v = jnp.concatenate([own[:, 320:480], far[:, 192:352]], axis=0)
        return split_heads(q).astype(BF), k, v

    def project(l, c):
        normed = FB[2 * l, c].reshape(ROWS, D)
        proj = dot_nn(normed, W[l, 0, :, :, :, :, 0:512].reshape(D, 512)) + bqkv[l]
        qkv[l, c] = proj.astype(BF)
        remote(qkv.at[l, c, :, 128:512], kvo.at[l, c], ks.at[l, c], kr.at[l, c], seq_dev).start()

    def attend(l, c):
        wait_bytes(kvo.at[l, c], kr.at[l, c])
        wait_bytes(kvo.at[l, c], ks.at[l, c])
        q2, k, v = heads_of(l, c)
        scores = dot_nt(q2, k.astype(BF)) * SCALING
        slot = lax.broadcasted_iota(jnp.int32, (1, 2 * ROWS), 1)
        slot = jnp.where(slot < ROWS, slot + s * ROWS, slot - s * ROWS)
        scores = jnp.where(slot < len_ref[c], scores, MASKED)
        top = jnp.max(scores, axis=-1, keepdims=True)
        powers = jnp.exp(scores - top)
        probs = powers / jnp.sum(powers, axis=-1, keepdims=True)
        prob[l, c] = probs
        low = probs.astype(BF)
        attended = dot_nn(
            jnp.concatenate([low[0:ROWS], low[ROWS:]], axis=1), split_heads(v).astype(BF)
        )
        wide = jnp.concatenate([jnp.zeros((ROWS, 96), F32), attended], axis=1).astype(BF)
        att[l, c] = wide
        rs_start(2 * l, c, lambda h: dot_nt(wide, W[l, 0, h, :, :, :, 384:640].reshape(640, 256)))

    def attend_rows(l, c):
        a = 2 * l
        middle = xrow[l, c] + rs_end(a, c) + vec(l, 4)
        midrow[l, c] = middle
        unit, _ = norm_parts(middle)
        ag_start(FB, 2 * l + 1, a, c, unit * vec(l, 1) + vec(l, 3))

    def feed(l, c):
        normed = FB[2 * l + 1, c].reshape(ROWS, D)
        pre = dot_nn(normed, W[l, 1].reshape(D, PART)) + bup_ref[l : l + 1, :].astype(F32)
        cdf = 0.5 * (1.0 + lax.erf(pre * math.sqrt(0.5)))
        activated = (pre * cdf).astype(BF)
        act[l, c] = activated
        slope[l, c] = cdf + pre * jnp.exp(-0.5 * pre * pre) * (1.0 / math.sqrt(2.0 * math.pi))
        if c == 0 and l == 0:
            ring_wait(DOWN0X)
            ring_wait(DOWN0Z)
        elif c == 0:
            ring_wait(DOWN1)
        rs_start(2 * l + 1, c, lambda h: dot_nt(activated, W[l, 2, h].reshape(640, PART)))

    def feed_rows(l, c):
        a = 2 * l + 1
        hidden = midrow[l, c] + rs_end(a, c) + vec(l, 5)
        if l == 0:
            xrow[1, c] = hidden
            unit, _ = norm_parts(hidden)
            hidden = unit * vec(1, 0) + vec(1, 2)
        ag_start(FB, 2 * l + 2, a, c, hidden)

    def feed_back(l, c):
        grad_act = dot_nn(BB[2 - 2 * l, c].reshape(ROWS, D), W[l, 2].reshape(D, PART))
        grad_pre = (grad_act * slope[l, c]).astype(BF)
        gpre[c] = grad_pre
        gb[2 + l : 3 + l, :] += jnp.sum(grad_pre.astype(F32), axis=0, keepdims=True)
        rs_start(6 - 2 * l, c, lambda h: dot_nt(grad_pre, W[l, 1, h].reshape(640, PART)))

    def feed_back_rows(l, c):
        a = 6 - 2 * l
        grad_norm = rs_end(a, c)
        unit, inv = norm_parts(midrow[l, c])
        gy = gyrow[c]
        grad_mid = gy + norm_back(grad_norm, vec(l, 1), unit, inv)
        gmidrow[c] = grad_mid
        ag_start(BB, 3 - 2 * l, a, c, grad_mid)
        GV[l, 1:2, 0:D] += jnp.sum(grad_norm * unit, axis=0, keepdims=True)
        GV[l, 3:4, 0:D] += jnp.sum(grad_norm, axis=0, keepdims=True)
        GV[l, 4:5, 0:D] += jnp.sum(grad_mid, axis=0, keepdims=True)
        GV[l, 5:6, 0:D] += jnp.sum(gy, axis=0, keepdims=True)

    def attend_back(l, c):
        wide = dot_nn(BB[3 - 2 * l, c].reshape(ROWS, D), W[l, 0, :, :, :, :, 384:640].reshape(D, 256))
        ga2 = split_heads(wide[:, 96:256]).astype(BF)
        q2, k, v = heads_of(l, c)
        probs = prob[l, c]
        grad_probs = dot_nt(ga2, v.astype(BF))
        grad_scores = probs * (grad_probs - jnp.sum(probs * grad_probs, axis=-1, keepdims=True))
        low = grad_scores.astype(BF)
        grad_v = dot_tn(probs.astype(BF), ga2)
        grad_k = dot_tn(low, q2) * SCALING
        pad = jnp.zeros((ROWS, 64), F32)
        gks[c] = jnp.concatenate([grad_k[ROWS:], grad_v[ROWS:], pad], axis=1).astype(BF)
        remote(gks.at[c], gkr.at[l, c], gs_s.at[c], gs_r.at[l, c], seq_dev).start()
        grad_q = (
            dot_nn(jnp.concatenate([low[0:ROWS], low[ROWS:]], axis=1), split_heads(k).astype(BF))
            * SCALING
        )
        gkeep[c, :, 0:160] = grad_q
        gkeep[c, :, 160:320] = grad_k[0:ROWS]
        gkeep[c, :, 320:480] = grad_v[0:ROWS]
        gkeep[c, :, 480:512] = jnp.zeros((ROWS, 32), F32)

    def project_back(l, c):
        wait_bytes(gkr.at[l, c], gs_r.at[l, c])
        wait_bytes(gkr.at[l, c], gs_s.at[c])
        far = gkr[l, c].astype(F32)
        gkeep[c, :, 160:480] += far[:, 0:320]
        grads = gkeep[c].astype(BF)
        gproj[c] = grads
        total = jnp.sum(grads.astype(F32), axis=0, keepdims=True)
        if l:
            gb[1:2, 0:512] += total
        else:
            for i in range(4):
                gq[i : i + 1, :] += total[:, 128 * i : 128 * i + 128]
        rs_start(7 - 2 * l, c, lambda h: dot_nt(grads, W[l, 0, h, :, :, :, 0:512].reshape(640, 512)))

    def project_back_rows(l, c):
        a = 7 - 2 * l
        grad_norm = rs_end(a, c)
        unit, inv = norm_parts(xrow[l, c])
        gy = gmidrow[c] + norm_back(grad_norm, vec(l, 0), unit, inv)
        gyrow[c] = gy
        ag_start(BB, 4 - 2 * l, a, c, gy)
        GV[l, 0:1, 0:D] += jnp.sum(grad_norm * unit, axis=0, keepdims=True)
        GV[l, 2:3, 0:D] += jnp.sum(grad_norm, axis=0, keepdims=True)

    def left_of(buf, i, m):
        return buf[i, :, :, :, :, 640 * m : 640 * m + 640].reshape(MICRO * ROWS, 640)

    def down_grad(l, m):
        right = act[l].reshape(MICRO * ROWS, PART)
        dW[l, 2, m] = dot_tn(left_of(BB, 2 - 2 * l, m), right).astype(BF).reshape(4, 2, SHARD, PART)

    def up_grad(l, m):
        right = gpre[...].reshape(MICRO * ROWS, PART)
        dW[l, 1, m] = dot_tn(left_of(FB, 2 * l + 1, m), right).astype(BF).reshape(4, 2, SHARD, PART)

    def out_grad(l, m):
        grad = dot_tn(left_of(BB, 3 - 2 * l, m), att[l].reshape(MICRO * ROWS, 256))
        dW[l, 0, m, :, :, :, 384:640] = grad.astype(BF).reshape(4, 2, SHARD, 256)

    def qkv_grad(l, m):
        grad = dot_tn(left_of(FB, 2 * l, m), gproj[...].reshape(MICRO * ROWS, 512))
        dW[l, 0, m, :, :, :, 0:384] = grad[:, 0:384].astype(BF).reshape(4, 2, SHARD, 384)
        rest = dW[l, 0, m, :, :, :, 384:512].astype(F32).reshape(640, 128) + grad[:, 384:512]
        dW[l, 0, m, :, :, :, 384:512] = rest.astype(BF).reshape(4, 2, SHARD, 128)

    @pl.loop(1, SHARDS)
    def _(k):
        remote(VG.at[me], VG.at[me], vs.at[0], vrs.at[0], shard_dev(k)[1]).start()

    gather_one(QKV0)
    gather_one(OUT0)
    pack(0, 1)
    pack(0, 2)
    V[...] = jnp.zeros_like(V)
    GV[...] = jnp.zeros_like(GV)
    gb[...] = jnp.zeros_like(gb)
    gq[...] = jnp.zeros_like(gq)
    bqkv[...] = jnp.zeros_like(bqkv)
    for l in range(2):
        bqkv[l, :, 0:160] = bqv_ref[l, 0:1, :].astype(F32)
        bqkv[l, :, 320:480] = bqv_ref[l, 1:2, :].astype(F32)
    gather_two(QKV0)
    wait_bytes(VG.at[pl.ds(0, SHARDS - 1)], vrs.at[0])
    wait_bytes(VG.at[pl.ds(0, SHARDS - 1)], vs.at[0])
    for i in range(SHARDS):
        low = SHARD * i // 128 * 128
        held = VG[i].astype(F32)
        V[0, :, low : low + 256] += held[0:8]
        V[1, :, low : low + 256] += held[8:16]
    cp_h.wait()
    cp_c.wait()
    gather_one(UP0)
    gather_one(DOWN0Z)
    gather_one(DOWN0X)
    for c in range(MICRO):
        whole = FB[0, c].reshape(ROWS, D).astype(F32)
        unit, _ = norm_parts(whole)
        xrow[0, c] = FB[0, c, y, core].astype(F32)
        FB[0, c] = (unit * vec(0, 0) + vec(0, 2)).astype(BF).reshape(4, 2, 16, D)
    gather_two(OUT0)
    ring_two(UP0)
    gather_wait(QKV0)

    def mask_grads():
        row = lax.broadcasted_iota(jnp.int32, (ROWS, 1), 0) + s * ROWS
        for c in range(MICRO):
            masked = jnp.where(row < len_ref[c], BB[0, c].reshape(ROWS, D).astype(F32), 0.0)
            BB[0, c] = masked.astype(BF).reshape(4, 2, 16, D)
            gyrow[c] = BB[0, c, y, core].astype(F32)

    def bias_sums():
        @pl.loop(1, SHARDS)
        def _(k):
            remote(gb, br.at[k - 1], es.at[1], er.at[1], shard_dev(k)[1]).start()

    def last_sums():
        @pl.loop(1, SHARDS)
        def _(k):
            remote(gq, bq.at[k - 1], es.at[3], er.at[3], shard_dev(k)[1]).start()

    def norm_sums():
        for i in range(11):
            GT[i, 0:8] = GV[0, :, 128 * i : 128 * i + 128]
            GT[i, 8:16] = GV[1, :, 128 * i : 128 * i + 128]

        @pl.loop(1, SHARDS)
        def _(k):
            j, dev = shard_dev(k)
            remote(GT.at[pl.ds(SHARD * j // 128, 2)], vr.at[k - 1], es.at[0], er.at[0], dev).start()

    cp_o = pltpu.make_async_copy(FB.at[4], out_ref, lsem.at[0])
    cp_g = pltpu.make_async_copy(BB.at[4], ingrad_ref, lsem.at[1])

    steps = []
    sums = {}
    for l in (0, 1):
        for c in range(MICRO):
            steps.append((partial(project, l, c), None))
        for c in range(MICRO):
            steps.append((partial(attend, l, c), (2 * l, c)))
            sums[2 * l, c] = (partial(attend_rows, l, c), FB, 2 * l + 1)
        for c in range(MICRO):
            steps.append((partial(feed, l, c), (2 * l + 1, c)))
            sums[2 * l + 1, c] = (partial(feed_rows, l, c), FB, 2 * l + 2)
    for l in (1, 0):
        a0, a1 = 6 - 2 * l, 7 - 2 * l
        for c in range(MICRO):
            steps.append((partial(feed_back, l, c), (a0, c)))
            sums[a0, c] = (partial(feed_back_rows, l, c), BB, 3 - 2 * l)
        for c in range(MICRO):
            steps.append((partial(attend_back, l, c), None))
        for c in range(MICRO):
            steps.append((partial(project_back, l, c), (a1, c)))
            sums[a1, c] = (partial(project_back_rows, l, c), BB, 4 - 2 * l)

    g1, g2, g3, g4 = gather_one, ring_two, ring_three, ring_wait
    d1, d2, d3 = reduce_one, reduce_two, reduce_three
    before = {
        2: [(g2, DOWN0X)],
        3: [(g2, DOWN0Z), (gather_wait, OUT0)],
        4: [(g3, UP0), (g1, PROJ1)],
        5: [(g3, DOWN0Z), (g3, DOWN0X)],
        6: [(g4, UP0), (g2, PROJ1), (g1, UP1)],
        8: [(g3, PROJ1), (g2, UP1), (g1, DOWN1)],
        9: [(g4, PROJ1)],
        10: [(g3, UP1), (g2, DOWN1)],
        12: [(g3, DOWN1)],
        15: [(g4, UP1)],
    }
    between = {
        3: [(pack, 1, 0)],
        4: [(pack, 1, 1)],
        5: [(pack, 1, 2)],
        6: [(mask_grads,)],
        18: [(down_grad, 1, 0)],
        20: [(up_grad, 1, 0)],
        24: [(out_grad, 1, 0), (out_grad, 1, 1), (d1, 1, OUT)],
        25: [(d2, 1, UP)],
        26: [(qkv_grad, 1, 0)],
        27: [(d2, 1, OUT)],
        29: [(down_grad, 0, 0)],
        30: [(up_grad, 0, 0)],
        31: [(up_grad, 0, 1), (d1, 0, UP), (bias_sums,)],
        33: [(out_grad, 0, 0), (out_grad, 0, 1), (d1, 0, OUT)],
        34: [(d2, 0, DOWN)],
        35: [(qkv_grad, 0, 0), (qkv_grad, 0, 1), (d1, 0, QKV), (last_sums,)],
        36: [(d2, 0, OUT)],
    }
    later = {
        18: [(down_grad, 1, 1), (d1, 1, DOWN)],
        20: [(up_grad, 1, 1), (d1, 1, UP)],
        24: [(d2, 1, DOWN)],
        26: [(qkv_grad, 1, 1), (d1, 1, QKV)],
        27: [(d3, 1, DOWN)],
        28: [(d3, 1, UP)],
        29: [(down_grad, 0, 1), (d1, 0, DOWN)],
        33: [(d2, 1, QKV)],
        34: [(d2, 0, UP), (d3, 1, OUT)],
    }
    for n in range(len(steps) + 2):
        for fn, *where in before.get(n, ()):
            fn(*where)
        if n < len(steps):
            steps[n][0]()
        for fn, *where in between.get(n, ()):
            fn(*where)
        if n < len(steps) and steps[n][1] is not None:
            rs_mid(*steps[n][1])
        if 1 <= n <= len(steps) and steps[n - 1][1] is not None:
            sums[steps[n - 1][1]][0]()
        if n == len(steps):
            norm_sums()
        if n >= 2 and steps[n - 2][1] is not None:
            a, c = steps[n - 2][1]
            ag_mid(sums[a, c][1], sums[a, c][2], a, c)
        for fn, *where in later.get(n, ()):
            fn(*where)
        if n >= 2 and steps[n - 2][1] is not None:
            ag_end(*steps[n - 2][1])
        if n == 19:
            cp_o.start()

    cp_g.start()
    for l, i in ((1, QKV), (0, DOWN), (0, UP)):
        reduce_three(l, i)
    wait_bytes(vr, er.at[0])
    wait_bytes(vr, es.at[0])
    own = GT[pl.ds(SHARD * me // 128, 2)]
    for k in range(SHARDS - 1):
        own = own + vr[k]
    vr2[7] = own

    @pl.loop(1, 8)
    def _(k):
        remote(vr2.at[7], vr2.at[k - 1], es.at[2], er.at[2], (f, s, (t + k) % 8)).start()

    wait_bytes(br, er.at[1])
    wait_bytes(br, es.at[1])
    wait_bytes(bq, er.at[3])
    wait_bytes(bq, es.at[3])
    totals = gb[...]
    lasts = gq[...]
    for k in range(SHARDS - 1):
        totals = totals + br[k]
        lasts = lasts + bq[k]
    bsum_ref[...] = totals
    for i in range(4):
        bsum_ref[0:1, 128 * i : 128 * i + 128] = lasts[i : i + 1]
    reduce_two(0, QKV)
    for l, i in ((0, OUT),):
        reduce_three(l, i)
    wait_bytes(vr2.at[pl.ds(0, 7)], er.at[2])
    wait_bytes(vr2.at[pl.ds(0, 7)], es.at[2])
    own = vr2[7]
    for k in range(7):
        own = own + vr2[k]
    vsum_ref[...] = own
    reduce_three(0, QKV)
    for l in range(2):
        for i in range(4):
            p, ways = piece(l, i)
            for way, cols in ways:
                pltpu.make_async_copy(dwo.at[l, p, :, cols], dwo_ref.at[l, p, :, cols], osem.at[l, i, way]).wait()
    cp_o.wait()
    cp_g.wait()


def finish(
    out_ref, ingrad_ref, dwo_ref, vsum_ref, bsum_ref,
    hidden_ref, grad_ref, gqkv_ref, gqv_ref, gout_ref, gbout_ref, gup_ref, gbup_ref, gdown_ref, gbdown_ref,
    ggain_ref, gshift_ref,
):
    me = lax.axis_index("fsdp") * 2 + lax.axis_index("seq")
    hidden_ref[...] = out_ref[...].astype(F32)
    grad_ref[...] = ingrad_ref[...].astype(F32)
    rows = jnp.concatenate([vsum_ref[0], vsum_ref[1]], axis=1)
    rows = pltpu.roll(rows, (256 - (SHARD * me) % 128) % 256, 1)
    for l in range(2):
        proj = dwo_ref[l, 0]
        for i in range(3):
            gqkv_ref[l, i] = proj[:, 160 * i : 160 * i + 160]
        gout_ref[l] = proj[:, 480:640].T
        gup_ref[l] = dwo_ref[l, 1]
        gdown_ref[l] = dwo_ref[l, 2]
        gqv_ref[l, 0:1, :] = bsum_ref[l : l + 1, 0:160]
        gqv_ref[l, 1:2, :] = bsum_ref[l : l + 1, 320:480]
        gbup_ref[l : l + 1, :] = bsum_ref[2 + l : 3 + l, :]
        ggain_ref[l] = rows[8 * l : 8 * l + 2, 0:SHARD]
        gshift_ref[l] = rows[8 * l + 2 : 8 * l + 4, 0:SHARD]
        gbout_ref[l : l + 1, :] = rows[8 * l + 4 : 8 * l + 5, 0:SHARD]
        gbdown_ref[l : l + 1, :] = rows[8 * l + 5 : 8 * l + 6, 0:SHARD]


def body(
    hidden_in, cotangent, lengths, qkv_weight, qv_bias, out_weight, out_bias,
    up_weight, up_bias, down_weight, down_bias, ln_gain, ln_bias,
):
    vmem = pl.BlockSpec(memory_space=pltpu.VMEM)
    anys = pl.BlockSpec(memory_space=pl.ANY)
    smem = pl.BlockSpec(memory_space=pltpu.SMEM)
    dma = pltpu.SemaphoreType.DMA
    blocks = (MICRO, 4, 2, 16, D)
    scratch = [
        pltpu.VMEM((2, 3, 2, 4, 2, SHARD, PART), BF),
        pltpu.VMEM((2, 3, 2, 4, 2, SHARD, PART), BF),
        pltpu.VMEM((2, 3, 3, 4, SHARD, 384), BF),
        pltpu.VMEM((2, 3, 3, 2, 2, SHARD, 384), BF),
        pltpu.VMEM((2, 3, 3, SHARD, PART), BF),
        pltpu.VMEM((5,) + blocks, BF),
        pltpu.VMEM((5,) + blocks, BF),
        pltpu.VMEM((8, MICRO, 4, 16, D), BF),
        pltpu.VMEM((8, MICRO, 3, 16, D), BF),
        pltpu.VMEM(blocks, BF),
        pltpu.VMEM((MICRO, 4, 16, D), BF),
        pltpu.VMEM((2, MICRO, ROWS, 512), BF),
        pltpu.VMEM((2, MICRO, ROWS, 384), BF),
        pltpu.VMEM((2, MICRO, 2 * ROWS, 2 * ROWS), F32),
        pltpu.VMEM((2, MICRO, ROWS, 256), BF),
        pltpu.VMEM((2, MICRO, 16, D), F32),
        pltpu.VMEM((2, MICRO, 16, D), F32),
        pltpu.VMEM((2, MICRO, ROWS, PART), F32),
        pltpu.VMEM((2, MICRO, ROWS, PART), BF),
        pltpu.VMEM((MICRO, ROWS, PART), BF),
        pltpu.VMEM((MICRO, ROWS, 512), F32),
        pltpu.VMEM((MICRO, ROWS, 512), BF),
        pltpu.VMEM((MICRO, ROWS, 384), BF),
        pltpu.VMEM((2, MICRO, ROWS, 384), BF),
        pltpu.VMEM((MICRO, 16, D), F32),
        pltpu.VMEM((MICRO, 16, D), F32),
        pltpu.VMEM((SHARDS, 16, 256), BF),
        pltpu.VMEM((2, 8, 1408), F32),
        pltpu.VMEM((2, 8, 1408), F32),
        pltpu.VMEM((11, 16, 128), F32),
        pltpu.VMEM((SHARDS - 1, 2, 16, 128), F32),
        pltpu.VMEM((8, 2, 16, 128), F32),
        pltpu.VMEM((8, PART), F32),
        pltpu.VMEM((SHARDS - 1, 8, PART), F32),
        pltpu.VMEM((8, 128), F32),
        pltpu.VMEM((SHARDS - 1, 8, 128), F32),
        pltpu.VMEM((16, 256), F32),
        pltpu.VMEM((2, 1, 512), F32),
        pltpu.VMEM((2, 3, SHARD, PART), F32),
        dma((8, 2)), dma((8, 2)), dma((8, 2)), dma((8, 2)), dma((8, 2)), dma((8, 2)),
        dma((2, 4, 2)), dma((2, 4, 2)), dma((2, 4, 2)), dma((2, 4, 2)),
        dma((MICRO, 2)), dma((8, MICRO, 2)), dma((MICRO,)), dma((8, MICRO)),
        dma((MICRO,)), dma((8, MICRO)), dma((MICRO,)), dma((8, MICRO)),
        dma((2, MICRO)), dma((2, MICRO)), dma((MICRO,)), dma((2, MICRO)),
        dma((1,)), dma((1,)), dma((4,)), dma((4,)), dma((2,)), dma((2, 2)), dma((2, 4, 2)),
    ]
    out, ingrad, dwo, vsum, bsum = pl.pallas_call(
        kernel,
        name="encoder",
        out_shape=(
            jax.ShapeDtypeStruct(blocks, BF),
            jax.ShapeDtypeStruct(blocks, BF),
            jax.ShapeDtypeStruct((2, 3, SHARD, PART), F32),
            jax.ShapeDtypeStruct((2, 16, 128), F32),
            jax.ShapeDtypeStruct((8, PART), F32),
        ),
        in_specs=[anys, anys, smem, vmem, vmem, vmem, vmem, anys, vmem, anys, vmem, vmem, vmem],
        out_specs=(anys, anys, anys, vmem, vmem),
        scratch_shapes=scratch,
        compiler_params=pltpu.CompilerParams(
            collective_id=0, has_side_effects=True, vmem_limit_bytes=63 * 1024 * 1024
        ),
    )(
        hidden_in.reshape(blocks), cotangent.reshape(blocks), lengths, qkv_weight, qv_bias, out_weight,
        out_bias, up_weight, up_bias, jnp.swapaxes(down_weight, 1, 2), down_bias, ln_gain, ln_bias,
    )
    rows = (MICRO, ROWS, D)
    shapes = (
        rows, rows, (2, 3, SHARD, 160), (2, 2, 160), (2, 160, SHARD), (2, SHARD), (2, SHARD, PART),
        (2, PART), (2, SHARD, PART), (2, SHARD), (2, 2, SHARD), (2, 2, SHARD),
    )
    outs = pl.pallas_call(
        finish,
        name="finish",
        out_shape=tuple(jax.ShapeDtypeStruct(shape, F32) for shape in shapes),
        in_specs=[vmem] * 5,
        out_specs=(vmem,) * 12,
        compiler_params=pltpu.CompilerParams(vmem_limit_bytes=63 * 1024 * 1024),
    )(out.reshape(rows), ingrad.reshape(rows), dwo, vsum, bsum)
    return outs[:8] + (jnp.swapaxes(outs[8], 1, 2),) + outs[9:]


def solution(mesh):
    placed = (
        P("fsdp", "seq", None),
        P("fsdp", "seq", None),
        P("fsdp"),
        P(None, None, ("fsdp", "seq"), "tp"),
        P(None, None, "tp"),
        P(None, "tp", ("fsdp", "seq")),
        P(None, ("fsdp", "seq")),
        P(None, ("fsdp", "seq"), "tp"),
        P(None, "tp"),
        P(None, "tp", ("fsdp", "seq")),
        P(None, ("fsdp", "seq")),
        P(None, None, ("fsdp", "seq")),
        P(None, None, ("fsdp", "seq")),
    )
    return jax.shard_map(
        body,
        mesh=mesh,
        in_specs=placed,
        out_specs=(
            P("fsdp", "seq", None),
            P("fsdp", "seq", None),
            P(None, None, ("fsdp", "seq"), "tp"),
            P(None, None, "tp"),
            P(None, "tp", ("fsdp", "seq")),
            P(None, ("fsdp", "seq")),
            P(None, ("fsdp", "seq"), "tp"),
            P(None, "tp"),
            P(None, "tp", ("fsdp", "seq")),
            P(None, ("fsdp", "seq")),
            P(None, None, ("fsdp", "seq")),
            P(None, None, ("fsdp", "seq")),
        ),
        check_vma=False,
    )
```

```python
from functools import partial
import math

import jax
import jax.numpy as jnp
from jax import lax
from jax.experimental import pallas as pl
from jax.experimental.pallas import tpu as pltpu
from jax.sharding import PartitionSpec as P

HD = 80
EPSILON = 1e-05
MASKED = -1000000000.0
MESH = pl.DeviceIdType.MESH
BF = jnp.bfloat16
F32 = jnp.float32
SCALING = 1.0 / math.sqrt(HD)

D = 1280
MICRO = 3
ROWS = 128
PART = 640
SHARDS = 16
SHARD = 80

PIECES = (
    (0, (256, 512), (0, 256)),
    (0, (512, 640), None),
    (1, (384, 640), (0, 384)),
    (2, (384, 640), (0, 384)),
)
QKV, OUT, UP, DOWN = range(4)
LOADS = (
    (0, 0, (256, 512), (0, 256)),
    (0, 0, (512, 640), None),
    (0, 1, None, (0, 640)),
    (0, 2, (0, 256), None),
    (0, 2, None, (256, 640)),
    (1, 0, (384, 640), (0, 384)),
    (1, 1, (384, 640), (0, 384)),
    (1, 2, (384, 640), (0, 384)),
)
QKV0, OUT0, UP0, DOWN0X, DOWN0Z, PROJ1, UP1, DOWN1 = range(8)


def dot_nn(a, b):
    return lax.dot_general(a, b, (((1,), (0,)), ((), ())), preferred_element_type=F32)


def dot_nt(a, b):
    return lax.dot_general(a, b, (((1,), (1,)), ((), ())), preferred_element_type=F32)


def dot_tn(a, b):
    return lax.dot_general(a, b, (((0,), (0,)), ((), ())), preferred_element_type=F32)


def norm_parts(values):
    row_mean = jnp.mean(values, axis=-1, keepdims=True)
    centred = values - row_mean
    row_var = jnp.mean(centred * centred, axis=-1, keepdims=True)
    inv = lax.rsqrt(row_var + EPSILON)
    return centred * inv, inv


def norm_back(grad, gain, unit, inv):
    scaled = grad * gain
    return inv * (
        scaled
        - jnp.mean(scaled, axis=-1, keepdims=True)
        - unit * jnp.mean(scaled * unit, axis=-1, keepdims=True)
    )


def split_heads(x):
    first = lax.broadcasted_iota(jnp.int32, x.shape, 1) < HD
    return jnp.concatenate([jnp.where(first, x, 0.0), jnp.where(first, 0.0, x)], axis=0)


def kernel(
    hid_ref, cot_ref, len_ref, wqkv_ref, bqv_ref, wout_ref, bout_ref, wup_ref, bup_ref, wdown_ref, bdown_ref,
    gain_ref, shift_ref,
    out_ref, ingrad_ref, dwo_ref, vsum_ref, bsum_ref,
    W, dW, rb1, rb2, rc, FB, BB, dr, yr, part, sb,
    qkv, kvo, prob, att, xrow, midrow, slope, act,
    gpre, gkeep, gproj, gks, gkr, gyrow, gmidrow,
    VG, V, GV, GT, vr, vr2, gb, br, gq, bq, vrow, bqkv, dwo,
    g1s, g1r, g2s, g2r, g3s, g3r, q1s, q1r, q2s, q2r,
    s1, r1, s2, r2, s3, r3, s4, r4, ks, kr, gs_s, gs_r, vs, vrs, es, er, lsem, wsem, osem,
):
    f, s, t = lax.axis_index("fsdp"), lax.axis_index("seq"), lax.axis_index("tp")
    me = f * 2 + s
    xh, z = f // 4, f % 4
    x = xh * 2 + s
    y, core = t // 2, t % 2
    other = 1 - core

    def shard_dev(k):
        j = (me + k) % SHARDS
        return j, (j // 2, j % 2, t)

    def x_dev(k):
        j = (x + k) % 4
        return j // 2, j % 2, ((j // 2) * 4 + z, j % 2, t)

    def z_dev(k):
        j = (z + k) % 4
        return j, (xh * 4 + j, s, t)

    def y_dev(k):
        j = (y + k) % 4
        return j, (f, s, j * 2 + core)

    core_dev = (f, s, y * 2 + other)
    seq_dev = (f, 1 - s, t)

    def remote(src, dst, ss, rs, dev):
        return pltpu.make_async_remote_copy(
            src_ref=src, dst_ref=dst, send_sem=ss, recv_sem=rs, device_id=dev, device_id_type=MESH
        )

    def wait_bytes(ref, sem):
        pltpu.make_async_copy(ref, ref, sem).wait()

    cp_h = pltpu.make_async_copy(hid_ref, FB.at[0], lsem.at[0])
    cp_c = pltpu.make_async_copy(cot_ref, BB.at[0], lsem.at[1])
    cp_h.start()
    cp_c.start()

    for l in range(2):
        for p in range(2):
            pltpu.make_async_copy((wup_ref, wdown_ref)[p].at[l], W.at[l, p + 1, xh, z, s], wsem.at[l, p]).start()

    barrier = pltpu.get_barrier_semaphore()

    @pl.loop(1, SHARDS)
    def _(k):
        pl.semaphore_signal(barrier, inc=1, device_id=shard_dev(k)[1], device_id_type=MESH)

    @pl.loop(1, 8)
    def _(k):
        pl.semaphore_signal(barrier, inc=1, device_id=(f, s, (t + k) % 8), device_id_type=MESH)

    def pack(l, p):
        if p == 0:
            parts = [wqkv_ref[l, i].astype(F32) for i in range(3)] + [wout_ref[l].astype(F32).T]
            W[l, 0, xh, z, s] = jnp.concatenate(parts, axis=1).astype(BF)
        else:
            pltpu.make_async_copy((wup_ref, wdown_ref)[p - 1].at[l], W.at[l, p, xh, z, s], wsem.at[l, p - 1]).wait()

    vrow[...] = jnp.zeros_like(vrow)
    for l in range(2):
        for r in range(2):
            vrow[8 * l + r : 8 * l + r + 1, 0:SHARD] = gain_ref[l, r : r + 1, :].astype(F32)
            vrow[8 * l + 2 + r : 8 * l + 3 + r, 0:SHARD] = shift_ref[l, r : r + 1, :].astype(F32)
        vrow[8 * l + 4 : 8 * l + 5, 0:SHARD] = bout_ref[l : l + 1, :].astype(F32)
        vrow[8 * l + 5 : 8 * l + 6, 0:SHARD] = bdown_ref[l : l + 1, :].astype(F32)
    VG[me] = pltpu.roll(vrow[...], (SHARD * me) % 128, 1).astype(BF)
    pack(0, 0)
    pl.semaphore_wait(barrier, 22)

    def load(n):
        l, p, one, two = LOADS[n]
        ways = ([(0, slice(*one))] if one else []) + ([(1, slice(*two))] if two else [])
        return l, p, ways

    def gather_one(n):
        l, p, ways = load(n)
        for way, cols in ways:
            own = W.at[l, p, xh, z, s, :, cols]
            for k in range(1, 4):
                dev = x_dev(k)[2] if way else z_dev(k)[1]
                remote(own, own, g1s.at[n, way], g1r.at[n, way], dev).start()

    def gather_mid(n):
        l, p, ways = load(n)
        for way, cols in ways:
            three = W.at[l, p, 0, pl.ds(0, 3), 0, :, cols]
            wait_bytes(three, g1r.at[n, way])
            wait_bytes(three, g1s.at[n, way])

    def gather_two(n):
        l, p, ways = load(n)
        gather_mid(n)
        for way, cols in ways:
            four = W.at[l, p, :, z, :, :, cols] if way else W.at[l, p, xh, :, s, :, cols]
            for k in range(1, 4):
                dev = z_dev(k)[1] if way else x_dev(k)[2]
                remote(four, four, g2s.at[n, way], g2r.at[n, way], dev).start()

    def gather_wait(n):
        l, p, ways = load(n)
        for way, cols in ways:
            twelve = W.at[l, p, :, pl.ds(0, 3), :, :, cols]
            wait_bytes(twelve, g2r.at[n, way])
            wait_bytes(twelve, g2s.at[n, way])

    def ring_dev(way, k):
        return z_dev(k)[1] if way else x_dev(k)[2]

    def ring_two(n):
        l, p, ways = load(n)
        gather_mid(n)
        for way, cols in ways:
            four = W.at[l, p, :, z, :, :, cols] if way else W.at[l, p, xh, :, s, :, cols]
            for k in (1, 3):
                remote(four, four, g2s.at[n, way], g2r.at[n, way], ring_dev(way, k)).start()

    def ring_mid(n):
        l, p, ways = load(n)
        for way, cols in ways:
            eight = W.at[l, p, 0, :, :, :, cols]
            wait_bytes(eight, g2r.at[n, way])
            wait_bytes(eight, g2s.at[n, way])

    def ring_three(n):
        l, p, ways = load(n)
        ring_mid(n)
        for way, cols in ways:
            if way:
                left = W.at[l, p, 0, (z + 3) % 4, :, :, cols]
                right = W.at[l, p, 1, (z + 1) % 4, :, :, cols]
            else:
                il, ir = (x + 3) % 4, (x + 1) % 4
                left = W.at[l, p, il // 2, pl.ds(0, 2), il % 2, :, cols]
                right = W.at[l, p, ir // 2, pl.ds(2, 2), ir % 2, :, cols]
            remote(left, left, g3s.at[n, way], g3r.at[n, way], ring_dev(way, 1)).start()
            remote(right, right, g3s.at[n, way], g3r.at[n, way], ring_dev(way, 3)).start()

    def ring_wait(n):
        l, p, ways = load(n)
        for way, cols in ways:
            four = W.at[l, p, 0, pl.ds(0, 2), :, :, cols]
            wait_bytes(four, g3r.at[n, way])
            wait_bytes(four, g3s.at[n, way])

    def piece(l, i):
        part_idx, one, two = PIECES[i]
        both = [(0, slice(*one))] + ([(1, slice(*two))] if two else [])
        return part_idx, both

    def reduce_one(l, i):
        p, ways = piece(l, i)
        for way, cols in ways:
            for k in range(1, 4):
                if way:
                    j, dev = z_dev(k)
                    four = dW.at[l, p, :, j, :, :, cols]
                    buf = rb2.at[l, p, k - 1, :, :, :, 0 : cols.stop - cols.start]
                else:
                    jh, jl, dev = x_dev(k)
                    four = dW.at[l, p, jh, :, jl, :, cols]
                    buf = rb1.at[l, p, k - 1, :, :, cols.start - 256 : cols.stop - 256]
                remote(four, buf, q1s.at[l, i, way], q1r.at[l, i, way], dev).start()

    def reduce_mid(l, i):
        p, ways = piece(l, i)
        for way, cols in ways:
            twelve = dW.at[l, p, :, pl.ds(0, 3), :, :, cols]
            wait_bytes(twelve, q1r.at[l, i, way])
            wait_bytes(twelve, q1s.at[l, i, way])

    def reduce_two(l, i):
        p, ways = piece(l, i)
        reduce_mid(l, i)

        @pl.loop(0, 4)
        def _(n):
            nh, nl = n // 2, n % 2
            for way, cols in ways:
                if way:
                    total = dW[l, p, nh, z, nl, :, cols].astype(F32)
                    for k in range(3):
                        total = total + rb2[l, p, k, nh, nl, :, 0 : cols.stop - cols.start].astype(F32)
                    dW[l, p, nh, z, nl, :, cols] = total.astype(BF)
                else:
                    total = dW[l, p, xh, n, s, :, cols].astype(F32)
                    for k in range(3):
                        total = total + rb1[l, p, k, n, :, cols.start - 256 : cols.stop - 256].astype(F32)
                    dW[l, p, xh, n, s, :, cols] = total.astype(BF)

        for way, cols in ways:
            for k in range(1, 4):
                if way:
                    jh, jl, dev = x_dev(k)
                    one = dW.at[l, p, jh, z, jl, :, cols]
                else:
                    j, dev = z_dev(k)
                    one = dW.at[l, p, xh, j, s, :, cols]
                remote(one, rc.at[l, p, k - 1, :, cols], q2s.at[l, i, way], q2r.at[l, i, way], dev).start()

    def reduce_last(l, i):
        p, ways = piece(l, i)
        for way, cols in ways:
            three = dW.at[l, p, 0, pl.ds(0, 3), 0, :, cols]
            wait_bytes(three, q2r.at[l, i, way])
            wait_bytes(three, q2s.at[l, i, way])

    def reduce_three(l, i):
        p, ways = piece(l, i)
        reduce_last(l, i)
        for way, cols in ways:
            total = dW[l, p, xh, z, s, :, cols].astype(F32)
            for k in range(3):
                total = total + rc[l, p, k, :, cols].astype(F32)
            dwo[l, p, :, cols] = total
            own = dwo.at[l, p, :, cols]
            pltpu.make_async_copy(own, dwo_ref.at[l, p, :, cols], osem.at[l, i, way]).start()

    def vec(l, r):
        return V[l, r : r + 1, 0:D]

    def rs_start(a, c, value_of):
        for h in range(2):
            lanes = slice(640 * h, 640 * h + 640)
            part[c, :, :, :, lanes] = value_of(h).astype(BF).reshape(4, 2, 16, 640)
            remote(
                part.at[c, :, other, :, lanes], dr.at[a, c, :, :, lanes], s1.at[c, h], r1.at[a, c, h], core_dev
            ).start()

    def rs_mid(a, c):
        for h in range(2):
            lanes = slice(640 * h, 640 * h + 640)
            half = dr.at[a, c, :, :, lanes]
            wait_bytes(half, r1.at[a, c, h])
            wait_bytes(half, s1.at[c, h])
            sb[c, :, :, lanes] = (
                part[c, :, core, :, lanes].astype(F32) + dr[a, c, :, :, lanes].astype(F32)
            ).astype(BF)
            for k in (2, 1, 3):
                j, dev = y_dev(k)
                remote(
                    sb.at[c, j, :, lanes], yr.at[a, c, k - 1, :, lanes], s2.at[c], r2.at[a, c], dev
                ).start()

    def rs_end(a, c):
        wait_bytes(yr.at[a, c], r2.at[a, c])
        wait_bytes(yr.at[a, c], s2.at[c])
        total = sb[c, y].astype(F32)
        for k in range(3):
            total = total + yr[a, c, k].astype(F32)
        return total

    def ag_start(buf, i, a, c, value):
        buf[i, c, y, core] = value.astype(BF)
        for k in (2, 1, 3):
            _, dev = y_dev(k)
            remote(buf.at[i, c, y, core], buf.at[i, c, y, core], s3.at[c], r3.at[a, c], dev).start()

    def ag_mid(buf, i, a, c):
        wait_bytes(yr.at[a, c], r3.at[a, c])
        wait_bytes(yr.at[a, c], s3.at[c])
        remote(buf.at[i, c, :, core], buf.at[i, c, :, core], s4.at[c], r4.at[a, c], core_dev).start()

    def ag_end(a, c):
        wait_bytes(dr.at[a, c], r4.at[a, c])
        wait_bytes(dr.at[a, c], s4.at[c])

    def heads_of(l, c):
        own = qkv[l, c].astype(F32)
        far = kvo[l, c].astype(F32)
        q = own[:, 0:160]
        k = jnp.concatenate([own[:, 160:320], far[:, 32:192]], axis=0)
        v = jnp.concatenate([own[:, 320:480], far[:, 192:352]], axis=0)
        return split_heads(q).astype(BF), k, v

    def project(l, c):
        normed = FB[2 * l, c].reshape(ROWS, D)
        proj = dot_nn(normed, W[l, 0, :, :, :, :, 0:512].reshape(D, 512)) + bqkv[l]
        qkv[l, c] = proj.astype(BF)
        remote(qkv.at[l, c, :, 128:512], kvo.at[l, c], ks.at[l, c], kr.at[l, c], seq_dev).start()

    def attend(l, c):
        wait_bytes(kvo.at[l, c], kr.at[l, c])
        wait_bytes(kvo.at[l, c], ks.at[l, c])
        q2, k, v = heads_of(l, c)
        scores = dot_nt(q2, k.astype(BF)) * SCALING
        slot = lax.broadcasted_iota(jnp.int32, (1, 2 * ROWS), 1)
        slot = jnp.where(slot < ROWS, slot + s * ROWS, slot - s * ROWS)
        scores = jnp.where(slot < len_ref[c], scores, MASKED)
        top = jnp.max(scores, axis=-1, keepdims=True)
        powers = jnp.exp(scores - top)
        probs = powers / jnp.sum(powers, axis=-1, keepdims=True)
        prob[l, c] = probs
        low = probs.astype(BF)
        attended = dot_nn(
            jnp.concatenate([low[0:ROWS], low[ROWS:]], axis=1), split_heads(v).astype(BF)
        )
        wide = jnp.concatenate([jnp.zeros((ROWS, 96), F32), attended], axis=1).astype(BF)
        att[l, c] = wide
        rs_start(2 * l, c, lambda h: dot_nt(wide, W[l, 0, h, :, :, :, 384:640].reshape(640, 256)))

    def attend_rows(l, c):
        a = 2 * l
        middle = xrow[l, c] + rs_end(a, c) + vec(l, 4)
        midrow[l, c] = middle
        unit, _ = norm_parts(middle)
        ag_start(FB, 2 * l + 1, a, c, unit * vec(l, 1) + vec(l, 3))

    def feed(l, c):
        normed = FB[2 * l + 1, c].reshape(ROWS, D)
        pre = dot_nn(normed, W[l, 1].reshape(D, PART)) + bup_ref[l : l + 1, :].astype(F32)
        cdf = 0.5 * (1.0 + lax.erf(pre * math.sqrt(0.5)))
        activated = (pre * cdf).astype(BF)
        act[l, c] = activated
        slope[l, c] = cdf + pre * jnp.exp(-0.5 * pre * pre) * (1.0 / math.sqrt(2.0 * math.pi))
        if c == 0 and l == 0:
            ring_wait(DOWN0X)
            ring_wait(DOWN0Z)
        elif c == 0:
            ring_wait(DOWN1)
        rs_start(2 * l + 1, c, lambda h: dot_nt(activated, W[l, 2, h].reshape(640, PART)))

    def feed_rows(l, c):
        a = 2 * l + 1
        hidden = midrow[l, c] + rs_end(a, c) + vec(l, 5)
        if l == 0:
            xrow[1, c] = hidden
            unit, _ = norm_parts(hidden)
            hidden = unit * vec(1, 0) + vec(1, 2)
        ag_start(FB, 2 * l + 2, a, c, hidden)

    def feed_back(l, c):
        grad_act = dot_nn(BB[2 - 2 * l, c].reshape(ROWS, D), W[l, 2].reshape(D, PART))
        grad_pre = (grad_act * slope[l, c]).astype(BF)
        gpre[c] = grad_pre
        gb[2 + l : 3 + l, :] += jnp.sum(grad_pre.astype(F32), axis=0, keepdims=True)
        rs_start(6 - 2 * l, c, lambda h: dot_nt(grad_pre, W[l, 1, h].reshape(640, PART)))

    def feed_back_rows(l, c):
        a = 6 - 2 * l
        grad_norm = rs_end(a, c)
        unit, inv = norm_parts(midrow[l, c])
        gy = gyrow[c]
        grad_mid = gy + norm_back(grad_norm, vec(l, 1), unit, inv)
        gmidrow[c] = grad_mid
        ag_start(BB, 3 - 2 * l, a, c, grad_mid)
        GV[l, 1:2, 0:D] += jnp.sum(grad_norm * unit, axis=0, keepdims=True)
        GV[l, 3:4, 0:D] += jnp.sum(grad_norm, axis=0, keepdims=True)
        GV[l, 4:5, 0:D] += jnp.sum(grad_mid, axis=0, keepdims=True)
        GV[l, 5:6, 0:D] += jnp.sum(gy, axis=0, keepdims=True)

    def attend_back(l, c):
        wide = dot_nn(BB[3 - 2 * l, c].reshape(ROWS, D), W[l, 0, :, :, :, :, 384:640].reshape(D, 256))
        ga2 = split_heads(wide[:, 96:256]).astype(BF)
        q2, k, v = heads_of(l, c)
        probs = prob[l, c]
        grad_probs = dot_nt(ga2, v.astype(BF))
        grad_scores = probs * (grad_probs - jnp.sum(probs * grad_probs, axis=-1, keepdims=True))
        low = grad_scores.astype(BF)
        grad_v = dot_tn(probs.astype(BF), ga2)
        grad_k = dot_tn(low, q2) * SCALING
        pad = jnp.zeros((ROWS, 64), F32)
        gks[c] = jnp.concatenate([grad_k[ROWS:], grad_v[ROWS:], pad], axis=1).astype(BF)
        remote(gks.at[c], gkr.at[l, c], gs_s.at[c], gs_r.at[l, c], seq_dev).start()
        grad_q = (
            dot_nn(jnp.concatenate([low[0:ROWS], low[ROWS:]], axis=1), split_heads(k).astype(BF))
            * SCALING
        )
        gkeep[c, :, 0:160] = grad_q
        gkeep[c, :, 160:320] = grad_k[0:ROWS]
        gkeep[c, :, 320:480] = grad_v[0:ROWS]
        gkeep[c, :, 480:512] = jnp.zeros((ROWS, 32), F32)

    def project_back(l, c):
        wait_bytes(gkr.at[l, c], gs_r.at[l, c])
        wait_bytes(gkr.at[l, c], gs_s.at[c])
        far = gkr[l, c].astype(F32)
        gkeep[c, :, 160:480] += far[:, 0:320]
        grads = gkeep[c].astype(BF)
        gproj[c] = grads
        total = jnp.sum(grads.astype(F32), axis=0, keepdims=True)
        if l:
            gb[1:2, 0:512] += total
        else:
            for i in range(4):
                gq[i : i + 1, :] += total[:, 128 * i : 128 * i + 128]
        rs_start(7 - 2 * l, c, lambda h: dot_nt(grads, W[l, 0, h, :, :, :, 0:512].reshape(640, 512)))

    def project_back_rows(l, c):
        a = 7 - 2 * l
        grad_norm = rs_end(a, c)
        unit, inv = norm_parts(xrow[l, c])
        gy = gmidrow[c] + norm_back(grad_norm, vec(l, 0), unit, inv)
        gyrow[c] = gy
        ag_start(BB, 4 - 2 * l, a, c, gy)
        GV[l, 0:1, 0:D] += jnp.sum(grad_norm * unit, axis=0, keepdims=True)
        GV[l, 2:3, 0:D] += jnp.sum(grad_norm, axis=0, keepdims=True)

    def left_of(buf, i, m):
        lanes = pl.ds(pl.multiple_of(m * 640, 128), 640)
        return buf[i, :, :, :, :, lanes].reshape(MICRO * ROWS, 640)

    def down_grad(l):
        @pl.loop(0, 2)
        def _(m):
            right = act[l].reshape(MICRO * ROWS, PART)
            dW[l, 2, m] = dot_tn(left_of(BB, 2 - 2 * l, m), right).astype(BF).reshape(4, 2, SHARD, PART)

    def up_grad(l):
        @pl.loop(0, 2)
        def _(m):
            right = gpre[...].reshape(MICRO * ROWS, PART)
            dW[l, 1, m] = dot_tn(left_of(FB, 2 * l + 1, m), right).astype(BF).reshape(4, 2, SHARD, PART)

    def out_grad(l):
        @pl.loop(0, 2)
        def _(m):
            grad = dot_tn(left_of(BB, 3 - 2 * l, m), att[l].reshape(MICRO * ROWS, 256))
            dW[l, 0, m, :, :, :, 384:640] = grad.astype(BF).reshape(4, 2, SHARD, 256)

    def qkv_grad(l):
        @pl.loop(0, 2)
        def _(m):
            grad = dot_tn(left_of(FB, 2 * l, m), gproj[...].reshape(MICRO * ROWS, 512))
            dW[l, 0, m, :, :, :, 0:384] = grad[:, 0:384].astype(BF).reshape(4, 2, SHARD, 384)
            rest = dW[l, 0, m, :, :, :, 384:512].astype(F32).reshape(640, 128) + grad[:, 384:512]
            dW[l, 0, m, :, :, :, 384:512] = rest.astype(BF).reshape(4, 2, SHARD, 128)

    @pl.loop(1, SHARDS)
    def _(k):
        remote(VG.at[me], VG.at[me], vs.at[0], vrs.at[0], shard_dev(k)[1]).start()

    gather_one(QKV0)
    gather_one(OUT0)
    pack(0, 1)
    pack(0, 2)
    V[...] = jnp.zeros_like(V)
    GV[...] = jnp.zeros_like(GV)
    gb[...] = jnp.zeros_like(gb)
    gq[...] = jnp.zeros_like(gq)
    bqkv[...] = jnp.zeros_like(bqkv)
    for l in range(2):
        bqkv[l, :, 0:160] = bqv_ref[l, 0:1, :].astype(F32)
        bqkv[l, :, 320:480] = bqv_ref[l, 1:2, :].astype(F32)
    gather_two(QKV0)
    wait_bytes(VG.at[pl.ds(0, SHARDS - 1)], vrs.at[0])
    wait_bytes(VG.at[pl.ds(0, SHARDS - 1)], vs.at[0])
    for i in range(SHARDS):
        low = SHARD * i // 128 * 128
        held = VG[i].astype(F32)
        V[0, :, low : low + 256] += held[0:8]
        V[1, :, low : low + 256] += held[8:16]
    cp_h.wait()
    cp_c.wait()
    gather_one(UP0)
    gather_one(DOWN0Z)
    gather_one(DOWN0X)
    for c in range(MICRO):
        whole = FB[0, c].reshape(ROWS, D).astype(F32)
        unit, _ = norm_parts(whole)
        xrow[0, c] = FB[0, c, y, core].astype(F32)
        FB[0, c] = (unit * vec(0, 0) + vec(0, 2)).astype(BF).reshape(4, 2, 16, D)
    gather_two(OUT0)
    ring_two(UP0)
    gather_wait(QKV0)

    def mask_grads():
        row = lax.broadcasted_iota(jnp.int32, (ROWS, 1), 0) + s * ROWS
        for c in range(MICRO):
            masked = jnp.where(row < len_ref[c], BB[0, c].reshape(ROWS, D).astype(F32), 0.0)
            BB[0, c] = masked.astype(BF).reshape(4, 2, 16, D)
            gyrow[c] = BB[0, c, y, core].astype(F32)

    def bias_sums():
        @pl.loop(1, SHARDS)
        def _(k):
            remote(gb, br.at[k - 1], es.at[1], er.at[1], shard_dev(k)[1]).start()

    def last_sums():
        @pl.loop(1, SHARDS)
        def _(k):
            remote(gq, bq.at[k - 1], es.at[3], er.at[3], shard_dev(k)[1]).start()

    def norm_sums():
        for i in range(11):
            GT[i, 0:8] = GV[0, :, 128 * i : 128 * i + 128]
            GT[i, 8:16] = GV[1, :, 128 * i : 128 * i + 128]

        @pl.loop(1, SHARDS)
        def _(k):
            j, dev = shard_dev(k)
            remote(GT.at[pl.ds(SHARD * j // 128, 2)], vr.at[k - 1], es.at[0], er.at[0], dev).start()

    cp_o = pltpu.make_async_copy(FB.at[4], out_ref, lsem.at[0])
    cp_g = pltpu.make_async_copy(BB.at[4], ingrad_ref, lsem.at[1])

    steps = []
    sums = {}
    for l in (0, 1):
        for c in range(MICRO):
            steps.append((partial(project, l, c), None))
        for c in range(MICRO):
            steps.append((partial(attend, l, c), (2 * l, c)))
            sums[2 * l, c] = (partial(attend_rows, l, c), FB, 2 * l + 1)
        for c in range(MICRO):
            steps.append((partial(feed, l, c), (2 * l + 1, c)))
            sums[2 * l + 1, c] = (partial(feed_rows, l, c), FB, 2 * l + 2)
    for l in (1, 0):
        a0, a1 = 6 - 2 * l, 7 - 2 * l
        for c in range(MICRO):
            steps.append((partial(feed_back, l, c), (a0, c)))
            sums[a0, c] = (partial(feed_back_rows, l, c), BB, 3 - 2 * l)
        for c in range(MICRO):
            steps.append((partial(attend_back, l, c), None))
        for c in range(MICRO):
            steps.append((partial(project_back, l, c), (a1, c)))
            sums[a1, c] = (partial(project_back_rows, l, c), BB, 4 - 2 * l)

    g1, g2, g3, g4 = gather_one, ring_two, ring_three, ring_wait
    d1, d2, d3 = reduce_one, reduce_two, reduce_three
    before = {
        2: [(g2, DOWN0X)],
        3: [(g2, DOWN0Z), (gather_wait, OUT0)],
        4: [(g3, UP0), (g1, PROJ1)],
        5: [(g3, DOWN0Z), (g3, DOWN0X)],
        6: [(g4, UP0), (g2, PROJ1), (g1, UP1)],
        8: [(g3, PROJ1), (g2, UP1), (g1, DOWN1)],
        9: [(g4, PROJ1)],
        10: [(g3, UP1), (g2, DOWN1)],
        12: [(g3, DOWN1)],
        15: [(g4, UP1)],
    }
    between = {
        3: [(pack, 1, 0)],
        4: [(pack, 1, 1)],
        5: [(pack, 1, 2)],
        6: [(mask_grads,)],
        18: [(down_grad, 1), (d1, 1, DOWN)],
        20: [(up_grad, 1), (d1, 1, UP)],
        24: [(out_grad, 1), (d1, 1, OUT)],
        25: [(d2, 1, UP)],
        26: [(qkv_grad, 1), (d1, 1, QKV)],
        27: [(d2, 1, OUT)],
        29: [(down_grad, 0), (d1, 0, DOWN)],
        30: [(up_grad, 0), (d1, 0, UP)],
        31: [(bias_sums,)],
        33: [(out_grad, 0), (d1, 0, OUT)],
        34: [(d2, 0, DOWN)],
        35: [(qkv_grad, 0), (d1, 0, QKV), (last_sums,)],
        36: [(d2, 0, OUT)],
    }
    later = {
        24: [(d2, 1, DOWN)],
        27: [(d3, 1, DOWN)],
        28: [(d3, 1, UP)],
        33: [(d2, 1, QKV)],
        34: [(d2, 0, UP), (d3, 1, OUT)],
    }
    for n in range(len(steps) + 2):
        for fn, *where in before.get(n, ()):
            fn(*where)
        if n < len(steps):
            steps[n][0]()
        for fn, *where in between.get(n, ()):
            fn(*where)
        if n < len(steps) and steps[n][1] is not None:
            rs_mid(*steps[n][1])
        if 1 <= n <= len(steps) and steps[n - 1][1] is not None:
            sums[steps[n - 1][1]][0]()
        if n == len(steps):
            norm_sums()
        if n >= 2 and steps[n - 2][1] is not None:
            a, c = steps[n - 2][1]
            ag_mid(sums[a, c][1], sums[a, c][2], a, c)
        for fn, *where in later.get(n, ()):
            fn(*where)
        if n >= 2 and steps[n - 2][1] is not None:
            ag_end(*steps[n - 2][1])
        if n == 19:
            cp_o.start()

    cp_g.start()
    for l, i in ((1, QKV), (0, DOWN), (0, UP)):
        reduce_three(l, i)
    wait_bytes(vr, er.at[0])
    wait_bytes(vr, es.at[0])
    own = GT[pl.ds(SHARD * me // 128, 2)]
    for k in range(SHARDS - 1):
        own = own + vr[k]
    vr2[7] = own

    @pl.loop(1, 8)
    def _(k):
        remote(vr2.at[7], vr2.at[k - 1], es.at[2], er.at[2], (f, s, (t + k) % 8)).start()

    wait_bytes(br, er.at[1])
    wait_bytes(br, es.at[1])
    wait_bytes(bq, er.at[3])
    wait_bytes(bq, es.at[3])
    totals = gb[...]
    lasts = gq[...]
    for k in range(SHARDS - 1):
        totals = totals + br[k]
        lasts = lasts + bq[k]
    bsum_ref[...] = totals
    for i in range(4):
        bsum_ref[0:1, 128 * i : 128 * i + 128] = lasts[i : i + 1]
    reduce_two(0, QKV)
    for l, i in ((0, OUT),):
        reduce_three(l, i)
    wait_bytes(vr2.at[pl.ds(0, 7)], er.at[2])
    wait_bytes(vr2.at[pl.ds(0, 7)], es.at[2])
    own = vr2[7]
    for k in range(7):
        own = own + vr2[k]
    vsum_ref[...] = own
    reduce_three(0, QKV)
    for l in range(2):
        for i in range(4):
            p, ways = piece(l, i)
            for way, cols in ways:
                pltpu.make_async_copy(dwo.at[l, p, :, cols], dwo_ref.at[l, p, :, cols], osem.at[l, i, way]).wait()
    cp_o.wait()
    cp_g.wait()


def finish(
    out_ref, ingrad_ref, dwo_ref, vsum_ref, bsum_ref,
    hidden_ref, grad_ref, gqkv_ref, gqv_ref, gout_ref, gbout_ref, gup_ref, gbup_ref, gdown_ref, gbdown_ref,
    ggain_ref, gshift_ref,
):
    me = lax.axis_index("fsdp") * 2 + lax.axis_index("seq")
    hidden_ref[...] = out_ref[...].astype(F32)
    grad_ref[...] = ingrad_ref[...].astype(F32)
    rows = jnp.concatenate([vsum_ref[0], vsum_ref[1]], axis=1)
    rows = pltpu.roll(rows, (256 - (SHARD * me) % 128) % 256, 1)
    for l in range(2):
        proj = dwo_ref[l, 0]
        for i in range(3):
            gqkv_ref[l, i] = proj[:, 160 * i : 160 * i + 160]
        gout_ref[l] = proj[:, 480:640].T
        gup_ref[l] = dwo_ref[l, 1]
        gdown_ref[l] = dwo_ref[l, 2]
        gqv_ref[l, 0:1, :] = bsum_ref[l : l + 1, 0:160]
        gqv_ref[l, 1:2, :] = bsum_ref[l : l + 1, 320:480]
        gbup_ref[l : l + 1, :] = bsum_ref[2 + l : 3 + l, :]
        ggain_ref[l] = rows[8 * l : 8 * l + 2, 0:SHARD]
        gshift_ref[l] = rows[8 * l + 2 : 8 * l + 4, 0:SHARD]
        gbout_ref[l : l + 1, :] = rows[8 * l + 4 : 8 * l + 5, 0:SHARD]
        gbdown_ref[l : l + 1, :] = rows[8 * l + 5 : 8 * l + 6, 0:SHARD]


def body(
    hidden_in, cotangent, lengths, qkv_weight, qv_bias, out_weight, out_bias,
    up_weight, up_bias, down_weight, down_bias, ln_gain, ln_bias,
):
    vmem = pl.BlockSpec(memory_space=pltpu.VMEM)
    anys = pl.BlockSpec(memory_space=pl.ANY)
    smem = pl.BlockSpec(memory_space=pltpu.SMEM)
    dma = pltpu.SemaphoreType.DMA
    blocks = (MICRO, 4, 2, 16, D)
    scratch = [
        pltpu.VMEM((2, 3, 2, 4, 2, SHARD, PART), BF),
        pltpu.VMEM((2, 3, 2, 4, 2, SHARD, PART), BF),
        pltpu.VMEM((2, 3, 3, 4, SHARD, 384), BF),
        pltpu.VMEM((2, 3, 3, 2, 2, SHARD, 384), BF),
        pltpu.VMEM((2, 3, 3, SHARD, PART), BF),
        pltpu.VMEM((5,) + blocks, BF),
        pltpu.VMEM((5,) + blocks, BF),
        pltpu.VMEM((8, MICRO, 4, 16, D), BF),
        pltpu.VMEM((8, MICRO, 3, 16, D), BF),
        pltpu.VMEM(blocks, BF),
        pltpu.VMEM((MICRO, 4, 16, D), BF),
        pltpu.VMEM((2, MICRO, ROWS, 512), BF),
        pltpu.VMEM((2, MICRO, ROWS, 384), BF),
        pltpu.VMEM((2, MICRO, 2 * ROWS, 2 * ROWS), F32),
        pltpu.VMEM((2, MICRO, ROWS, 256), BF),
        pltpu.VMEM((2, MICRO, 16, D), F32),
        pltpu.VMEM((2, MICRO, 16, D), F32),
        pltpu.VMEM((2, MICRO, ROWS, PART), F32),
        pltpu.VMEM((2, MICRO, ROWS, PART), BF),
        pltpu.VMEM((MICRO, ROWS, PART), BF),
        pltpu.VMEM((MICRO, ROWS, 512), F32),
        pltpu.VMEM((MICRO, ROWS, 512), BF),
        pltpu.VMEM((MICRO, ROWS, 384), BF),
        pltpu.VMEM((2, MICRO, ROWS, 384), BF),
        pltpu.VMEM((MICRO, 16, D), F32),
        pltpu.VMEM((MICRO, 16, D), F32),
        pltpu.VMEM((SHARDS, 16, 256), BF),
        pltpu.VMEM((2, 8, 1408), F32),
        pltpu.VMEM((2, 8, 1408), F32),
        pltpu.VMEM((11, 16, 128), F32),
        pltpu.VMEM((SHARDS - 1, 2, 16, 128), F32),
        pltpu.VMEM((8, 2, 16, 128), F32),
        pltpu.VMEM((8, PART), F32),
        pltpu.VMEM((SHARDS - 1, 8, PART), F32),
        pltpu.VMEM((8, 128), F32),
        pltpu.VMEM((SHARDS - 1, 8, 128), F32),
        pltpu.VMEM((16, 256), F32),
        pltpu.VMEM((2, 1, 512), F32),
        pltpu.VMEM((2, 3, SHARD, PART), F32),
        dma((8, 2)), dma((8, 2)), dma((8, 2)), dma((8, 2)), dma((8, 2)), dma((8, 2)),
        dma((2, 4, 2)), dma((2, 4, 2)), dma((2, 4, 2)), dma((2, 4, 2)),
        dma((MICRO, 2)), dma((8, MICRO, 2)), dma((MICRO,)), dma((8, MICRO)),
        dma((MICRO,)), dma((8, MICRO)), dma((MICRO,)), dma((8, MICRO)),
        dma((2, MICRO)), dma((2, MICRO)), dma((MICRO,)), dma((2, MICRO)),
        dma((1,)), dma((1,)), dma((4,)), dma((4,)), dma((2,)), dma((2, 2)), dma((2, 4, 2)),
    ]
    out, ingrad, dwo, vsum, bsum = pl.pallas_call(
        kernel,
        name="encoder",
        out_shape=(
            jax.ShapeDtypeStruct(blocks, BF),
            jax.ShapeDtypeStruct(blocks, BF),
            jax.ShapeDtypeStruct((2, 3, SHARD, PART), F32),
            jax.ShapeDtypeStruct((2, 16, 128), F32),
            jax.ShapeDtypeStruct((8, PART), F32),
        ),
        in_specs=[anys, anys, smem, vmem, vmem, vmem, vmem, anys, vmem, anys, vmem, vmem, vmem],
        out_specs=(anys, anys, anys, vmem, vmem),
        scratch_shapes=scratch,
        compiler_params=pltpu.CompilerParams(
            collective_id=0, has_side_effects=True, vmem_limit_bytes=63 * 1024 * 1024
        ),
    )(
        hidden_in.reshape(blocks), cotangent.reshape(blocks), lengths, qkv_weight, qv_bias, out_weight,
        out_bias, up_weight, up_bias, jnp.swapaxes(down_weight, 1, 2), down_bias, ln_gain, ln_bias,
    )
    rows = (MICRO, ROWS, D)
    shapes = (
        rows, rows, (2, 3, SHARD, 160), (2, 2, 160), (2, 160, SHARD), (2, SHARD), (2, SHARD, PART),
        (2, PART), (2, SHARD, PART), (2, SHARD), (2, 2, SHARD), (2, 2, SHARD),
    )
    outs = pl.pallas_call(
        finish,
        name="finish",
        out_shape=tuple(jax.ShapeDtypeStruct(shape, F32) for shape in shapes),
        in_specs=[vmem] * 5,
        out_specs=(vmem,) * 12,
        compiler_params=pltpu.CompilerParams(vmem_limit_bytes=63 * 1024 * 1024),
    )(out.reshape(rows), ingrad.reshape(rows), dwo, vsum, bsum)
    return outs[:8] + (jnp.swapaxes(outs[8], 1, 2),) + outs[9:]


def solution(mesh):
    placed = (
        P("fsdp", "seq", None),
        P("fsdp", "seq", None),
        P("fsdp"),
        P(None, None, ("fsdp", "seq"), "tp"),
        P(None, None, "tp"),
        P(None, "tp", ("fsdp", "seq")),
        P(None, ("fsdp", "seq")),
        P(None, ("fsdp", "seq"), "tp"),
        P(None, "tp"),
        P(None, "tp", ("fsdp", "seq")),
        P(None, ("fsdp", "seq")),
        P(None, None, ("fsdp", "seq")),
        P(None, None, ("fsdp", "seq")),
    )
    return jax.shard_map(
        body,
        mesh=mesh,
        in_specs=placed,
        out_specs=(
            P("fsdp", "seq", None),
            P("fsdp", "seq", None),
            P(None, None, ("fsdp", "seq"), "tp"),
            P(None, None, "tp"),
            P(None, "tp", ("fsdp", "seq")),
            P(None, ("fsdp", "seq")),
            P(None, ("fsdp", "seq"), "tp"),
            P(None, "tp"),
            P(None, "tp", ("fsdp", "seq")),
            P(None, ("fsdp", "seq")),
            P(None, None, ("fsdp", "seq")),
            P(None, None, ("fsdp", "seq")),
        ),
        check_vma=False,
    )
```

```python
from functools import partial
import math

import jax
import jax.numpy as jnp
from jax import lax
from jax.experimental import pallas as pl
from jax.experimental.pallas import tpu as pltpu
from jax.sharding import PartitionSpec as P

HD = 80
EPSILON = 1e-05
MASKED = -1000000000.0
MESH = pl.DeviceIdType.MESH
BF = jnp.bfloat16
F32 = jnp.float32
SCALING = 1.0 / math.sqrt(HD)

D = 1280
MICRO = 3
ROWS = 128
PART = 640
SHARDS = 16
SHARD = 80

PIECES = (
    (0, (256, 512), (0, 256)),
    (0, (512, 640), None),
    (1, (384, 640), (0, 384)),
    (2, (384, 640), (0, 384)),
)
QKV, OUT, UP, DOWN = range(4)
LOADS = (
    (0, 0, (256, 512), (0, 256)),
    (0, 0, (512, 640), None),
    (0, 1, (384, 640), (0, 384)),
    (0, 2, (384, 640), (0, 384)),
    (1, 0, (384, 640), (0, 384)),
    (1, 1, (384, 640), (0, 384)),
    (1, 2, (384, 640), (0, 384)),
)
QKV0, OUT0, UP0, DOWN0, PROJ1, UP1, DOWN1 = range(7)


def dot_nn(a, b):
    return lax.dot_general(a, b, (((1,), (0,)), ((), ())), preferred_element_type=F32)


def dot_nt(a, b):
    return lax.dot_general(a, b, (((1,), (1,)), ((), ())), preferred_element_type=F32)


def dot_tn(a, b):
    return lax.dot_general(a, b, (((0,), (0,)), ((), ())), preferred_element_type=F32)


def norm_parts(values):
    row_mean = jnp.mean(values, axis=-1, keepdims=True)
    centred = values - row_mean
    row_var = jnp.mean(centred * centred, axis=-1, keepdims=True)
    inv = lax.rsqrt(row_var + EPSILON)
    return centred * inv, inv


def norm_back(grad, gain, unit, inv):
    scaled = grad * gain
    return inv * (
        scaled
        - jnp.mean(scaled, axis=-1, keepdims=True)
        - unit * jnp.mean(scaled * unit, axis=-1, keepdims=True)
    )


def split_heads(x):
    first = lax.broadcasted_iota(jnp.int32, x.shape, 1) < HD
    return jnp.concatenate([jnp.where(first, x, 0.0), jnp.where(first, 0.0, x)], axis=0)


def kernel(
    hid_ref, cot_ref, len_ref, wqkv_ref, bqv_ref, wout_ref, bout_ref, wup_ref, bup_ref, wdown_ref, bdown_ref,
    gain_ref, shift_ref,
    out_ref, ingrad_ref, dwo_ref, vsum_ref, bsum_ref,
    W, dW, rb1, rb2, rc, FB, BB, dr, yr, part, sb,
    qkv, kvo, prob, att, xrow, midrow, slope, act,
    gpre, gkeep, gproj, gks, gkr, gyrow, gmidrow,
    VG, V, GV, GT, vr, vr2, gb, br, gq, bq, vrow, bqkv, dwo,
    g1s, g1r, g2s, g2r, g3s, g3r, q1s, q1r, q2s, q2r,
    s1, r1, s2, r2, s3, r3, s4, r4, ks, kr, gs_s, gs_r, vs, vrs, es, er, lsem, wsem, osem,
):
    f, s, t = lax.axis_index("fsdp"), lax.axis_index("seq"), lax.axis_index("tp")
    me = f * 2 + s
    xh, z = f // 4, f % 4
    x = xh * 2 + s
    y, core = t // 2, t % 2
    other = 1 - core

    def shard_dev(k):
        j = (me + k) % SHARDS
        return j, (j // 2, j % 2, t)

    def x_dev(k):
        j = (x + k) % 4
        return j // 2, j % 2, ((j // 2) * 4 + z, j % 2, t)

    def z_dev(k):
        j = (z + k) % 4
        return j, (xh * 4 + j, s, t)

    def y_dev(k):
        j = (y + k) % 4
        return j, (f, s, j * 2 + core)

    core_dev = (f, s, y * 2 + other)
    seq_dev = (f, 1 - s, t)

    def remote(src, dst, ss, rs, dev):
        return pltpu.make_async_remote_copy(
            src_ref=src, dst_ref=dst, send_sem=ss, recv_sem=rs, device_id=dev, device_id_type=MESH
        )

    def wait_bytes(ref, sem):
        pltpu.make_async_copy(ref, ref, sem).wait()

    barrier = pltpu.get_barrier_semaphore()

    @pl.loop(1, SHARDS)
    def _(k):
        pl.semaphore_signal(barrier, inc=1, device_id=shard_dev(k)[1], device_id_type=MESH)

    @pl.loop(1, 8)
    def _(k):
        pl.semaphore_signal(barrier, inc=1, device_id=(f, s, (t + k) % 8), device_id_type=MESH)

    cp_h = pltpu.make_async_copy(hid_ref, FB.at[0], lsem.at[0])
    cp_c = pltpu.make_async_copy(cot_ref, BB.at[0], lsem.at[1])
    cp_h.start()
    cp_c.start()

    for l in range(2):
        for p in range(2):
            pltpu.make_async_copy((wup_ref, wdown_ref)[p].at[l], W.at[l, p + 1, xh, z, s], wsem.at[l, p]).start()

    def pack(l, p):
        if p == 0:
            parts = [wqkv_ref[l, i].astype(F32) for i in range(3)] + [wout_ref[l].astype(F32).T]
            W[l, 0, xh, z, s] = jnp.concatenate(parts, axis=1).astype(BF)
        else:
            pltpu.make_async_copy((wup_ref, wdown_ref)[p - 1].at[l], W.at[l, p, xh, z, s], wsem.at[l, p - 1]).wait()

    vrow[...] = jnp.zeros_like(vrow)
    for l in range(2):
        for r in range(2):
            vrow[8 * l + r : 8 * l + r + 1, 0:SHARD] = gain_ref[l, r : r + 1, :].astype(F32)
            vrow[8 * l + 2 + r : 8 * l + 3 + r, 0:SHARD] = shift_ref[l, r : r + 1, :].astype(F32)
        vrow[8 * l + 4 : 8 * l + 5, 0:SHARD] = bout_ref[l : l + 1, :].astype(F32)
        vrow[8 * l + 5 : 8 * l + 6, 0:SHARD] = bdown_ref[l : l + 1, :].astype(F32)
    VG[me] = pltpu.roll(vrow[...], (SHARD * me) % 128, 1).astype(BF)
    pack(0, 0)
    pl.semaphore_wait(barrier, 22)

    def load(n):
        l, p, one, two = LOADS[n]
        ways = ([(0, slice(*one))] if one else []) + ([(1, slice(*two))] if two else [])
        return l, p, ways

    def gather_one(n):
        l, p, ways = load(n)
        for way, cols in ways:
            own = W.at[l, p, xh, z, s, :, cols]
            for k in (2, 1, 3):
                dev = x_dev(k)[2] if way else z_dev(k)[1]
                remote(own, own, g1s.at[n, way], g1r.at[n, way], dev).start()

    def gather_mid(n):
        l, p, ways = load(n)
        for way, cols in ways:
            three = W.at[l, p, 0, pl.ds(0, 3), 0, :, cols]
            wait_bytes(three, g1r.at[n, way])
            wait_bytes(three, g1s.at[n, way])

    def gather_two(n):
        l, p, ways = load(n)
        gather_mid(n)
        for way, cols in ways:
            four = W.at[l, p, :, z, :, :, cols] if way else W.at[l, p, xh, :, s, :, cols]
            for k in (2, 1, 3):
                dev = z_dev(k)[1] if way else x_dev(k)[2]
                remote(four, four, g2s.at[n, way], g2r.at[n, way], dev).start()

    def gather_wait(n):
        l, p, ways = load(n)
        for way, cols in ways:
            twelve = W.at[l, p, :, pl.ds(0, 3), :, :, cols]
            wait_bytes(twelve, g2r.at[n, way])
            wait_bytes(twelve, g2s.at[n, way])

    def ring_dev(way, k):
        return z_dev(k)[1] if way else x_dev(k)[2]

    def ring_two(n):
        l, p, ways = load(n)
        gather_mid(n)
        for way, cols in ways:
            four = W.at[l, p, :, z, :, :, cols] if way else W.at[l, p, xh, :, s, :, cols]
            for k in (1, 3):
                remote(four, four, g2s.at[n, way], g2r.at[n, way], ring_dev(way, k)).start()

    def ring_mid(n):
        l, p, ways = load(n)
        for way, cols in ways:
            eight = W.at[l, p, 0, :, :, :, cols]
            wait_bytes(eight, g2r.at[n, way])
            wait_bytes(eight, g2s.at[n, way])

    def ring_three(n):
        l, p, ways = load(n)
        ring_mid(n)
        for way, cols in ways:
            if way:
                left = W.at[l, p, 0, (z + 3) % 4, :, :, cols]
                right = W.at[l, p, 1, (z + 1) % 4, :, :, cols]
            else:
                il, ir = (x + 3) % 4, (x + 1) % 4
                left = W.at[l, p, il // 2, pl.ds(0, 2), il % 2, :, cols]
                right = W.at[l, p, ir // 2, pl.ds(2, 2), ir % 2, :, cols]
            remote(left, left, g3s.at[n, way], g3r.at[n, way], ring_dev(way, 1)).start()
            remote(right, right, g3s.at[n, way], g3r.at[n, way], ring_dev(way, 3)).start()

    def ring_wait(n):
        l, p, ways = load(n)
        for way, cols in ways:
            four = W.at[l, p, 0, pl.ds(0, 2), :, :, cols]
            wait_bytes(four, g3r.at[n, way])
            wait_bytes(four, g3s.at[n, way])

    def piece(l, i):
        part_idx, one, two = PIECES[i]
        both = [(0, slice(*one))] + ([(1, slice(*two))] if two else [])
        return part_idx, both

    def reduce_one(l, i):
        p, ways = piece(l, i)
        for way, cols in ways:
            for k in (2, 1, 3):
                if way:
                    j, dev = z_dev(k)
                    four = dW.at[l, p, :, j, :, :, cols]
                    buf = rb2.at[l, p, k - 1, :, :, :, 0 : cols.stop - cols.start]
                else:
                    jh, jl, dev = x_dev(k)
                    four = dW.at[l, p, jh, :, jl, :, cols]
                    buf = rb1.at[l, p, k - 1, :, :, cols.start - 256 : cols.stop - 256]
                remote(four, buf, q1s.at[l, i, way], q1r.at[l, i, way], dev).start()

    def reduce_mid(l, i):
        p, ways = piece(l, i)
        for way, cols in ways:
            twelve = dW.at[l, p, :, pl.ds(0, 3), :, :, cols]
            wait_bytes(twelve, q1r.at[l, i, way])
            wait_bytes(twelve, q1s.at[l, i, way])

    def reduce_two(l, i):
        p, ways = piece(l, i)
        reduce_mid(l, i)

        @pl.loop(0, 4)
        def _(n):
            nh, nl = n // 2, n % 2
            for way, cols in ways:
                if way:
                    total = dW[l, p, nh, z, nl, :, cols].astype(F32)
                    for k in range(3):
                        total = total + rb2[l, p, k, nh, nl, :, 0 : cols.stop - cols.start].astype(F32)
                    dW[l, p, nh, z, nl, :, cols] = total.astype(BF)
                else:
                    total = dW[l, p, xh, n, s, :, cols].astype(F32)
                    for k in range(3):
                        total = total + rb1[l, p, k, n, :, cols.start - 256 : cols.stop - 256].astype(F32)
                    dW[l, p, xh, n, s, :, cols] = total.astype(BF)

        for way, cols in ways:
            for k in (2, 1, 3):
                if way:
                    jh, jl, dev = x_dev(k)
                    one = dW.at[l, p, jh, z, jl, :, cols]
                else:
                    j, dev = z_dev(k)
                    one = dW.at[l, p, xh, j, s, :, cols]
                remote(one, rc.at[l, p, k - 1, :, cols], q2s.at[l, i, way], q2r.at[l, i, way], dev).start()

    def reduce_last(l, i):
        p, ways = piece(l, i)
        for way, cols in ways:
            three = dW.at[l, p, 0, pl.ds(0, 3), 0, :, cols]
            wait_bytes(three, q2r.at[l, i, way])
            wait_bytes(three, q2s.at[l, i, way])

    def reduce_three(l, i):
        p, ways = piece(l, i)
        reduce_last(l, i)
        for way, cols in ways:
            total = dW[l, p, xh, z, s, :, cols].astype(F32)
            for k in range(3):
                total = total + rc[l, p, k, :, cols].astype(F32)
            dwo[l, p, :, cols] = total
            own = dwo.at[l, p, :, cols]
            pltpu.make_async_copy(own, dwo_ref.at[l, p, :, cols], osem.at[l, i, way]).start()

    def vec(l, r):
        return V[l, r : r + 1, 0:D]

    def rs_start(a, c, value_of):
        for h in range(2):
            lanes = slice(640 * h, 640 * h + 640)
            part[c, :, :, :, lanes] = value_of(h).astype(BF).reshape(4, 2, 16, 640)
            remote(
                part.at[c, :, other, :, lanes], dr.at[a, c, :, :, lanes], s1.at[c, h], r1.at[a, c, h], core_dev
            ).start()

    def rs_mid(a, c):
        for h in range(2):
            lanes = slice(640 * h, 640 * h + 640)
            half = dr.at[a, c, :, :, lanes]
            wait_bytes(half, r1.at[a, c, h])
            wait_bytes(half, s1.at[c, h])
            sb[c, :, :, lanes] = (
                part[c, :, core, :, lanes].astype(F32) + dr[a, c, :, :, lanes].astype(F32)
            ).astype(BF)
            for k in (2, 1, 3):
                j, dev = y_dev(k)
                remote(
                    sb.at[c, j, :, lanes], yr.at[a, c, k - 1, :, lanes], s2.at[c], r2.at[a, c], dev
                ).start()

    def rs_end(a, c):
        wait_bytes(yr.at[a, c], r2.at[a, c])
        wait_bytes(yr.at[a, c], s2.at[c])
        total = sb[c, y].astype(F32)
        for k in range(3):
            total = total + yr[a, c, k].astype(F32)
        return total

    def ag_start(buf, i, a, c, value):
        buf[i, c, y, core] = value.astype(BF)
        for k in (2, 1, 3):
            _, dev = y_dev(k)
            remote(buf.at[i, c, y, core], buf.at[i, c, y, core], s3.at[c], r3.at[a, c], dev).start()

    def ag_mid(buf, i, a, c):
        wait_bytes(yr.at[a, c], r3.at[a, c])
        wait_bytes(yr.at[a, c], s3.at[c])
        remote(buf.at[i, c, :, core], buf.at[i, c, :, core], s4.at[c], r4.at[a, c], core_dev).start()

    def ag_end(a, c):
        wait_bytes(dr.at[a, c], r4.at[a, c])
        wait_bytes(dr.at[a, c], s4.at[c])

    def heads_of(l, c):
        own = qkv[l, c].astype(F32)
        far = kvo[l, c].astype(F32)
        q = own[:, 0:160]
        k = jnp.concatenate([own[:, 160:320], far[:, 32:192]], axis=0)
        v = jnp.concatenate([own[:, 320:480], far[:, 192:352]], axis=0)
        return split_heads(q).astype(BF), k, v

    def project(l, c):
        normed = FB[2 * l, c].reshape(ROWS, D)
        proj = dot_nn(normed, W[l, 0, :, :, :, :, 0:512].reshape(D, 512)) + bqkv[l]
        qkv[l, c] = proj.astype(BF)
        remote(qkv.at[l, c, :, 128:512], kvo.at[l, c], ks.at[l, c], kr.at[l, c], seq_dev).start()

    def attend(l, c):
        wait_bytes(kvo.at[l, c], kr.at[l, c])
        wait_bytes(kvo.at[l, c], ks.at[l, c])
        q2, k, v = heads_of(l, c)
        scores = dot_nt(q2, k.astype(BF)) * SCALING
        slot = lax.broadcasted_iota(jnp.int32, (1, 2 * ROWS), 1)
        slot = jnp.where(slot < ROWS, slot + s * ROWS, slot - s * ROWS)
        scores = jnp.where(slot < len_ref[c], scores, MASKED)
        top = jnp.max(scores, axis=-1, keepdims=True)
        powers = jnp.exp(scores - top)
        probs = powers / jnp.sum(powers, axis=-1, keepdims=True)
        prob[l, c] = probs
        low = probs.astype(BF)
        attended = dot_nn(
            jnp.concatenate([low[0:ROWS], low[ROWS:]], axis=1), split_heads(v).astype(BF)
        )
        wide = jnp.concatenate([jnp.zeros((ROWS, 96), F32), attended], axis=1).astype(BF)
        att[l, c] = wide
        rs_start(2 * l, c, lambda h: dot_nt(wide, W[l, 0, h, :, :, :, 384:640].reshape(640, 256)))

    def attend_rows(l, c):
        a = 2 * l
        middle = xrow[l, c] + rs_end(a, c) + vec(l, 4)
        midrow[l, c] = middle
        unit, _ = norm_parts(middle)
        ag_start(FB, 2 * l + 1, a, c, unit * vec(l, 1) + vec(l, 3))

    def feed(l, c):
        normed = FB[2 * l + 1, c].reshape(ROWS, D)
        pre = dot_nn(normed, W[l, 1].reshape(D, PART)) + bup_ref[l : l + 1, :].astype(F32)
        cdf = 0.5 * (1.0 + lax.erf(pre * math.sqrt(0.5)))
        activated = (pre * cdf).astype(BF)
        act[l, c] = activated
        if c == 0:
            ring_wait(DOWN1 if l else DOWN0)
        rs_start(2 * l + 1, c, lambda h: dot_nt(activated, W[l, 2, h].reshape(640, PART)))
        slope[l, c] = cdf + pre * jnp.exp(-0.5 * pre * pre) * (1.0 / math.sqrt(2.0 * math.pi))

    def feed_rows(l, c):
        a = 2 * l + 1
        hidden = midrow[l, c] + rs_end(a, c) + vec(l, 5)
        if l == 0:
            xrow[1, c] = hidden
            unit, _ = norm_parts(hidden)
            hidden = unit * vec(1, 0) + vec(1, 2)
        ag_start(FB, 2 * l + 2, a, c, hidden)

    def feed_back(l, c):
        grad_act = dot_nn(BB[2 - 2 * l, c].reshape(ROWS, D), W[l, 2].reshape(D, PART))
        grad_pre = (grad_act * slope[l, c]).astype(BF)
        gpre[c] = grad_pre
        rs_start(6 - 2 * l, c, lambda h: dot_nt(grad_pre, W[l, 1, h].reshape(640, PART)))
        gb[2 + l : 3 + l, :] += jnp.sum(grad_pre.astype(F32), axis=0, keepdims=True)

    def feed_back_rows(l, c):
        a = 6 - 2 * l
        grad_norm = rs_end(a, c)
        unit, inv = norm_parts(midrow[l, c])
        gy = gyrow[c]
        grad_mid = gy + norm_back(grad_norm, vec(l, 1), unit, inv)
        gmidrow[c] = grad_mid
        ag_start(BB, 3 - 2 * l, a, c, grad_mid)
        GV[l, 1:2, 0:D] += jnp.sum(grad_norm * unit, axis=0, keepdims=True)
        GV[l, 3:4, 0:D] += jnp.sum(grad_norm, axis=0, keepdims=True)
        GV[l, 4:5, 0:D] += jnp.sum(grad_mid, axis=0, keepdims=True)
        GV[l, 5:6, 0:D] += jnp.sum(gy, axis=0, keepdims=True)

    def attend_back(l, c):
        wide = dot_nn(BB[3 - 2 * l, c].reshape(ROWS, D), W[l, 0, :, :, :, :, 384:640].reshape(D, 256))
        ga2 = split_heads(wide[:, 96:256]).astype(BF)
        q2, k, v = heads_of(l, c)
        probs = prob[l, c]
        grad_probs = dot_nt(ga2, v.astype(BF))
        grad_scores = probs * (grad_probs - jnp.sum(probs * grad_probs, axis=-1, keepdims=True))
        low = grad_scores.astype(BF)
        grad_v = dot_tn(probs.astype(BF), ga2)
        grad_k = dot_tn(low, q2) * SCALING
        pad = jnp.zeros((ROWS, 64), F32)
        gks[c] = jnp.concatenate([grad_k[ROWS:], grad_v[ROWS:], pad], axis=1).astype(BF)
        remote(gks.at[c], gkr.at[l, c], gs_s.at[c], gs_r.at[l, c], seq_dev).start()
        grad_q = (
            dot_nn(jnp.concatenate([low[0:ROWS], low[ROWS:]], axis=1), split_heads(k).astype(BF))
            * SCALING
        )
        gkeep[c, :, 0:160] = grad_q
        gkeep[c, :, 160:320] = grad_k[0:ROWS]
        gkeep[c, :, 320:480] = grad_v[0:ROWS]
        gkeep[c, :, 480:512] = jnp.zeros((ROWS, 32), F32)

    def project_back(l, c):
        wait_bytes(gkr.at[l, c], gs_r.at[l, c])
        wait_bytes(gkr.at[l, c], gs_s.at[c])
        far = gkr[l, c].astype(F32)
        gkeep[c, :, 160:480] += far[:, 0:320]
        grads = gkeep[c].astype(BF)
        gproj[c] = grads
        rs_start(7 - 2 * l, c, lambda h: dot_nt(grads, W[l, 0, h, :, :, :, 0:512].reshape(640, 512)))
        total = jnp.sum(grads.astype(F32), axis=0, keepdims=True)
        if l:
            gb[1:2, 0:512] += total
        else:
            for i in range(4):
                gq[i : i + 1, :] += total[:, 128 * i : 128 * i + 128]

    def project_back_rows(l, c):
        a = 7 - 2 * l
        grad_norm = rs_end(a, c)
        unit, inv = norm_parts(xrow[l, c])
        gy = gmidrow[c] + norm_back(grad_norm, vec(l, 0), unit, inv)
        gyrow[c] = gy
        ag_start(BB, 4 - 2 * l, a, c, gy)
        GV[l, 0:1, 0:D] += jnp.sum(grad_norm * unit, axis=0, keepdims=True)
        GV[l, 2:3, 0:D] += jnp.sum(grad_norm, axis=0, keepdims=True)

    def left_of(buf, i, m):
        lanes = pl.ds(pl.multiple_of(m * 640, 128), 640)
        return buf[i, :, :, :, :, lanes].reshape(MICRO * ROWS, 640)

    def down_grad(l):
        @pl.loop(0, 2)
        def _(m):
            right = act[l].reshape(MICRO * ROWS, PART)
            dW[l, 2, m] = dot_tn(left_of(BB, 2 - 2 * l, m), right).astype(BF).reshape(4, 2, SHARD, PART)

    def up_grad(l):
        @pl.loop(0, 2)
        def _(m):
            right = gpre[...].reshape(MICRO * ROWS, PART)
            dW[l, 1, m] = dot_tn(left_of(FB, 2 * l + 1, m), right).astype(BF).reshape(4, 2, SHARD, PART)

    def out_grad(l):
        @pl.loop(0, 2)
        def _(m):
            grad = dot_tn(left_of(BB, 3 - 2 * l, m), att[l].reshape(MICRO * ROWS, 256))
            dW[l, 0, m, :, :, :, 384:640] = grad.astype(BF).reshape(4, 2, SHARD, 256)

    def qkv_grad(l):
        @pl.loop(0, 2)
        def _(m):
            grad = dot_tn(left_of(FB, 2 * l, m), gproj[...].reshape(MICRO * ROWS, 512))
            dW[l, 0, m, :, :, :, 0:384] = grad[:, 0:384].astype(BF).reshape(4, 2, SHARD, 384)
            rest = dW[l, 0, m, :, :, :, 384:512].astype(F32).reshape(640, 128) + grad[:, 384:512]
            dW[l, 0, m, :, :, :, 384:512] = rest.astype(BF).reshape(4, 2, SHARD, 128)

    gather_one(QKV0)

    @pl.loop(1, SHARDS)
    def _(k):
        remote(VG.at[me], VG.at[me], vs.at[0], vrs.at[0], shard_dev(k)[1]).start()

    gather_one(OUT0)
    pack(0, 1)
    pack(0, 2)
    V[...] = jnp.zeros_like(V)
    GV[...] = jnp.zeros_like(GV)
    gb[...] = jnp.zeros_like(gb)
    gq[...] = jnp.zeros_like(gq)
    bqkv[...] = jnp.zeros_like(bqkv)
    for l in range(2):
        bqkv[l, :, 0:160] = bqv_ref[l, 0:1, :].astype(F32)
        bqkv[l, :, 320:480] = bqv_ref[l, 1:2, :].astype(F32)
    gather_two(QKV0)
    wait_bytes(VG.at[pl.ds(0, SHARDS - 1)], vrs.at[0])
    wait_bytes(VG.at[pl.ds(0, SHARDS - 1)], vs.at[0])
    for i in range(SHARDS):
        low = SHARD * i // 128 * 128
        held = VG[i].astype(F32)
        V[0, :, low : low + 256] += held[0:8]
        V[1, :, low : low + 256] += held[8:16]
    cp_h.wait()
    cp_c.wait()
    gather_one(UP0)
    gather_one(DOWN0)
    for c in range(MICRO):
        whole = FB[0, c].reshape(ROWS, D).astype(F32)
        unit, _ = norm_parts(whole)
        xrow[0, c] = FB[0, c, y, core].astype(F32)
        FB[0, c] = (unit * vec(0, 0) + vec(0, 2)).astype(BF).reshape(4, 2, 16, D)
    gather_two(OUT0)
    ring_two(UP0)
    gather_wait(QKV0)

    def mask_grads():
        row = lax.broadcasted_iota(jnp.int32, (ROWS, 1), 0) + s * ROWS
        for c in range(MICRO):
            masked = jnp.where(row < len_ref[c], BB[0, c].reshape(ROWS, D).astype(F32), 0.0)
            BB[0, c] = masked.astype(BF).reshape(4, 2, 16, D)
            gyrow[c] = BB[0, c, y, core].astype(F32)

    def bias_sums():
        @pl.loop(1, SHARDS)
        def _(k):
            remote(gb, br.at[k - 1], es.at[1], er.at[1], shard_dev(k)[1]).start()

    def last_sums():
        @pl.loop(1, SHARDS)
        def _(k):
            remote(gq, bq.at[k - 1], es.at[3], er.at[3], shard_dev(k)[1]).start()

    def norm_sums():
        for i in range(11):
            lanes = slice(128 * i, 128 * i + 128)
            GT[i] = jnp.concatenate([GV[0, :, lanes], GV[1, :, lanes]], axis=0).astype(BF)

        @pl.loop(1, SHARDS)
        def _(k):
            j, dev = shard_dev(k)
            remote(GT.at[pl.ds(SHARD * j // 128, 2)], vr.at[k - 1], es.at[0], er.at[0], dev).start()

    cp_o = pltpu.make_async_copy(FB.at[4], out_ref, lsem.at[0])
    cp_g = pltpu.make_async_copy(BB.at[4], ingrad_ref, lsem.at[1])

    steps = []
    sums = {}
    for l in (0, 1):
        for c in range(MICRO):
            steps.append((partial(project, l, c), None))
        for c in range(MICRO):
            steps.append((partial(attend, l, c), (2 * l, c)))
            sums[2 * l, c] = (partial(attend_rows, l, c), FB, 2 * l + 1)
        for c in range(MICRO):
            steps.append((partial(feed, l, c), (2 * l + 1, c)))
            sums[2 * l + 1, c] = (partial(feed_rows, l, c), FB, 2 * l + 2)
    for l in (1, 0):
        a0, a1 = 6 - 2 * l, 7 - 2 * l
        for c in range(MICRO):
            steps.append((partial(feed_back, l, c), (a0, c)))
            sums[a0, c] = (partial(feed_back_rows, l, c), BB, 3 - 2 * l)
        for c in range(MICRO):
            steps.append((partial(attend_back, l, c), None))
        for c in range(MICRO):
            steps.append((partial(project_back, l, c), (a1, c)))
            sums[a1, c] = (partial(project_back_rows, l, c), BB, 4 - 2 * l)

    g1, g2, g3, g4 = gather_one, ring_two, ring_three, ring_wait
    d1, d2, d3 = reduce_one, reduce_two, reduce_three
    before = {
        3: [(g2, DOWN0), (gather_wait, OUT0)],
        4: [(g1, PROJ1)],
        5: [(g3, DOWN0), (g2, PROJ1)],
        6: [(g4, UP0), (g1, UP1)],
        7: [(g3, PROJ1), (g2, UP1), (g1, DOWN1)],
        9: [(g4, PROJ1), (g3, UP1), (g2, DOWN1)],
        12: [(g3, DOWN1)],
        15: [(g4, UP1)],
    }
    between = {
        3: [(g3, UP0), (pack, 1, 0)],
        4: [(pack, 1, 1)],
        5: [(pack, 1, 2)],
        6: [(mask_grads,)],
        18: [(down_grad, 1), (d1, 1, DOWN)],
        20: [(up_grad, 1), (d1, 1, UP)],
        22: [(d2, 1, DOWN)],
        24: [(out_grad, 1), (d1, 1, OUT)],
        26: [(qkv_grad, 1), (d1, 1, QKV)],
        27: [(d2, 1, OUT)],
        29: [(down_grad, 0), (d1, 0, DOWN)],
        30: [(up_grad, 0), (d1, 0, UP)],
        31: [(d2, 1, QKV), (bias_sums,)],
        33: [(out_grad, 0), (d1, 0, OUT)],
        34: [(d2, 0, DOWN)],
        35: [(qkv_grad, 0), (d1, 0, QKV), (last_sums,)],
        36: [(d2, 0, OUT)],
    }
    later = {
        25: [(d2, 1, UP)],
        34: [(d2, 0, UP)],
    }
    for n in range(len(steps) + 2):
        for fn, *where in before.get(n, ()):
            fn(*where)
        if n < len(steps):
            steps[n][0]()
        for fn, *where in between.get(n, ()):
            fn(*where)
        if n < len(steps) and steps[n][1] is not None:
            rs_mid(*steps[n][1])
        if 1 <= n <= len(steps) and steps[n - 1][1] is not None:
            sums[steps[n - 1][1]][0]()
        if n == len(steps):
            norm_sums()
        if n == len(steps) + 1:
            reduce_two(0, QKV)
        if n >= 2 and steps[n - 2][1] is not None:
            a, c = steps[n - 2][1]
            ag_mid(sums[a, c][1], sums[a, c][2], a, c)
        for fn, *where in later.get(n, ()):
            fn(*where)
        if n >= 2 and steps[n - 2][1] is not None:
            ag_end(*steps[n - 2][1])
        if n == 19:
            cp_o.start()

    cp_g.start()
    for l, i in ((1, DOWN), (1, UP), (1, OUT), (1, QKV)):
        reduce_three(l, i)
    wait_bytes(vr, er.at[0])
    wait_bytes(vr, es.at[0])
    own = GT[pl.ds(SHARD * me // 128, 2)].astype(F32)
    for k in range(SHARDS - 1):
        own = own + vr[k].astype(F32)
    vr2[7] = own

    @pl.loop(1, 8)
    def _(k):
        remote(vr2.at[7], vr2.at[k - 1], es.at[2], er.at[2], (f, s, (t + k) % 8)).start()

    wait_bytes(br, er.at[1])
    wait_bytes(br, es.at[1])
    wait_bytes(bq, er.at[3])
    wait_bytes(bq, es.at[3])
    totals = gb[...]
    lasts = gq[...]
    for k in range(SHARDS - 1):
        totals = totals + br[k]
        lasts = lasts + bq[k]
    bsum_ref[...] = totals
    for i in range(4):
        bsum_ref[0:1, 128 * i : 128 * i + 128] = lasts[i : i + 1]
    for l, i in ((0, DOWN), (0, UP), (0, OUT)):
        reduce_three(l, i)
    wait_bytes(vr2.at[pl.ds(0, 7)], er.at[2])
    wait_bytes(vr2.at[pl.ds(0, 7)], es.at[2])
    own = vr2[7]
    for k in range(7):
        own = own + vr2[k]
    vsum_ref[...] = own
    reduce_three(0, QKV)
    for l in range(2):
        for i in range(4):
            p, ways = piece(l, i)
            for way, cols in ways:
                pltpu.make_async_copy(dwo.at[l, p, :, cols], dwo_ref.at[l, p, :, cols], osem.at[l, i, way]).wait()
    cp_o.wait()
    cp_g.wait()


def finish(
    out_ref, ingrad_ref, dwo_ref, vsum_ref, bsum_ref,
    hidden_ref, grad_ref, gqkv_ref, gqv_ref, gout_ref, gbout_ref, gup_ref, gbup_ref, gdown_ref, gbdown_ref,
    ggain_ref, gshift_ref,
):
    me = lax.axis_index("fsdp") * 2 + lax.axis_index("seq")
    hidden_ref[...] = out_ref[...].astype(F32)
    grad_ref[...] = ingrad_ref[...].astype(F32)
    rows = jnp.concatenate([vsum_ref[0], vsum_ref[1]], axis=1)
    rows = pltpu.roll(rows, (256 - (SHARD * me) % 128) % 256, 1)
    for l in range(2):
        proj = dwo_ref[l, 0]
        for i in range(3):
            gqkv_ref[l, i] = proj[:, 160 * i : 160 * i + 160]
        gout_ref[l] = proj[:, 480:640].T
        gup_ref[l] = dwo_ref[l, 1]
        gdown_ref[l] = dwo_ref[l, 2]
        gqv_ref[l, 0:1, :] = bsum_ref[l : l + 1, 0:160]
        gqv_ref[l, 1:2, :] = bsum_ref[l : l + 1, 320:480]
        gbup_ref[l : l + 1, :] = bsum_ref[2 + l : 3 + l, :]
        ggain_ref[l] = rows[8 * l : 8 * l + 2, 0:SHARD]
        gshift_ref[l] = rows[8 * l + 2 : 8 * l + 4, 0:SHARD]
        gbout_ref[l : l + 1, :] = rows[8 * l + 4 : 8 * l + 5, 0:SHARD]
        gbdown_ref[l : l + 1, :] = rows[8 * l + 5 : 8 * l + 6, 0:SHARD]


def body(
    hidden_in, cotangent, lengths, qkv_weight, qv_bias, out_weight, out_bias,
    up_weight, up_bias, down_weight, down_bias, ln_gain, ln_bias,
):
    vmem = pl.BlockSpec(memory_space=pltpu.VMEM)
    anys = pl.BlockSpec(memory_space=pl.ANY)
    smem = pl.BlockSpec(memory_space=pltpu.SMEM)
    dma = pltpu.SemaphoreType.DMA
    blocks = (MICRO, 4, 2, 16, D)
    scratch = [
        pltpu.VMEM((2, 3, 2, 4, 2, SHARD, PART), BF),
        pltpu.VMEM((2, 3, 2, 4, 2, SHARD, PART), BF),
        pltpu.VMEM((2, 3, 3, 4, SHARD, 384), BF),
        pltpu.VMEM((2, 3, 3, 2, 2, SHARD, 384), BF),
        pltpu.VMEM((2, 3, 3, SHARD, PART), BF),
        pltpu.VMEM((5,) + blocks, BF),
        pltpu.VMEM((5,) + blocks, BF),
        pltpu.VMEM((8, MICRO, 4, 16, D), BF),
        pltpu.VMEM((8, MICRO, 3, 16, D), BF),
        pltpu.VMEM(blocks, BF),
        pltpu.VMEM((MICRO, 4, 16, D), BF),
        pltpu.VMEM((2, MICRO, ROWS, 512), BF),
        pltpu.VMEM((2, MICRO, ROWS, 384), BF),
        pltpu.VMEM((2, MICRO, 2 * ROWS, 2 * ROWS), F32),
        pltpu.VMEM((2, MICRO, ROWS, 256), BF),
        pltpu.VMEM((2, MICRO, 16, D), F32),
        pltpu.VMEM((2, MICRO, 16, D), F32),
        pltpu.VMEM((2, MICRO, ROWS, PART), F32),
        pltpu.VMEM((2, MICRO, ROWS, PART), BF),
        pltpu.VMEM((MICRO, ROWS, PART), BF),
        pltpu.VMEM((MICRO, ROWS, 512), F32),
        pltpu.VMEM((MICRO, ROWS, 512), BF),
        pltpu.VMEM((MICRO, ROWS, 384), BF),
        pltpu.VMEM((2, MICRO, ROWS, 384), BF),
        pltpu.VMEM((MICRO, 16, D), F32),
        pltpu.VMEM((MICRO, 16, D), F32),
        pltpu.VMEM((SHARDS, 16, 256), BF),
        pltpu.VMEM((2, 8, 1408), F32),
        pltpu.VMEM((2, 8, 1408), F32),
        pltpu.VMEM((11, 16, 128), BF),
        pltpu.VMEM((SHARDS - 1, 2, 16, 128), BF),
        pltpu.VMEM((8, 2, 16, 128), F32),
        pltpu.VMEM((8, PART), F32),
        pltpu.VMEM((SHARDS - 1, 8, PART), F32),
        pltpu.VMEM((8, 128), F32),
        pltpu.VMEM((SHARDS - 1, 8, 128), F32),
        pltpu.VMEM((16, 256), F32),
        pltpu.VMEM((2, 1, 512), F32),
        pltpu.VMEM((2, 3, SHARD, PART), F32),
        dma((8, 2)), dma((8, 2)), dma((8, 2)), dma((8, 2)), dma((8, 2)), dma((8, 2)),
        dma((2, 4, 2)), dma((2, 4, 2)), dma((2, 4, 2)), dma((2, 4, 2)),
        dma((MICRO, 2)), dma((8, MICRO, 2)), dma((MICRO,)), dma((8, MICRO)),
        dma((MICRO,)), dma((8, MICRO)), dma((MICRO,)), dma((8, MICRO)),
        dma((2, MICRO)), dma((2, MICRO)), dma((MICRO,)), dma((2, MICRO)),
        dma((1,)), dma((1,)), dma((4,)), dma((4,)), dma((2,)), dma((2, 2)), dma((2, 4, 2)),
    ]
    out, ingrad, dwo, vsum, bsum = pl.pallas_call(
        kernel,
        name="encoder",
        out_shape=(
            jax.ShapeDtypeStruct(blocks, BF),
            jax.ShapeDtypeStruct(blocks, BF),
            jax.ShapeDtypeStruct((2, 3, SHARD, PART), F32),
            jax.ShapeDtypeStruct((2, 16, 128), F32),
            jax.ShapeDtypeStruct((8, PART), F32),
        ),
        in_specs=[anys, anys, smem, vmem, vmem, vmem, vmem, anys, vmem, anys, vmem, vmem, vmem],
        out_specs=(anys, anys, anys, vmem, vmem),
        scratch_shapes=scratch,
        compiler_params=pltpu.CompilerParams(
            collective_id=0, has_side_effects=True, vmem_limit_bytes=63 * 1024 * 1024
        ),
    )(
        hidden_in.reshape(blocks), cotangent.reshape(blocks), lengths, qkv_weight, qv_bias, out_weight,
        out_bias, up_weight, up_bias, jnp.swapaxes(down_weight, 1, 2), down_bias, ln_gain, ln_bias,
    )
    rows = (MICRO, ROWS, D)
    shapes = (
        rows, rows, (2, 3, SHARD, 160), (2, 2, 160), (2, 160, SHARD), (2, SHARD), (2, SHARD, PART),
        (2, PART), (2, SHARD, PART), (2, SHARD), (2, 2, SHARD), (2, 2, SHARD),
    )
    outs = pl.pallas_call(
        finish,
        name="finish",
        out_shape=tuple(jax.ShapeDtypeStruct(shape, F32) for shape in shapes),
        in_specs=[vmem] * 5,
        out_specs=(vmem,) * 12,
        compiler_params=pltpu.CompilerParams(vmem_limit_bytes=63 * 1024 * 1024),
    )(out.reshape(rows), ingrad.reshape(rows), dwo, vsum, bsum)
    return outs[:8] + (jnp.swapaxes(outs[8], 1, 2),) + outs[9:]


def solution(mesh):
    placed = (
        P("fsdp", "seq", None),
        P("fsdp", "seq", None),
        P("fsdp"),
        P(None, None, ("fsdp", "seq"), "tp"),
        P(None, None, "tp"),
        P(None, "tp", ("fsdp", "seq")),
        P(None, ("fsdp", "seq")),
        P(None, ("fsdp", "seq"), "tp"),
        P(None, "tp"),
        P(None, "tp", ("fsdp", "seq")),
        P(None, ("fsdp", "seq")),
        P(None, None, ("fsdp", "seq")),
        P(None, None, ("fsdp", "seq")),
    )
    return jax.shard_map(
        body,
        mesh=mesh,
        in_specs=placed,
        out_specs=(
            P("fsdp", "seq", None),
            P("fsdp", "seq", None),
            P(None, None, ("fsdp", "seq"), "tp"),
            P(None, None, "tp"),
            P(None, "tp", ("fsdp", "seq")),
            P(None, ("fsdp", "seq")),
            P(None, ("fsdp", "seq"), "tp"),
            P(None, "tp"),
            P(None, "tp", ("fsdp", "seq")),
            P(None, ("fsdp", "seq")),
            P(None, None, ("fsdp", "seq")),
            P(None, None, ("fsdp", "seq")),
        ),
        check_vma=False,
    )
```

```python
from functools import partial
import math

import jax
import jax.numpy as jnp
from jax import lax
from jax.experimental import pallas as pl
from jax.experimental.pallas import tpu as pltpu
from jax.sharding import PartitionSpec as P

HD = 80
EPSILON = 1e-05
MASKED = -1000000000.0
MESH = pl.DeviceIdType.MESH
BF = jnp.bfloat16
F32 = jnp.float32
SCALING = 1.0 / math.sqrt(HD)

D = 1280
MICRO = 3
ROWS = 128
PART = 640
SHARDS = 16
SHARD = 80

PIECES = (
    (0, (256, 512), (0, 256)),
    (0, (512, 640), None),
    (1, (384, 640), (0, 384)),
    (2, (384, 640), (0, 384)),
)
QKV, OUT, UP, DOWN = range(4)
LOADS = (
    (0, 0, (256, 512), (0, 256)),
    (0, 0, (512, 640), None),
    (0, 1, (384, 640), (0, 384)),
    (0, 2, (384, 640), (0, 384)),
    (1, 0, (384, 640), (0, 384)),
    (1, 1, (384, 640), (0, 384)),
    (1, 2, (384, 640), (0, 384)),
)
QKV0, OUT0, UP0, DOWN0, PROJ1, UP1, DOWN1 = range(7)


def dot_nn(a, b):
    return lax.dot_general(a, b, (((1,), (0,)), ((), ())), preferred_element_type=F32)


def dot_nt(a, b):
    return lax.dot_general(a, b, (((1,), (1,)), ((), ())), preferred_element_type=F32)


def dot_tn(a, b):
    return lax.dot_general(a, b, (((0,), (0,)), ((), ())), preferred_element_type=F32)


def norm_parts(values):
    row_mean = jnp.mean(values, axis=-1, keepdims=True)
    centred = values - row_mean
    row_var = jnp.mean(centred * centred, axis=-1, keepdims=True)
    inv = lax.rsqrt(row_var + EPSILON)
    return centred * inv, inv


def norm_back(grad, gain, unit, inv):
    scaled = grad * gain
    return inv * (
        scaled
        - jnp.mean(scaled, axis=-1, keepdims=True)
        - unit * jnp.mean(scaled * unit, axis=-1, keepdims=True)
    )


def split_heads(x):
    first = lax.broadcasted_iota(jnp.int32, x.shape, 1) < HD
    return jnp.concatenate([jnp.where(first, x, 0.0), jnp.where(first, 0.0, x)], axis=0)


def kernel(
    hid_ref, cot_ref, len_ref, wqkv_ref, bqv_ref, wout_ref, bout_ref, wup_ref, bup_ref, wdown_ref, bdown_ref,
    gain_ref, shift_ref,
    out_ref, ingrad_ref, dwo_ref, vsum_ref, bsum_ref,
    W, dW, rb1, rb2, rc, FB, BB, dr, yr, part, sb,
    qkv, kvo, prob, att, xrow, midrow, slope, act,
    gpre, gkeep, gproj, gks, gkr, gyrow, gmidrow,
    VG, V, GV, GT, vr, vr2, gb, br, gq, bq, vrow, bqkv, dwo,
    g1s, g1r, g2s, g2r, g3s, g3r, q1s, q1r, q2s, q2r,
    s1, r1, s2, r2, s3, r3, s4, r4, ks, kr, gs_s, gs_r, vs, vrs, es, er, lsem, wsem, osem,
):
    f, s, t = lax.axis_index("fsdp"), lax.axis_index("seq"), lax.axis_index("tp")
    me = f * 2 + s
    xh, z = f // 4, f % 4
    x = xh * 2 + s
    y, core = t // 2, t % 2
    other = 1 - core

    def shard_dev(k):
        j = (me + k) % SHARDS
        return j, (j // 2, j % 2, t)

    def x_dev(k):
        j = (x + k) % 4
        return j // 2, j % 2, ((j // 2) * 4 + z, j % 2, t)

    def z_dev(k):
        j = (z + k) % 4
        return j, (xh * 4 + j, s, t)

    def y_dev(k):
        j = (y + k) % 4
        return j, (f, s, j * 2 + core)

    core_dev = (f, s, y * 2 + other)
    seq_dev = (f, 1 - s, t)

    def remote(src, dst, ss, rs, dev):
        return pltpu.make_async_remote_copy(
            src_ref=src, dst_ref=dst, send_sem=ss, recv_sem=rs, device_id=dev, device_id_type=MESH
        )

    def wait_bytes(ref, sem):
        pltpu.make_async_copy(ref, ref, sem).wait()

    barrier = pltpu.get_barrier_semaphore()

    @pl.loop(1, SHARDS)
    def _(k):
        pl.semaphore_signal(barrier, inc=1, device_id=shard_dev(k)[1], device_id_type=MESH)

    @pl.loop(1, 8)
    def _(k):
        pl.semaphore_signal(barrier, inc=1, device_id=(f, s, (t + k) % 8), device_id_type=MESH)

    cp_h = pltpu.make_async_copy(hid_ref, FB.at[0], lsem.at[0])
    cp_c = pltpu.make_async_copy(cot_ref, BB.at[0], lsem.at[1])
    cp_h.start()
    cp_c.start()

    for l in range(2):
        for p in range(2):
            pltpu.make_async_copy((wup_ref, wdown_ref)[p].at[l], W.at[l, p + 1, xh, z, s], wsem.at[l, p]).start()

    def pack(l, p):
        if p == 0:
            parts = [wqkv_ref[l, i].astype(F32) for i in range(3)] + [wout_ref[l].astype(F32).T]
            W[l, 0, xh, z, s] = jnp.concatenate(parts, axis=1).astype(BF)
        else:
            pltpu.make_async_copy((wup_ref, wdown_ref)[p - 1].at[l], W.at[l, p, xh, z, s], wsem.at[l, p - 1]).wait()

    vrow[...] = jnp.zeros_like(vrow)
    for l in range(2):
        for r in range(2):
            vrow[8 * l + r : 8 * l + r + 1, 0:SHARD] = gain_ref[l, r : r + 1, :].astype(F32)
            vrow[8 * l + 2 + r : 8 * l + 3 + r, 0:SHARD] = shift_ref[l, r : r + 1, :].astype(F32)
        vrow[8 * l + 4 : 8 * l + 5, 0:SHARD] = bout_ref[l : l + 1, :].astype(F32)
        vrow[8 * l + 5 : 8 * l + 6, 0:SHARD] = bdown_ref[l : l + 1, :].astype(F32)
    VG[me] = pltpu.roll(vrow[...], (SHARD * me) % 128, 1).astype(BF)
    pack(0, 0)
    pl.semaphore_wait(barrier, 22)

    def load(n):
        l, p, one, two = LOADS[n]
        ways = ([(0, slice(*one))] if one else []) + ([(1, slice(*two))] if two else [])
        return l, p, ways

    def gather_one(n):
        l, p, ways = load(n)
        for way, cols in ways:
            own = W.at[l, p, xh, z, s, :, cols]
            for k in (2, 1, 3):
                dev = x_dev(k)[2] if way else z_dev(k)[1]
                remote(own, own, g1s.at[n, way], g1r.at[n, way], dev).start()

    def gather_mid(n):
        l, p, ways = load(n)
        for way, cols in ways:
            three = W.at[l, p, 0, pl.ds(0, 3), 0, :, cols]
            wait_bytes(three, g1r.at[n, way])
            wait_bytes(three, g1s.at[n, way])

    def gather_two(n):
        l, p, ways = load(n)
        gather_mid(n)
        for way, cols in ways:
            four = W.at[l, p, :, z, :, :, cols] if way else W.at[l, p, xh, :, s, :, cols]
            for k in (2, 1, 3):
                dev = z_dev(k)[1] if way else x_dev(k)[2]
                remote(four, four, g2s.at[n, way], g2r.at[n, way], dev).start()

    def gather_wait(n):
        l, p, ways = load(n)
        for way, cols in ways:
            twelve = W.at[l, p, :, pl.ds(0, 3), :, :, cols]
            wait_bytes(twelve, g2r.at[n, way])
            wait_bytes(twelve, g2s.at[n, way])

    def ring_dev(way, k):
        return z_dev(k)[1] if way else x_dev(k)[2]

    def ring_two(n):
        l, p, ways = load(n)
        gather_mid(n)
        for way, cols in ways:
            four = W.at[l, p, :, z, :, :, cols] if way else W.at[l, p, xh, :, s, :, cols]
            for k in (1, 3):
                remote(four, four, g2s.at[n, way], g2r.at[n, way], ring_dev(way, k)).start()

    def ring_mid(n):
        l, p, ways = load(n)
        for way, cols in ways:
            eight = W.at[l, p, 0, :, :, :, cols]
            wait_bytes(eight, g2r.at[n, way])
            wait_bytes(eight, g2s.at[n, way])

    def ring_three(n):
        l, p, ways = load(n)
        ring_mid(n)
        for way, cols in ways:
            if way:
                left = W.at[l, p, 0, (z + 3) % 4, :, :, cols]
                right = W.at[l, p, 1, (z + 1) % 4, :, :, cols]
            else:
                il, ir = (x + 3) % 4, (x + 1) % 4
                left = W.at[l, p, il // 2, pl.ds(0, 2), il % 2, :, cols]
                right = W.at[l, p, ir // 2, pl.ds(2, 2), ir % 2, :, cols]
            remote(left, left, g3s.at[n, way], g3r.at[n, way], ring_dev(way, 1)).start()
            remote(right, right, g3s.at[n, way], g3r.at[n, way], ring_dev(way, 3)).start()

    def ring_wait(n):
        l, p, ways = load(n)
        for way, cols in ways:
            four = W.at[l, p, 0, pl.ds(0, 2), :, :, cols]
            wait_bytes(four, g3r.at[n, way])
            wait_bytes(four, g3s.at[n, way])

    def piece(l, i):
        part_idx, one, two = PIECES[i]
        both = [(0, slice(*one))] + ([(1, slice(*two))] if two else [])
        return part_idx, both

    def reduce_one(l, i):
        p, ways = piece(l, i)
        for way, cols in ways:
            for k in (2, 1, 3):
                if way:
                    j, dev = z_dev(k)
                    four = dW.at[l, p, :, j, :, :, cols]
                    buf = rb2.at[l, p, k - 1, :, :, :, 0 : cols.stop - cols.start]
                else:
                    jh, jl, dev = x_dev(k)
                    four = dW.at[l, p, jh, :, jl, :, cols]
                    buf = rb1.at[l, p, k - 1, :, :, cols.start - 256 : cols.stop - 256]
                remote(four, buf, q1s.at[l, i, way], q1r.at[l, i, way], dev).start()

    def reduce_mid(l, i):
        p, ways = piece(l, i)
        for way, cols in ways:
            twelve = dW.at[l, p, :, pl.ds(0, 3), :, :, cols]
            wait_bytes(twelve, q1r.at[l, i, way])
            wait_bytes(twelve, q1s.at[l, i, way])

    def reduce_two(l, i):
        p, ways = piece(l, i)
        reduce_mid(l, i)

        @pl.loop(0, 4)
        def _(n):
            nh, nl = n // 2, n % 2
            for way, cols in ways:
                if way:
                    total = dW[l, p, nh, z, nl, :, cols].astype(F32)
                    for k in range(3):
                        total = total + rb2[l, p, k, nh, nl, :, 0 : cols.stop - cols.start].astype(F32)
                    dW[l, p, nh, z, nl, :, cols] = total.astype(BF)
                else:
                    total = dW[l, p, xh, n, s, :, cols].astype(F32)
                    for k in range(3):
                        total = total + rb1[l, p, k, n, :, cols.start - 256 : cols.stop - 256].astype(F32)
                    dW[l, p, xh, n, s, :, cols] = total.astype(BF)

        for way, cols in ways:
            for k in (2, 1, 3):
                if way:
                    jh, jl, dev = x_dev(k)
                    one = dW.at[l, p, jh, z, jl, :, cols]
                else:
                    j, dev = z_dev(k)
                    one = dW.at[l, p, xh, j, s, :, cols]
                remote(one, rc.at[l, p, k - 1, :, cols], q2s.at[l, i, way], q2r.at[l, i, way], dev).start()

    def reduce_last(l, i):
        p, ways = piece(l, i)
        for way, cols in ways:
            three = dW.at[l, p, 0, pl.ds(0, 3), 0, :, cols]
            wait_bytes(three, q2r.at[l, i, way])
            wait_bytes(three, q2s.at[l, i, way])

    def reduce_three(l, i):
        p, ways = piece(l, i)
        reduce_last(l, i)
        for way, cols in ways:
            total = dW[l, p, xh, z, s, :, cols].astype(F32)
            for k in range(3):
                total = total + rc[l, p, k, :, cols].astype(F32)
            dwo[l, p, :, cols] = total
            own = dwo.at[l, p, :, cols]
            pltpu.make_async_copy(own, dwo_ref.at[l, p, :, cols], osem.at[l, i, way]).start()

    def vec(l, r):
        return V[l, r : r + 1, 0:D]

    def rs_start(a, c, value_of):
        for h in range(2):
            lanes = slice(640 * h, 640 * h + 640)
            part[c, :, :, :, lanes] = value_of(h).astype(BF).reshape(4, 2, 16, 640)
            remote(
                part.at[c, :, other, :, lanes], dr.at[a, c, :, :, lanes], s1.at[c, h], r1.at[a, c, h], core_dev
            ).start()

    def place(a, c):
        return c + MICRO if a == 3 else c

    def rs_mid(a, c):
        q = place(a, c)
        for h in range(2):
            lanes = slice(640 * h, 640 * h + 640)
            half = dr.at[a, c, :, :, lanes]
            wait_bytes(half, r1.at[a, c, h])
            wait_bytes(half, s1.at[c, h])
            sb[q, :, :, lanes] = (
                part[c, :, core, :, lanes].astype(F32) + dr[a, c, :, :, lanes].astype(F32)
            ).astype(BF)
            for k in (2, 1, 3):
                j, dev = y_dev(k)
                remote(
                    sb.at[q, j, :, lanes], yr.at[a, c, k - 1, :, lanes], s2.at[q], r2.at[a, c], dev
                ).start()

    def rs_end(a, c):
        wait_bytes(yr.at[a, c], r2.at[a, c])
        wait_bytes(yr.at[a, c], s2.at[place(a, c)])
        total = sb[place(a, c), y].astype(F32)
        for k in range(3):
            total = total + yr[a, c, k].astype(F32)
        return total

    def ag_start(buf, i, a, c, value):
        buf[i, c, y, core] = value.astype(BF)
        for k in (2, 1, 3):
            _, dev = y_dev(k)
            remote(buf.at[i, c, y, core], buf.at[i, c, y, core], s3.at[place(a, c)], r3.at[a, c], dev).start()

    def ag_mid(buf, i, a, c):
        wait_bytes(yr.at[a, c], r3.at[a, c])
        wait_bytes(yr.at[a, c], s3.at[place(a, c)])
        remote(buf.at[i, c, :, core], buf.at[i, c, :, core], s4.at[place(a, c)], r4.at[a, c], core_dev).start()

    def ag_end(a, c):
        wait_bytes(dr.at[a, c], r4.at[a, c])
        wait_bytes(dr.at[a, c], s4.at[place(a, c)])

    def heads_of(l, c):
        own = qkv[l, c].astype(F32)
        far = kvo[l, c].astype(F32)
        q = own[:, 0:160]
        k = jnp.concatenate([own[:, 160:320], far[:, 32:192]], axis=0)
        v = jnp.concatenate([own[:, 320:480], far[:, 192:352]], axis=0)
        return split_heads(q).astype(BF), k, v

    def project(l, c):
        normed = FB[2 * l, c].reshape(ROWS, D)
        proj = dot_nn(normed, W[l, 0, :, :, :, :, 0:512].reshape(D, 512)) + bqkv[l]
        qkv[l, c] = proj.astype(BF)
        remote(qkv.at[l, c, :, 128:512], kvo.at[l, c], ks.at[l, c], kr.at[l, c], seq_dev).start()

    def attend(l, c):
        wait_bytes(kvo.at[l, c], kr.at[l, c])
        wait_bytes(kvo.at[l, c], ks.at[l, c])
        q2, k, v = heads_of(l, c)
        scores = dot_nt(q2, k.astype(BF)) * SCALING
        slot = lax.broadcasted_iota(jnp.int32, (1, 2 * ROWS), 1)
        slot = jnp.where(slot < ROWS, slot + s * ROWS, slot - s * ROWS)
        scores = jnp.where(slot < len_ref[c], scores, MASKED)
        top = jnp.max(scores, axis=-1, keepdims=True)
        powers = jnp.exp(scores - top)
        probs = powers / jnp.sum(powers, axis=-1, keepdims=True)
        prob[l, c] = probs
        low = probs.astype(BF)
        attended = dot_nn(
            jnp.concatenate([low[0:ROWS], low[ROWS:]], axis=1), split_heads(v).astype(BF)
        )
        wide = jnp.concatenate([jnp.zeros((ROWS, 96), F32), attended], axis=1).astype(BF)
        att[l, c] = wide
        rs_start(2 * l, c, lambda h: dot_nt(wide, W[l, 0, h, :, :, :, 384:640].reshape(640, 256)))

    def attend_rows(l, c):
        a = 2 * l
        middle = xrow[l, c] + rs_end(a, c) + vec(l, 4)
        midrow[l, c] = middle
        unit, _ = norm_parts(middle)
        ag_start(FB, 2 * l + 1, a, c, unit * vec(l, 1) + vec(l, 3))

    def feed(l, c):
        normed = FB[2 * l + 1, c].reshape(ROWS, D)
        pre = dot_nn(normed, W[l, 1].reshape(D, PART)) + bup_ref[l : l + 1, :].astype(F32)
        cdf = 0.5 * (1.0 + lax.erf(pre * math.sqrt(0.5)))
        activated = (pre * cdf).astype(BF)
        act[l, c] = activated
        if c == 0:
            ring_wait(DOWN1 if l else DOWN0)
        rs_start(2 * l + 1, c, lambda h: dot_nt(activated, W[l, 2, h].reshape(640, PART)))
        slope[l, c] = cdf + pre * jnp.exp(-0.5 * pre * pre) * (1.0 / math.sqrt(2.0 * math.pi))

    def feed_rows(l, c):
        a = 2 * l + 1
        hidden = midrow[l, c] + rs_end(a, c) + vec(l, 5)
        if l == 0:
            xrow[1, c] = hidden
            unit, _ = norm_parts(hidden)
            hidden = unit * vec(1, 0) + vec(1, 2)
        ag_start(FB, 2 * l + 2, a, c, hidden)

    def feed_back(l, c):
        grad_act = dot_nn(BB[2 - 2 * l, c].reshape(ROWS, D), W[l, 2].reshape(D, PART))
        grad_pre = (grad_act * slope[l, c]).astype(BF)
        gpre[c] = grad_pre
        rs_start(6 - 2 * l, c, lambda h: dot_nt(grad_pre, W[l, 1, h].reshape(640, PART)))
        gb[2 + l : 3 + l, :] += jnp.sum(grad_pre.astype(F32), axis=0, keepdims=True)

    def feed_back_rows(l, c):
        a = 6 - 2 * l
        grad_norm = rs_end(a, c)
        unit, inv = norm_parts(midrow[l, c])
        gy = gyrow[c]
        grad_mid = gy + norm_back(grad_norm, vec(l, 1), unit, inv)
        gmidrow[c] = grad_mid
        ag_start(BB, 3 - 2 * l, a, c, grad_mid)
        GV[l, 1:2, 0:D] += jnp.sum(grad_norm * unit, axis=0, keepdims=True)
        GV[l, 3:4, 0:D] += jnp.sum(grad_norm, axis=0, keepdims=True)
        GV[l, 4:5, 0:D] += jnp.sum(grad_mid, axis=0, keepdims=True)
        GV[l, 5:6, 0:D] += jnp.sum(gy, axis=0, keepdims=True)

    def attend_back(l, c):
        wide = dot_nn(BB[3 - 2 * l, c].reshape(ROWS, D), W[l, 0, :, :, :, :, 384:640].reshape(D, 256))
        ga2 = split_heads(wide[:, 96:256]).astype(BF)
        q2, k, v = heads_of(l, c)
        probs = prob[l, c]
        grad_probs = dot_nt(ga2, v.astype(BF))
        grad_scores = probs * (grad_probs - jnp.sum(probs * grad_probs, axis=-1, keepdims=True))
        low = grad_scores.astype(BF)
        grad_v = dot_tn(probs.astype(BF), ga2)
        grad_k = dot_tn(low, q2) * SCALING
        pad = jnp.zeros((ROWS, 64), F32)
        gks[c] = jnp.concatenate([grad_k[ROWS:], grad_v[ROWS:], pad], axis=1).astype(BF)
        remote(gks.at[c], gkr.at[l, c], gs_s.at[c], gs_r.at[l, c], seq_dev).start()
        grad_q = (
            dot_nn(jnp.concatenate([low[0:ROWS], low[ROWS:]], axis=1), split_heads(k).astype(BF))
            * SCALING
        )
        gkeep[c, :, 0:160] = grad_q
        gkeep[c, :, 160:320] = grad_k[0:ROWS]
        gkeep[c, :, 320:480] = grad_v[0:ROWS]
        gkeep[c, :, 480:512] = jnp.zeros((ROWS, 32), F32)

    def project_back(l, c):
        wait_bytes(gkr.at[l, c], gs_r.at[l, c])
        wait_bytes(gkr.at[l, c], gs_s.at[c])
        far = gkr[l, c].astype(F32)
        gkeep[c, :, 160:480] += far[:, 0:320]
        grads = gkeep[c].astype(BF)
        gproj[c] = grads
        rs_start(7 - 2 * l, c, lambda h: dot_nt(grads, W[l, 0, h, :, :, :, 0:512].reshape(640, 512)))
        total = jnp.sum(grads.astype(F32), axis=0, keepdims=True)
        if l:
            gb[1:2, 0:512] += total
        else:
            for i in range(4):
                gq[i : i + 1, :] += total[:, 128 * i : 128 * i + 128]

    def project_back_rows(l, c):
        a = 7 - 2 * l
        grad_norm = rs_end(a, c)
        unit, inv = norm_parts(xrow[l, c])
        gy = gmidrow[c] + norm_back(grad_norm, vec(l, 0), unit, inv)
        gyrow[c] = gy
        ag_start(BB, 4 - 2 * l, a, c, gy)
        GV[l, 0:1, 0:D] += jnp.sum(grad_norm * unit, axis=0, keepdims=True)
        GV[l, 2:3, 0:D] += jnp.sum(grad_norm, axis=0, keepdims=True)

    def left_of(buf, i, m):
        lanes = pl.ds(pl.multiple_of(m * 640, 128), 640)
        return buf[i, :, :, :, :, lanes].reshape(MICRO * ROWS, 640)

    def down_grad(l):
        @pl.loop(0, 2)
        def _(m):
            right = act[l].reshape(MICRO * ROWS, PART)
            dW[l, 2, m] = dot_tn(left_of(BB, 2 - 2 * l, m), right).astype(BF).reshape(4, 2, SHARD, PART)

    def up_grad(l):
        @pl.loop(0, 2)
        def _(m):
            right = gpre[...].reshape(MICRO * ROWS, PART)
            dW[l, 1, m] = dot_tn(left_of(FB, 2 * l + 1, m), right).astype(BF).reshape(4, 2, SHARD, PART)

    def out_grad(l):
        @pl.loop(0, 2)
        def _(m):
            grad = dot_tn(left_of(BB, 3 - 2 * l, m), att[l].reshape(MICRO * ROWS, 256))
            dW[l, 0, m, :, :, :, 384:640] = grad.astype(BF).reshape(4, 2, SHARD, 256)

    def qkv_grad(l):
        @pl.loop(0, 2)
        def _(m):
            grad = dot_tn(left_of(FB, 2 * l, m), gproj[...].reshape(MICRO * ROWS, 512))
            dW[l, 0, m, :, :, :, 0:384] = grad[:, 0:384].astype(BF).reshape(4, 2, SHARD, 384)
            rest = dW[l, 0, m, :, :, :, 384:512].astype(F32).reshape(640, 128) + grad[:, 384:512]
            dW[l, 0, m, :, :, :, 384:512] = rest.astype(BF).reshape(4, 2, SHARD, 128)

    gather_one(QKV0)

    @pl.loop(1, SHARDS)
    def _(k):
        remote(VG.at[me], VG.at[me], vs.at[0], vrs.at[0], shard_dev(k)[1]).start()

    gather_one(OUT0)
    pack(0, 1)
    pack(0, 2)
    V[...] = jnp.zeros_like(V)
    GV[...] = jnp.zeros_like(GV)
    gb[...] = jnp.zeros_like(gb)
    gq[...] = jnp.zeros_like(gq)
    bqkv[...] = jnp.zeros_like(bqkv)
    for l in range(2):
        bqkv[l, :, 0:160] = bqv_ref[l, 0:1, :].astype(F32)
        bqkv[l, :, 320:480] = bqv_ref[l, 1:2, :].astype(F32)
    gather_two(QKV0)
    wait_bytes(VG.at[pl.ds(0, SHARDS - 1)], vrs.at[0])
    wait_bytes(VG.at[pl.ds(0, SHARDS - 1)], vs.at[0])
    for i in range(SHARDS):
        low = SHARD * i // 128 * 128
        held = VG[i].astype(F32)
        V[0, :, low : low + 256] += held[0:8]
        V[1, :, low : low + 256] += held[8:16]
    cp_h.wait()
    cp_c.wait()
    gather_one(UP0)
    gather_one(DOWN0)
    for c in range(MICRO):
        whole = FB[0, c].reshape(ROWS, D).astype(F32)
        unit, _ = norm_parts(whole)
        xrow[0, c] = FB[0, c, y, core].astype(F32)
        FB[0, c] = (unit * vec(0, 0) + vec(0, 2)).astype(BF).reshape(4, 2, 16, D)
    gather_two(OUT0)
    ring_two(UP0)
    gather_wait(QKV0)

    def mask_grads():
        row = lax.broadcasted_iota(jnp.int32, (ROWS, 1), 0) + s * ROWS
        for c in range(MICRO):
            masked = jnp.where(row < len_ref[c], BB[0, c].reshape(ROWS, D).astype(F32), 0.0)
            BB[0, c] = masked.astype(BF).reshape(4, 2, 16, D)
            gyrow[c] = BB[0, c, y, core].astype(F32)

    def bias_sums():
        @pl.loop(1, SHARDS)
        def _(k):
            remote(gb, br.at[k - 1], es.at[1], er.at[1], shard_dev(k)[1]).start()

    def last_sums():
        @pl.loop(1, SHARDS)
        def _(k):
            remote(gq, bq.at[k - 1], es.at[3], er.at[3], shard_dev(k)[1]).start()

    def norm_sums():
        for i in range(11):
            lanes = slice(128 * i, 128 * i + 128)
            GT[i] = jnp.concatenate([GV[0, :, lanes], GV[1, :, lanes]], axis=0).astype(BF)

        @pl.loop(1, SHARDS)
        def _(k):
            j, dev = shard_dev(k)
            remote(GT.at[pl.ds(SHARD * j // 128, 2)], vr.at[k - 1], es.at[0], er.at[0], dev).start()

    cp_o = pltpu.make_async_copy(FB.at[4], out_ref, lsem.at[0])
    cp_g = pltpu.make_async_copy(BB.at[4], ingrad_ref, lsem.at[1])

    steps = []
    sums = {}
    for l in (0, 1):
        for c in range(MICRO):
            steps.append((partial(project, l, c), None))
        for c in range(MICRO):
            steps.append((partial(attend, l, c), (2 * l, c)))
            sums[2 * l, c] = (partial(attend_rows, l, c), FB, 2 * l + 1)
        for c in range(MICRO):
            steps.append((partial(feed, l, c), (2 * l + 1, c)))
            sums[2 * l + 1, c] = (partial(feed_rows, l, c), FB, 2 * l + 2)
    for l in (1, 0):
        a0, a1 = 6 - 2 * l, 7 - 2 * l
        for c in range(MICRO):
            steps.append((partial(feed_back, l, c), (a0, c)))
            sums[a0, c] = (partial(feed_back_rows, l, c), BB, 3 - 2 * l)
        for c in range(MICRO):
            steps.append((partial(attend_back, l, c), None))
        for c in range(MICRO):
            steps.append((partial(project_back, l, c), (a1, c)))
            sums[a1, c] = (partial(project_back_rows, l, c), BB, 4 - 2 * l)

    g1, g2, g3, g4 = gather_one, ring_two, ring_three, ring_wait
    d1, d2, d3 = reduce_one, reduce_two, reduce_three
    before = {
        3: [(g2, DOWN0), (gather_wait, OUT0)],
        4: [(g1, PROJ1)],
        5: [(g3, DOWN0), (g2, PROJ1)],
        6: [(g4, UP0), (g1, UP1)],
        7: [(g3, PROJ1), (g2, UP1), (g1, DOWN1)],
        9: [(g4, PROJ1), (g3, UP1), (g2, DOWN1)],
        12: [(g3, DOWN1)],
        15: [(g4, UP1)],
    }
    between = {
        3: [(g3, UP0), (pack, 1, 0)],
        4: [(pack, 1, 1)],
        5: [(pack, 1, 2)],
        6: [(mask_grads,)],
        17: [(down_grad, 1), (d1, 1, DOWN)],
        20: [(up_grad, 1), (d1, 1, UP)],
        22: [(d2, 1, DOWN)],
        24: [(out_grad, 1), (d1, 1, OUT)],
        26: [(qkv_grad, 1), (d1, 1, QKV)],
        27: [(d2, 1, OUT)],
        29: [(down_grad, 0), (d1, 0, DOWN)],
        30: [(up_grad, 0), (d1, 0, UP)],
        31: [(d2, 1, QKV), (bias_sums,)],
        33: [(out_grad, 0), (d1, 0, OUT)],
        34: [(d2, 0, DOWN)],
        35: [(qkv_grad, 0), (d1, 0, QKV), (last_sums,)],
        36: [(d2, 0, OUT)],
    }
    later = {
        25: [(d2, 1, UP)],
        34: [(d2, 0, UP)],
    }
    for n in range(len(steps) + 2):
        for fn, *where in before.get(n, ()):
            fn(*where)
        if n < len(steps):
            steps[n][0]()
        for fn, *where in between.get(n, ()):
            fn(*where)
        if n < len(steps) and steps[n][1] is not None:
            rs_mid(*steps[n][1])
        if n == 18:
            for c in range(MICRO):
                sums[3, c][0]()
        one = steps[n - 1][1] if 1 <= n <= len(steps) else None
        two = steps[n - 2][1] if n >= 2 else None
        if one is not None and one[0] != 3:
            sums[one][0]()
        if n == len(steps):
            norm_sums()
        if n == len(steps) + 1:
            reduce_two(0, QKV)
        if n == 22:
            for c in range(MICRO):
                ag_mid(FB, 4, 3, c)
        if two is not None and two[0] != 3:
            ag_mid(sums[two][1], sums[two][2], *two)
        for fn, *where in later.get(n, ()):
            fn(*where)
        if two is not None and two[0] != 3:
            ag_end(*two)
        if n == 22:
            for c in range(MICRO):
                ag_end(3, c)
            cp_o.start()

    cp_g.start()
    for l, i in ((1, DOWN), (1, UP), (1, OUT), (1, QKV)):
        reduce_three(l, i)
    wait_bytes(vr, er.at[0])
    wait_bytes(vr, es.at[0])
    own = GT[pl.ds(SHARD * me // 128, 2)].astype(F32)
    for k in range(SHARDS - 1):
        own = own + vr[k].astype(F32)
    vr2[7] = own

    @pl.loop(1, 8)
    def _(k):
        remote(vr2.at[7], vr2.at[k - 1], es.at[2], er.at[2], (f, s, (t + k) % 8)).start()

    wait_bytes(br, er.at[1])
    wait_bytes(br, es.at[1])
    wait_bytes(bq, er.at[3])
    wait_bytes(bq, es.at[3])
    totals = gb[...]
    lasts = gq[...]
    for k in range(SHARDS - 1):
        totals = totals + br[k]
        lasts = lasts + bq[k]
    bsum_ref[...] = totals
    for i in range(4):
        bsum_ref[0:1, 128 * i : 128 * i + 128] = lasts[i : i + 1]
    for l, i in ((0, DOWN), (0, UP), (0, OUT)):
        reduce_three(l, i)
    wait_bytes(vr2.at[pl.ds(0, 7)], er.at[2])
    wait_bytes(vr2.at[pl.ds(0, 7)], es.at[2])
    own = vr2[7]
    for k in range(7):
        own = own + vr2[k]
    vsum_ref[...] = own
    reduce_three(0, QKV)
    for l in range(2):
        for i in range(4):
            p, ways = piece(l, i)
            for way, cols in ways:
                pltpu.make_async_copy(dwo.at[l, p, :, cols], dwo_ref.at[l, p, :, cols], osem.at[l, i, way]).wait()
    cp_o.wait()
    cp_g.wait()


def finish(
    out_ref, ingrad_ref, dwo_ref, vsum_ref, bsum_ref,
    hidden_ref, grad_ref, gqkv_ref, gqv_ref, gout_ref, gbout_ref, gup_ref, gbup_ref, gdown_ref, gbdown_ref,
    ggain_ref, gshift_ref,
):
    me = lax.axis_index("fsdp") * 2 + lax.axis_index("seq")
    hidden_ref[...] = out_ref[...].astype(F32)
    grad_ref[...] = ingrad_ref[...].astype(F32)
    rows = jnp.concatenate([vsum_ref[0], vsum_ref[1]], axis=1)
    rows = pltpu.roll(rows, (256 - (SHARD * me) % 128) % 256, 1)
    for l in range(2):
        proj = dwo_ref[l, 0]
        for i in range(3):
            gqkv_ref[l, i] = proj[:, 160 * i : 160 * i + 160]
        gout_ref[l] = proj[:, 480:640].T
        gup_ref[l] = dwo_ref[l, 1]
        gdown_ref[l] = dwo_ref[l, 2]
        gqv_ref[l, 0:1, :] = bsum_ref[l : l + 1, 0:160]
        gqv_ref[l, 1:2, :] = bsum_ref[l : l + 1, 320:480]
        gbup_ref[l : l + 1, :] = bsum_ref[2 + l : 3 + l, :]
        ggain_ref[l] = rows[8 * l : 8 * l + 2, 0:SHARD]
        gshift_ref[l] = rows[8 * l + 2 : 8 * l + 4, 0:SHARD]
        gbout_ref[l : l + 1, :] = rows[8 * l + 4 : 8 * l + 5, 0:SHARD]
        gbdown_ref[l : l + 1, :] = rows[8 * l + 5 : 8 * l + 6, 0:SHARD]


def body(
    hidden_in, cotangent, lengths, qkv_weight, qv_bias, out_weight, out_bias,
    up_weight, up_bias, down_weight, down_bias, ln_gain, ln_bias,
):
    vmem = pl.BlockSpec(memory_space=pltpu.VMEM)
    anys = pl.BlockSpec(memory_space=pl.ANY)
    smem = pl.BlockSpec(memory_space=pltpu.SMEM)
    dma = pltpu.SemaphoreType.DMA
    blocks = (MICRO, 4, 2, 16, D)
    scratch = [
        pltpu.VMEM((2, 3, 2, 4, 2, SHARD, PART), BF),
        pltpu.VMEM((2, 3, 2, 4, 2, SHARD, PART), BF),
        pltpu.VMEM((2, 3, 3, 4, SHARD, 384), BF),
        pltpu.VMEM((2, 3, 3, 2, 2, SHARD, 384), BF),
        pltpu.VMEM((2, 3, 3, SHARD, PART), BF),
        pltpu.VMEM((5,) + blocks, BF),
        pltpu.VMEM((5,) + blocks, BF),
        pltpu.VMEM((8, MICRO, 4, 16, D), BF),
        pltpu.VMEM((8, MICRO, 3, 16, D), BF),
        pltpu.VMEM(blocks, BF),
        pltpu.VMEM((2 * MICRO, 4, 16, D), BF),
        pltpu.VMEM((2, MICRO, ROWS, 512), BF),
        pltpu.VMEM((2, MICRO, ROWS, 384), BF),
        pltpu.VMEM((2, MICRO, 2 * ROWS, 2 * ROWS), F32),
        pltpu.VMEM((2, MICRO, ROWS, 256), BF),
        pltpu.VMEM((2, MICRO, 16, D), F32),
        pltpu.VMEM((2, MICRO, 16, D), F32),
        pltpu.VMEM((2, MICRO, ROWS, PART), F32),
        pltpu.VMEM((2, MICRO, ROWS, PART), BF),
        pltpu.VMEM((MICRO, ROWS, PART), BF),
        pltpu.VMEM((MICRO, ROWS, 512), F32),
        pltpu.VMEM((MICRO, ROWS, 512), BF),
        pltpu.VMEM((MICRO, ROWS, 384), BF),
        pltpu.VMEM((2, MICRO, ROWS, 384), BF),
        pltpu.VMEM((MICRO, 16, D), F32),
        pltpu.VMEM((MICRO, 16, D), F32),
        pltpu.VMEM((SHARDS, 16, 256), BF),
        pltpu.VMEM((2, 8, 1408), F32),
        pltpu.VMEM((2, 8, 1408), F32),
        pltpu.VMEM((11, 16, 128), BF),
        pltpu.VMEM((SHARDS - 1, 2, 16, 128), BF),
        pltpu.VMEM((8, 2, 16, 128), F32),
        pltpu.VMEM((8, PART), F32),
        pltpu.VMEM((SHARDS - 1, 8, PART), F32),
        pltpu.VMEM((8, 128), F32),
        pltpu.VMEM((SHARDS - 1, 8, 128), F32),
        pltpu.VMEM((16, 256), F32),
        pltpu.VMEM((2, 1, 512), F32),
        pltpu.VMEM((2, 3, SHARD, PART), F32),
        dma((8, 2)), dma((8, 2)), dma((8, 2)), dma((8, 2)), dma((8, 2)), dma((8, 2)),
        dma((2, 4, 2)), dma((2, 4, 2)), dma((2, 4, 2)), dma((2, 4, 2)),
        dma((MICRO, 2)), dma((8, MICRO, 2)), dma((2 * MICRO,)), dma((8, MICRO)),
        dma((2 * MICRO,)), dma((8, MICRO)), dma((2 * MICRO,)), dma((8, MICRO)),
        dma((2, MICRO)), dma((2, MICRO)), dma((MICRO,)), dma((2, MICRO)),
        dma((1,)), dma((1,)), dma((4,)), dma((4,)), dma((2,)), dma((2, 2)), dma((2, 4, 2)),
    ]
    out, ingrad, dwo, vsum, bsum = pl.pallas_call(
        kernel,
        name="encoder",
        out_shape=(
            jax.ShapeDtypeStruct(blocks, BF),
            jax.ShapeDtypeStruct(blocks, BF),
            jax.ShapeDtypeStruct((2, 3, SHARD, PART), F32),
            jax.ShapeDtypeStruct((2, 16, 128), F32),
            jax.ShapeDtypeStruct((8, PART), F32),
        ),
        in_specs=[anys, anys, smem, vmem, vmem, vmem, vmem, anys, vmem, anys, vmem, vmem, vmem],
        out_specs=(anys, anys, anys, vmem, vmem),
        scratch_shapes=scratch,
        compiler_params=pltpu.CompilerParams(
            collective_id=0, has_side_effects=True, vmem_limit_bytes=63 * 1024 * 1024
        ),
    )(
        hidden_in.reshape(blocks), cotangent.reshape(blocks), lengths, qkv_weight, qv_bias, out_weight,
        out_bias, up_weight, up_bias, jnp.swapaxes(down_weight, 1, 2), down_bias, ln_gain, ln_bias,
    )
    rows = (MICRO, ROWS, D)
    shapes = (
        rows, rows, (2, 3, SHARD, 160), (2, 2, 160), (2, 160, SHARD), (2, SHARD), (2, SHARD, PART),
        (2, PART), (2, SHARD, PART), (2, SHARD), (2, 2, SHARD), (2, 2, SHARD),
    )
    outs = pl.pallas_call(
        finish,
        name="finish",
        out_shape=tuple(jax.ShapeDtypeStruct(shape, F32) for shape in shapes),
        in_specs=[vmem] * 5,
        out_specs=(vmem,) * 12,
        compiler_params=pltpu.CompilerParams(vmem_limit_bytes=63 * 1024 * 1024),
    )(out.reshape(rows), ingrad.reshape(rows), dwo, vsum, bsum)
    return outs[:8] + (jnp.swapaxes(outs[8], 1, 2),) + outs[9:]


def solution(mesh):
    placed = (
        P("fsdp", "seq", None),
        P("fsdp", "seq", None),
        P("fsdp"),
        P(None, None, ("fsdp", "seq"), "tp"),
        P(None, None, "tp"),
        P(None, "tp", ("fsdp", "seq")),
        P(None, ("fsdp", "seq")),
        P(None, ("fsdp", "seq"), "tp"),
        P(None, "tp"),
        P(None, "tp", ("fsdp", "seq")),
        P(None, ("fsdp", "seq")),
        P(None, None, ("fsdp", "seq")),
        P(None, None, ("fsdp", "seq")),
    )
    return jax.shard_map(
        body,
        mesh=mesh,
        in_specs=placed,
        out_specs=(
            P("fsdp", "seq", None),
            P("fsdp", "seq", None),
            P(None, None, ("fsdp", "seq"), "tp"),
            P(None, None, "tp"),
            P(None, "tp", ("fsdp", "seq")),
            P(None, ("fsdp", "seq")),
            P(None, ("fsdp", "seq"), "tp"),
            P(None, "tp"),
            P(None, "tp", ("fsdp", "seq")),
            P(None, ("fsdp", "seq")),
            P(None, None, ("fsdp", "seq")),
            P(None, None, ("fsdp", "seq")),
        ),
        check_vma=False,
    )
```
